256 devices in a mesh: dp: 64 (over y, z, core), mp: 4 (over x).
Axes of the slice: x: 4, y: 4, z: 8, core: 2. Of those that a mesh axis runs over, the one named last changes fastest.
Arguments:
- passage_states: bfloat16 [768, 180, 768], P('dp'), may hold values from -6 to 6
- query_states: bfloat16 [192, 32, 768], P('dp'), may hold values from -6 to 6
- lengths: int32 [768], replicated, may hold values from 22 to 180, as said below
- owner_map: int32 [768], replicated, may hold values from 0 to 767, as said below
- candidates: int32 [192, 64], P('dp', 'mp'), may hold values from 0 to 767, as said below
- teacher_scores: float32 [192, 64], P('dp', 'mp'), may hold values from -8 to 8
- up_weight: bfloat16 [768, 3072], P(None, 'mp'), may hold values from -0.21875 to 0.21875
- down_weight: bfloat16 [3072, 768], P('mp'), may hold values from -0.109375 to 0.109375
- proj_weight: bfloat16 [768, 128], replicated, may hold values from -0.21875 to 0.21875
Outputs:
- query_loss: float32 [192], P('dp')
- grad_up: float32 [768, 3072], P('dp', 'mp')
- grad_down: float32 [3072, 768], P('mp', 'dp')
- grad_proj: float32 [768, 128], P('dp')
The draws below stay inside these ranges and needn't reach their ends.
Inputs may be any that keep to these rules, and one draw needn't show every extreme that they name: A permutation: passage id k sits at pool position owner_map[k], held by dp index owner_map[k] // 12. `candidates`: on one device (the 3 queries of one dp index and the 16 candidate columns of one mp index) at most 2 candidate slots name passages of one owner; in every draw some owner gets exactly 2 from every device. A passage may appear more than once. `lengths`: the 12 pool positions of each dp index include one passage of 180 tokens.
All inputs are finite; a program needn't handle non-finite values.
Results may differ from the reference program's by a relative error of at most 0.03.
Values may be sent and summed in bfloat16 or wider, within the bound.
A program may use at most 192 MiB of HBM per device.

```python
import jax
import jax.numpy as jnp
from jax import lax

D = 768
FF = 3072
E = 128
QLEN = 32
PLEN = 180
CANDS = 64
Q_DEV = 3
P_DEV = 12
QUERIES = 192
POOL = 768
SLOTS = 48
CAP = 2
N_DP = 64
N_MP = 4


def layout_helper(key):
    perm_key, hot_key, order_key, shuffle_key, place_key = jax.random.split(key, 5)
    owner_map = jax.random.permutation(perm_key, POOL).astype(jnp.int32)
    hot_owner = jax.random.randint(hot_key, (), 0, N_DP)
    others = (hot_owner + 1 + jnp.arange((N_DP - 1) * CAP) % (N_DP - 1)) % N_DP
    block_count = N_DP * N_MP
    order_keys = jax.random.split(order_key, block_count)
    shuffle_keys = jax.random.split(shuffle_key, block_count)

    def one_block(first_key, second_key):
        picked_others = jax.random.permutation(first_key, others)[:SLOTS - CAP]
        block_owners = jnp.concatenate([jnp.full((CAP,), hot_owner, jnp.int32), picked_others.astype(jnp.int32)])
        return jax.random.permutation(second_key, block_owners)
    slot_owners = jax.vmap(one_block)(order_keys, shuffle_keys)
    inside = jax.random.randint(place_key, (block_count, SLOTS), 0, P_DEV)
    positions = slot_owners * P_DEV + inside
    positions = positions.reshape(N_DP, N_MP, Q_DEV, CANDS // N_MP)
    positions = jnp.transpose(positions, (0, 2, 1, 3)).reshape(QUERIES, CANDS)
    inverse_map = jnp.zeros((POOL,), jnp.int32).at[owner_map].set(jnp.arange(POOL, dtype=jnp.int32))
    candidates = jnp.take(inverse_map, positions)
    return (owner_map, candidates.astype(jnp.int32))


def draw_owner_map(key, part):
    return layout_helper(key)[0]


def draw_candidates(key, part):
    return layout_helper(key)[1]


def draw_lengths(key, part):
    key = jax.random.fold_in(key, 7)
    first_key, second_key = jax.random.split(key)
    token_counts = jax.random.randint(first_key, (POOL,), max(1, PLEN // 8), PLEN + 1)
    longest = jnp.arange(N_DP) * P_DEV + jax.random.randint(second_key, (N_DP,), 0, P_DEV)
    return token_counts.at[longest].set(PLEN).astype(jnp.int32)


def block_scale(stream_key, dims, cuts, low, top_value):
    gain = 1.0
    for axis_at, shards_of in cuts:
        heights = jax.random.uniform(jax.random.fold_in(jax.random.fold_in(stream_key, 6), axis_at), (shards_of,), jnp.float32, low / len(cuts), top_value / len(cuts))
        gain = gain * jnp.repeat(jnp.exp(heights), dims[axis_at] // shards_of).reshape((-1,) + (1,) * (len(dims) - 1 - axis_at))
    return gain


def normal_values(stream_key, shape, deviation, most, shards=(), kind=jnp.bfloat16):
    array = deviation * jax.random.normal(stream_key, shape, jnp.float32)
    if shards:
        array = array * block_scale(stream_key, shape, shards, -0.22, 0.18)
    return jnp.clip(array, -most, most).astype(kind)


def setup_inputs(seed: int = 0) -> dict:
    seeds = jax.random.split(jax.random.key(seed), 10)
    passage_states = normal_values(seeds[0], (POOL, PLEN, D), 1.0, 6.0, ((0, 64),))
    query_states = normal_values(seeds[1], (QUERIES, QLEN, D), 1.0, 6.0, ((0, 64),))
    lengths = draw_lengths(jax.random.fold_in(seeds[9], 71), 0)
    owner_map = draw_owner_map(jax.random.fold_in(seeds[9], 71), 0)
    candidates = draw_candidates(jax.random.fold_in(seeds[9], 71), 0)
    teacher_scores = normal_values(seeds[5], (QUERIES, CANDS), 2.0, 8.0, ((0, 64), (1, 4)), jnp.float32)
    up_weight = normal_values(seeds[6], (D, FF), D ** -0.5, 0.21875, ((1, 4),))
    down_weight = normal_values(seeds[7], (FF, D), FF ** -0.5, 0.109375, ((0, 4),))
    proj_weight = normal_values(seeds[8], (D, E), D ** -0.5, 0.21875)
    return {"passage_states": passage_states, "query_states": query_states, "lengths": lengths, "owner_map": owner_map, "candidates": candidates, "teacher_scores": teacher_scores, "up_weight": up_weight, "down_weight": down_weight, "proj_weight": proj_weight}


TAU = 0.05
EPS = 1e-06

def up_section(token_rows, up_weight):
    pre_act = jnp.dot(token_rows, up_weight, preferred_element_type=jnp.float32)
    hidden = jax.nn.gelu(pre_act).astype(jnp.bfloat16)
    return (pre_act, hidden)

def shard_sum(hidden, down_weight, pieces):
    shard_width = hidden.shape[1] // pieces
    ffn_total = jnp.zeros((hidden.shape[0], down_weight.shape[1]), jnp.float32)
    for shard in range(pieces):
        lower = shard * shard_width
        shard_term = jnp.dot(hidden[:, lower:lower + shard_width], down_weight[lower:lower + shard_width], preferred_element_type=jnp.float32).astype(jnp.bfloat16)
        ffn_total = ffn_total + lax.optimization_barrier(shard_term).astype(jnp.float32)
    return ffn_total

def proj_section(token_rows, ffn_total, proj_weight):
    mixed = (token_rows.astype(jnp.float32) + ffn_total).astype(jnp.bfloat16)
    projected = jnp.dot(mixed, proj_weight, preferred_element_type=jnp.float32)
    inverse_norm = lax.rsqrt(lax.optimization_barrier(jnp.sum(projected * projected, axis=-1, keepdims=True)) + EPS)
    unit_rows = projected * inverse_norm
    return (mixed, unit_rows, inverse_norm, unit_rows.astype(jnp.bfloat16))

def back_section(token_rows, pre_act, hidden, mixed, unit_rows, inverse_norm, emb_cot, down_weight, proj_weight):
    along = lax.optimization_barrier(jnp.sum(emb_cot * unit_rows, axis=-1, keepdims=True))
    unit_cot = (inverse_norm * (emb_cot - unit_rows * along)).astype(jnp.bfloat16)
    grad_proj = jnp.dot(mixed.T, unit_cot, preferred_element_type=jnp.float32)
    mixed_cot = jnp.dot(unit_cot, proj_weight.T, preferred_element_type=jnp.float32).astype(jnp.bfloat16)
    grad_down = jnp.dot(hidden.T, mixed_cot, preferred_element_type=jnp.float32)
    hidden_cot = jnp.dot(mixed_cot, down_weight.T, preferred_element_type=jnp.float32)
    pre_cot = jax.vjp(jax.nn.gelu, pre_act)[1](hidden_cot)[0].astype(jnp.bfloat16)
    grad_up = jnp.dot(token_rows.T, pre_cot, preferred_element_type=jnp.float32)
    return (grad_up, grad_down, grad_proj)

def smooth_scores(query_slots, blocks, slot_len):
    similar = jnp.einsum('sie,ste->sit', query_slots, blocks, preferred_element_type=jnp.float32)
    live_mask = jnp.arange(blocks.shape[1])[None, :] < slot_len[:, None]
    exp_terms = jnp.where(live_mask[:, None, :], jnp.exp(similar / TAU), 0.0)
    denoms = lax.optimization_barrier(jnp.sum(exp_terms, axis=-1))
    scores = TAU * lax.optimization_barrier(jnp.sum(jnp.log(denoms), axis=-1))
    return (scores, exp_terms / denoms[..., None])

def slot_grads(score_cot, attend, query_slots, blocks):
    weights = (score_cot[:, None, None] * attend).astype(jnp.bfloat16)
    query_cot = jnp.einsum('sit,ste->sie', weights, blocks, preferred_element_type=jnp.float32)
    block_cot = jnp.einsum('sit,sie->ste', weights, query_slots, preferred_element_type=jnp.float32)
    return (query_cot, block_cot)

def encode(token_rows, up_weight, down_weight, proj_weight):
    pre_act, hidden = up_section(token_rows, up_weight)
    ffn_total = shard_sum(hidden, down_weight, N_MP)
    mixed, unit_rows, inverse_norm, embedded = proj_section(token_rows, ffn_total, proj_weight)
    return (pre_act, hidden, mixed, unit_rows, inverse_norm, embedded)

def reference(passage_states, query_states, lengths, owner_map, candidates, teacher_scores, up_weight, down_weight, proj_weight):
    pass_blocks = passage_states.reshape(N_DP, P_DEV * PLEN, D)

    def embed_block(token_rows):
        return encode(token_rows, up_weight, down_weight, proj_weight)[5]
    pool_emb = lax.map(embed_block, pass_blocks).reshape(POOL, PLEN, E)
    query_rows = query_states.reshape(QUERIES * QLEN, D)
    query_pre, query_hidden, query_mixed, query_unit, query_inverse, query_flat = encode(query_rows, up_weight, down_weight, proj_weight)
    query_emb = query_flat.reshape(QUERIES, QLEN, E)
    positions = jnp.take(owner_map, candidates).astype(jnp.int32)

    def per_query(grad_carry, query_item):
        one_query, where_rows, teacher = query_item
        blocks = jnp.take(pool_emb, where_rows, axis=0)
        slot_len = jnp.take(lengths, where_rows)
        query_slots = jnp.broadcast_to(one_query, (CANDS, QLEN, E))
        scores, attend = smooth_scores(query_slots, blocks, slot_len)
        student_exp = jnp.exp(scores)
        teacher_exp = jnp.exp(teacher)
        student_sum = jnp.sum(student_exp)
        teacher_sum = jnp.sum(teacher_exp)
        cross_sum = jnp.sum(teacher_exp * (teacher - scores))
        loss_value = cross_sum / teacher_sum - jnp.log(teacher_sum) + jnp.log(student_sum)
        score_cot = student_exp / student_sum - teacher_exp / teacher_sum
        query_cot, block_cot = slot_grads(score_cot, attend, query_slots, blocks)
        grad_carry = grad_carry.at[where_rows].add(block_cot)
        return (grad_carry, (loss_value, lax.optimization_barrier(jnp.sum(query_cot, axis=0))))
    pool_cot, (query_loss, query_cot) = lax.scan(per_query, jnp.zeros((POOL, PLEN, E), jnp.float32), (query_emb, positions, teacher_scores))
    cot_blocks = pool_cot.reshape(N_DP, P_DEV * PLEN, E)
    start_terms = back_section(query_rows, query_pre, query_hidden, query_mixed, query_unit, query_inverse, query_cot.reshape(QUERIES * QLEN, E), down_weight, proj_weight)

    def back_block(totals, block_item):
        token_rows, emb_cot = block_item
        pre_act, hidden, mixed, unit_rows, inverse_norm, unused = encode(token_rows, up_weight, down_weight, proj_weight)
        terms = back_section(token_rows, pre_act, hidden, mixed, unit_rows, inverse_norm, emb_cot, down_weight, proj_weight)
        return ((totals[0] + terms[0], totals[1] + terms[1], totals[2] + terms[2]), None)
    totals, unused_out = lax.scan(back_block, start_terms, (pass_blocks, cot_blocks))
    return (query_loss, totals[0], totals[1], totals[2])
```

```python
import jax
import jax.numpy as jnp
from jax import lax
from jax.sharding import PartitionSpec as P

TAU = 0.05
EPS = 1e-06
F32 = jnp.float32
BF16 = jnp.bfloat16


def dot(a, b, dims):
    return lax.dot_general(a, b, (dims, ((), ())), preferred_element_type=F32)


def project(rows, ffn, proj_weight):
    mixed = (rows.astype(F32) + ffn.astype(F32)).astype(BF16)
    projected = dot(mixed, proj_weight, (((mixed.ndim - 1,), (0,))))
    inverse = lax.rsqrt(jnp.sum(projected * projected, axis=-1, keepdims=True) + EPS)
    return mixed, projected * inverse, inverse


def unit_cotangent(g, unit, inverse):
    along = jnp.sum(g * unit, axis=-1, keepdims=True)
    return (inverse * (g - unit * along)).astype(BF16)


def local(
    passage_states,
    query_states,
    lengths,
    owner_map,
    candidates,
    teacher_scores,
    up_weight,
    down_weight,
    proj_weight,
):
    p_dev, pass_len, width = passage_states.shape
    q_dev, q_len, _ = query_states.shape
    emb = proj_weight.shape[1]
    n_dp, n_mp = lax.axis_size("dp"), lax.axis_size("mp")
    me_dp, me_mp = lax.axis_index("dp"), lax.axis_index("mp")
    p_own = p_dev // n_mp
    q_rows = q_dev * q_len
    q_own = q_rows // n_mp
    queries = n_dp * q_dev

    positions = jnp.take(owner_map, candidates)
    table = jnp.stack([positions.astype(F32), teacher_scores], axis=1)
    table = lax.all_gather(table.reshape(q_dev, -1), ("dp", "mp"), axis=0, tiled=True)
    table = table.reshape(n_dp, n_mp, q_dev, 2, -1)
    table = jnp.transpose(table, (3, 0, 2, 1, 4)).reshape(2, queries, -1)
    pos_all, teacher = table[0], table[1]
    teacher_exp = jnp.exp(teacher)
    teacher_sum = jnp.sum(teacher_exp, axis=1)
    teacher_dot = jnp.sum(teacher_exp * teacher, axis=1)
    base = me_dp * p_dev + me_mp * p_own
    mine = base + jnp.arange(p_own)
    hit = pos_all[None] == mine[:, None, None].astype(F32)
    count = jnp.sum(hit.astype(F32), axis=2)
    teacher_mass = jnp.sum(jnp.where(hit, teacher_exp[None], 0.0), axis=2)

    rows_q = query_states.reshape(q_rows, width)
    pre_q = dot(rows_q, up_weight, ((1,), (0,)))
    hid_q = jax.nn.gelu(pre_q).astype(BF16)
    part_q = dot(hid_q, down_weight, ((1,), (0,))).astype(BF16)
    ffn_q = lax.psum_scatter(part_q, "mp", scatter_dimension=0, tiled=True)
    own_q = lax.dynamic_slice_in_dim(rows_q, me_mp * q_own, q_own, 0)
    mixed_q, unit_q, inv_q = project(own_q, ffn_q, proj_weight)
    q_all = lax.all_gather(unit_q.astype(BF16), ("dp", "mp"), axis=0, tiled=True)

    pre_p = dot(passage_states, up_weight, ((2,), (0,)))
    hid_p = jax.nn.gelu(pre_p).astype(BF16)
    part_p = dot(hid_p, down_weight, ((2,), (0,))).astype(BF16)
    ffn_p = lax.psum_scatter(part_p, "mp", scatter_dimension=0, tiled=True)
    own_p = lax.dynamic_slice_in_dim(passage_states, me_mp * p_own, p_own, 0)
    mixed_p, unit_p, inv_p = project(own_p, ffn_p, proj_weight)
    emb_p = unit_p.astype(BF16)

    own_len = lax.dynamic_slice_in_dim(lengths, base, p_own, 0)
    similar = dot(emb_p, q_all, ((2,), (1,)))
    live = jnp.arange(pass_len)[None, :] < own_len[:, None]
    terms = jnp.where(live[:, :, None], jnp.exp(similar / TAU), 0.0)
    denom = jnp.sum(terms, axis=1)
    scores = TAU * jnp.sum(jnp.log(denom).reshape(p_own, queries, q_len), axis=2)
    student = count * jnp.exp(scores)
    sums = lax.psum(
        jnp.stack([jnp.sum(student, axis=0), jnp.sum(teacher_mass * scores, axis=0)]),
        ("dp", "mp"),
    )
    student_sum = sums[0]
    loss = (teacher_dot - sums[1]) / teacher_sum - jnp.log(teacher_sum) + jnp.log(student_sum)
    query_loss = lax.dynamic_slice_in_dim(loss, me_dp * q_dev, q_dev, 0)
    score_cot = student / student_sum - teacher_mass / teacher_sum
    scale = (score_cot[:, :, None] / denom.reshape(p_own, queries, q_len)).reshape(p_own, 1, -1)
    weights = (terms * scale).astype(BF16)
    cot_p = dot(weights, q_all, ((2,), (0,)))
    cot_q = dot(weights, emb_p, ((0, 1), (0, 1))).astype(BF16)
    cot_q = lax.psum_scatter(cot_q, ("dp", "mp"), scatter_dimension=0, tiled=True).astype(F32)

    uc_p = unit_cotangent(cot_p, unit_p, inv_p)
    uc_q = unit_cotangent(cot_q, unit_q, inv_q)
    grad_proj = dot(mixed_p, uc_p, ((0, 1), (0, 1))) + dot(mixed_q, uc_q, ((0,), (0,)))
    uc_p = lax.all_gather(uc_p, "mp", axis=0, tiled=True)
    uc_q = lax.all_gather(uc_q, "mp", axis=0, tiled=True)

    def back(rows, pre, hid, uc):
        axes = tuple(range(rows.ndim - 1))
        last = (rows.ndim - 1,)
        mixed_cot = dot(uc, proj_weight, (last, (1,))).astype(BF16)
        down = dot(mixed_cot, hid, (axes, axes))
        hid_cot = dot(mixed_cot, down_weight, (last, (1,)))
        pre_cot = jax.vjp(jax.nn.gelu, pre)[1](hid_cot)[0].astype(BF16)
        return dot(rows, pre_cot, (axes, axes)), down

    up_p, down_p = back(passage_states, pre_p, hid_p, uc_p)
    up_q, down_q = back(rows_q, pre_q, hid_q, uc_q)
    grads = jnp.concatenate([up_p + up_q, down_p + down_q, grad_proj], axis=1).astype(BF16)
    grads = lax.psum_scatter(grads, "dp", scatter_dimension=0, tiled=True).astype(F32)
    hidden = up_weight.shape[1]
    grad_proj = lax.psum(grads[:, 2 * hidden :], "mp")
    return (query_loss, grads[:, :hidden], grads[:, hidden : 2 * hidden].T, grad_proj)


def solution(mesh):
    return jax.shard_map(
        local,
        mesh=mesh,
        in_specs=(
            P("dp", None, None),
            P("dp", None, None),
            P(),
            P(),
            P("dp", "mp"),
            P("dp", "mp"),
            P(None, "mp"),
            P("mp", None),
            P(),
        ),
        out_specs=(P("dp"), P("dp", "mp"), P("mp", "dp"), P("dp", None)),
        check_vma=False,
    )
```

```python
import functools

import jax
import jax.numpy as jnp
from jax import lax
from jax.experimental import pallas as pl
from jax.experimental.pallas import tpu as pltpu
from jax.sharding import PartitionSpec as P

TAU = 0.05
EPS = 1e-06
F32 = jnp.float32
BF16 = jnp.bfloat16
NY, NZ, NC, NX = 4, 8, 2, 4
MESH = pl.DeviceIdType.MESH
VMEM = pl.BlockSpec(memory_space=pltpu.VMEM)


def dot(a, b, dims):
    return lax.dot_general(a, b, (dims, ((), ())), preferred_element_type=F32)


def place():
    dp, x = lax.axis_index("dp"), lax.axis_index("mp")
    return dp // (NZ * NC), (dp // NC) % NZ, dp % NC, x


def at(y, z, c, x):
    return ((y * NZ + z) * NC + c, x)


def peers(axis):
    y, z, c, x = place()
    out = []
    size = {"x": NX, "y": NY, "z": NZ, "c": NC}[axis]
    mine = {"x": x, "y": y, "z": z, "c": c}[axis]
    for k in range(1, size):
        to = (mine + k) % size
        frm = (mine + size - k) % size
        who = {"x": (y, z, c, to), "y": (to, z, c, x), "z": (y, to, c, x), "c": (y, z, to, x)}[axis]
        out.append((k, at(*who), to, frm))
    return out


def greet(axes):
    barrier = pltpu.get_barrier_semaphore()
    total = 0
    for axis in axes:
        for _, who, _, _ in peers(axis):
            pl.semaphore_signal(barrier, inc=1, device_id=who, device_id_type=MESH)
            total += 1
    pl.semaphore_wait(barrier, total)


class Stage:
    def __init__(self, axis, send_sem, recv_sem):
        self.axis, self.send_sem, self.recv_sem = axis, send_sem, recv_sem
        self.sent = []

    def start(self, src, dst):
        for k, who, to, _ in peers(self.axis):
            copy = pltpu.make_async_remote_copy(
                src_ref=src(to),
                dst_ref=dst(k),
                send_sem=self.send_sem.at[k - 1],
                recv_sem=self.recv_sem.at[k - 1],
                device_id=who,
                device_id_type=MESH,
            )
            copy.start()
            self.sent.append(copy)

    def arrive(self, dst):
        for k, who, _, frm in peers(self.axis):
            ref = dst(k, frm)
            pltpu.make_async_remote_copy(
                src_ref=ref,
                dst_ref=ref,
                send_sem=self.send_sem.at[k - 1],
                recv_sem=self.recv_sem.at[k - 1],
                device_id=who,
                device_id_type=MESH,
            ).wait_recv()

    def finish(self):
        for copy in self.sent:
            copy.wait_send()


def sems(n):
    return [pltpu.SemaphoreType.DMA((max(n, 1),)), pltpu.SemaphoreType.DMA((max(n, 1),))]


def call(kernel, outs, scratch, number, *args):
    return pl.pallas_call(
        kernel,
        out_shape=outs,
        in_specs=[VMEM] * len(args),
        out_specs=[VMEM] * len(outs),
        scratch_shapes=scratch,
        compiler_params=pltpu.CompilerParams(
            collective_id=number, has_side_effects=True, vmem_limit_bytes=48 * 2**20
        ),
        cost_estimate=pl.CostEstimate(flops=10**9, bytes_accessed=60 * 10**6, transcendentals=0),
    )(*args)


def gather_kernel(
    part, rows, proj, table, q_all, t_all, mixed, unit, inverse, pbuf, tbuf, *sem
):
    y, z, c, x = place()
    greet("xzyc")
    sx, tx = Stage("x", sem[0], sem[1]), Stage("x", sem[2], sem[3])
    sz, tz = Stage("z", sem[4], sem[5]), Stage("z", sem[6], sem[7])
    sy, ty = Stage("y", sem[8], sem[9]), Stage("y", sem[10], sem[11])
    sc, tc = Stage("c", sem[12], sem[13]), Stage("c", sem[14], sem[15])
    tx.start(lambda to: table, lambda k: tbuf.at[x])
    sx.start(lambda to: part, lambda k: pbuf.at[x])
    tbuf[x] = table[...]
    pbuf[x] = part[...]
    tx.arrive(lambda k, frm: tbuf.at[frm])
    merged = tbuf[0]
    for i in range(1, NX):
        merged = merged + tbuf[i]
    t_all[c, y, z] = merged
    tz.start(lambda to: t_all.at[c, y, z], lambda k: t_all.at[c, y, z])
    sx.arrive(lambda k, frm: pbuf.at[frm])
    ffn = pbuf[0].astype(F32)
    for i in range(1, NX):
        ffn = ffn + pbuf[i].astype(F32)
    blend = (rows[...].astype(F32) + ffn).astype(BF16)
    mixed[...] = blend
    projected = jnp.dot(blend, proj[...], preferred_element_type=F32)
    inv = lax.rsqrt(jnp.sum(projected * projected, axis=-1, keepdims=True) + EPS)
    inverse[...] = inv
    unit[...] = projected * inv
    q_all[c, y, z] = (projected * inv).astype(BF16)
    sz.start(lambda to: q_all.at[c, y, z], lambda k: q_all.at[c, y, z])
    tz.arrive(lambda k, frm: t_all.at[c, y, frm])
    ty.start(lambda to: t_all.at[c, y], lambda k: t_all.at[c, y])
    sz.arrive(lambda k, frm: q_all.at[c, y, frm])
    sy.start(lambda to: q_all.at[c, y], lambda k: q_all.at[c, y])
    ty.arrive(lambda k, frm: t_all.at[c, frm])
    tc.start(lambda to: t_all.at[c], lambda k: t_all.at[c])
    sy.arrive(lambda k, frm: q_all.at[c, frm])
    sc.start(lambda to: q_all.at[c], lambda k: q_all.at[c])
    tc.arrive(lambda k, frm: t_all.at[frm])
    sc.arrive(lambda k, frm: q_all.at[frm])
    for stage in (sx, tx, sz, tz, sy, ty, sc, tc):
        stage.finish()


def gather_queries(part, rows, proj, table):
    n, width = part.shape
    emb = proj.shape[1]
    shape = jax.ShapeDtypeStruct
    outs = [
        shape((NC, NY, NZ, n, emb), BF16),
        shape((NC, NY, NZ) + table.shape, F32),
        shape((n, width), BF16),
        shape((n, emb), F32),
        shape((n, 1), F32),
    ]
    scratch = [pltpu.VMEM((NX, n, width), BF16), pltpu.VMEM((NX,) + table.shape, F32)]
    for size in (NX, NX, NZ, NZ, NY, NY, NC, NC):
        scratch += sems(size - 1)
    return call(gather_kernel, outs, scratch, 1, part, rows, proj, table)


def total_kernel(vec, out, abuf, bbuf, *sem):
    y, z, c, x = place()
    barrier = pltpu.get_barrier_semaphore()
    groups = [
        (NY * NX, y * NX + x, lambda i: at(i // NX, z, c, i % NX)),
        (NZ * NC, z * NC + c, lambda i: at(y, i // NC, i % NC, x)),
    ]
    for size, mine, who in groups:
        for k in range(1, size):
            pl.semaphore_signal(
                barrier, inc=1, device_id=who((mine + k) % size), device_id_type=MESH
            )
    pl.semaphore_wait(barrier, NY * NX + NZ * NC - 2)
    held = vec
    for (size, mine, who), buf, send, recv in zip(
        groups, (abuf, bbuf), (sem[0], sem[2]), (sem[1], sem[3])
    ):
        copies = []
        buf[mine] = held[...]
        for k in range(1, size):
            copy = pltpu.make_async_remote_copy(
                src_ref=held,
                dst_ref=buf.at[mine],
                send_sem=send.at[k - 1],
                recv_sem=recv.at[k - 1],
                device_id=who((mine + k) % size),
                device_id_type=MESH,
            )
            copy.start()
            copies.append(copy)
        for k in range(1, size):
            ref = buf.at[(mine + size - k) % size]
            pltpu.make_async_remote_copy(
                src_ref=ref,
                dst_ref=ref,
                send_sem=send.at[k - 1],
                recv_sem=recv.at[k - 1],
                device_id=who((mine + k) % size),
                device_id_type=MESH,
            ).wait_recv()
        total = buf[0]
        for i in range(1, size):
            total = total + buf[i]
        for copy in copies:
            copy.wait_send()
        out[...] = total
        held = out


def total(vec):
    outs = [jax.ShapeDtypeStruct(vec.shape, F32)]
    scratch = [
        pltpu.VMEM((NY * NX,) + vec.shape, F32),
        pltpu.VMEM((NZ * NC,) + vec.shape, F32),
    ] + sems(NY * NX - 1) + sems(NZ * NC - 1)
    return call(total_kernel, outs, scratch, 2, vec)[0]


def add_into(dst, index, first, others):
    def body(i, carry):
        value = first(i).astype(F32)
        for other in others:
            value = value + other[i].astype(F32)
        dst[i] = value.astype(dst.dtype)
        return carry

    lax.fori_loop(0, index, body, 0)


def cot_kernel(cot, uc, out, uc_all, cbuf, abuf, ybuf, bbuf, zbuf, xbuf, *sem):
    y, z, c, x = place()
    greet("xzyc")
    sc, su = Stage("c", sem[0], sem[1]), Stage("x", sem[2], sem[3])
    sy, sz, sx = Stage("y", sem[4], sem[5]), Stage("z", sem[6], sem[7]), Stage("x", sem[8], sem[9])
    sc.start(lambda to: cot.at[to], lambda k: cbuf)
    su.start(lambda to: uc, lambda k: uc_all.at[x])
    uc_all[x] = uc[...]
    sc.arrive(lambda k, frm: cbuf)
    for i in range(NY):
        add_into(abuf.at[i], NZ, lambda j: cot[c, i, j], [cbuf.at[i]])
    sy.start(lambda to: abuf.at[to], lambda k: ybuf.at[k - 1])
    sy.arrive(lambda k, frm: ybuf.at[k - 1])
    add_into(bbuf, NZ, lambda j: abuf[y, j], [ybuf.at[i] for i in range(NY - 1)])
    sz.start(lambda to: bbuf.at[to], lambda k: zbuf.at[k - 1])
    sz.arrive(lambda k, frm: zbuf.at[k - 1])
    value = bbuf[z].astype(F32)
    for i in range(NZ - 1):
        value = value + zbuf[i].astype(F32)
    xbuf[x] = value.astype(BF16)
    sx.start(lambda to: xbuf.at[x], lambda k: xbuf.at[x])
    sx.arrive(lambda k, frm: xbuf.at[frm])
    value = xbuf[0].astype(F32)
    for i in range(1, NX):
        value = value + xbuf[i].astype(F32)
    out[...] = value
    su.arrive(lambda k, frm: uc_all.at[frm])
    for stage in (sc, su, sy, sz, sx):
        stage.finish()


def exchange_cot(cot, uc):
    n, emb = cot.shape[-2:]
    outs = [
        jax.ShapeDtypeStruct((n, emb), F32),
        jax.ShapeDtypeStruct((NX,) + uc.shape, BF16),
    ]
    scratch = [
        pltpu.VMEM((NY, NZ, n, emb), BF16),
        pltpu.VMEM((NY, NZ, n, emb), BF16),
        pltpu.VMEM((NY - 1, NZ, n, emb), BF16),
        pltpu.VMEM((NZ, n, emb), BF16),
        pltpu.VMEM((NZ - 1, n, emb), BF16),
        pltpu.VMEM((NX, n, emb), BF16),
    ]
    for size in (NC, NX, NY, NZ, NX):
        scratch += sems(size - 1)
    return call(cot_kernel, outs, scratch, 3, cot, uc)


def grad_kernel(emb, grads, out, proj_out, cbuf, abuf, ybuf, bbuf, zbuf, xbuf, *sem):
    y, z, c, x = place()
    greet("xzyc")
    sc = Stage("c", sem[0], sem[1])
    sy, sz, sx = Stage("y", sem[2], sem[3]), Stage("z", sem[4], sem[5]), Stage("x", sem[6], sem[7])
    sc.start(lambda to: grads.at[to], lambda k: cbuf)
    sc.arrive(lambda k, frm: cbuf)
    for i in range(NY):
        add_into(abuf.at[i], NZ, lambda j: grads[c, i, j], [cbuf.at[i]])
    sy.start(lambda to: abuf.at[to], lambda k: ybuf.at[k - 1])
    sy.arrive(lambda k, frm: ybuf.at[k - 1])
    add_into(bbuf, NZ, lambda j: abuf[y, j], [ybuf.at[i] for i in range(NY - 1)])
    sz.start(lambda to: bbuf.at[to], lambda k: zbuf.at[k - 1])
    sz.arrive(lambda k, frm: zbuf.at[k - 1])
    value = bbuf[z].astype(F32)
    for i in range(NZ - 1):
        value = value + zbuf[i].astype(F32)
    width = value.shape[1] - emb
    out[...] = value[:, :width]
    xbuf[x] = value[:, width:]
    sx.start(lambda to: xbuf.at[x], lambda k: xbuf.at[x])
    sx.arrive(lambda k, frm: xbuf.at[frm])
    value = xbuf[0]
    for i in range(1, NX):
        value = value + xbuf[i]
    proj_out[...] = value
    for stage in (sc, sy, sz, sx):
        stage.finish()


def exchange_grads(grads, emb):
    n, width = grads.shape[-2:]
    outs = [
        jax.ShapeDtypeStruct((n, width - emb), F32),
        jax.ShapeDtypeStruct((n, emb), F32),
    ]
    scratch = [
        pltpu.VMEM((NY, NZ, n, width), BF16),
        pltpu.VMEM((NY, NZ, n, width), BF16),
        pltpu.VMEM((NY - 1, NZ, n, width), BF16),
        pltpu.VMEM((NZ, n, width), BF16),
        pltpu.VMEM((NZ - 1, n, width), BF16),
        pltpu.VMEM((NX, n, emb), F32),
    ]
    for size in (NC, NY, NZ, NX):
        scratch += sems(size - 1)
    return call(functools.partial(grad_kernel, emb), outs, scratch, 4, grads)


def unit_cotangent(g, unit, inverse):
    along = jnp.sum(g * unit, axis=-1, keepdims=True)
    return (inverse * (g - unit * along)).astype(BF16)


def local(
    passage_states,
    query_states,
    lengths,
    owner_map,
    candidates,
    teacher_scores,
    up_weight,
    down_weight,
    proj_weight,
):
    p_dev, pass_len, width = passage_states.shape
    q_dev, q_len, _ = query_states.shape
    emb = proj_weight.shape[1]
    hidden = up_weight.shape[1]
    n_dp = NY * NZ * NC
    me_dp, me_mp = lax.axis_index("dp"), lax.axis_index("mp")
    y, z, c, _ = place()
    my_block = (c * NY + y) * NZ + z
    p_own = p_dev // NX
    q_rows = q_dev * q_len
    q_own = q_rows // NX
    queries = n_dp * q_dev
    cands = candidates.shape[1]
    all_cands = cands * NX

    rows_q = query_states.reshape(q_rows, width)
    pre_q = dot(rows_q, up_weight, ((1,), (0,)))
    hid_q = jax.nn.gelu(pre_q).astype(BF16)
    part_q = dot(hid_q, down_weight, ((1,), (0,))).astype(BF16)
    pre_p = dot(passage_states, up_weight, ((2,), (0,)))
    hid_p = jax.nn.gelu(pre_p).astype(BF16)
    part_p = dot(hid_p, down_weight, ((2,), (0,))).astype(BF16)

    positions = jnp.take(owner_map, candidates).astype(F32)
    table = jnp.zeros((8, 2 * all_cands), F32)
    table = lax.dynamic_update_slice(table, positions, (0, me_mp * cands))
    table = lax.dynamic_update_slice(table, teacher_scores, (0, all_cands + me_mp * cands))

    part_p, part_q = lax.optimization_barrier((part_p, part_q))
    ffn_p = lax.psum_scatter(part_p, "mp", scatter_dimension=0, tiled=True)
    q_all, t_all, mixed_q, unit_q, inv_q = gather_queries(part_q, rows_q, proj_weight, table)
    q_all = q_all.reshape(n_dp * q_rows, emb)
    table = t_all.reshape(n_dp, 8, 2 * all_cands)[:, :q_dev].reshape(queries, -1)
    pos_all, teacher = table[:, :all_cands], table[:, all_cands:]
    teacher_exp = jnp.exp(teacher)
    teacher_sum = jnp.sum(teacher_exp, axis=1)
    teacher_dot = jnp.sum(teacher_exp * teacher, axis=1)
    base = me_dp * p_dev + me_mp * p_own
    mine = base + jnp.arange(p_own)
    hit = pos_all[None] == mine[:, None, None].astype(F32)
    count = jnp.sum(hit.astype(F32), axis=2)
    teacher_mass = jnp.sum(jnp.where(hit, teacher_exp[None], 0.0), axis=2)

    own_p = lax.dynamic_slice_in_dim(passage_states, me_mp * p_own, p_own, 0)
    mixed_p = (own_p.astype(F32) + ffn_p.astype(F32)).astype(BF16)
    projected = dot(mixed_p, proj_weight, ((2,), (0,)))
    inv_p = lax.rsqrt(jnp.sum(projected * projected, axis=-1, keepdims=True) + EPS)
    unit_p = projected * inv_p
    emb_p = unit_p.astype(BF16)

    own_len = lax.dynamic_slice_in_dim(lengths, base, p_own, 0)
    similar = dot(emb_p, q_all, ((2,), (1,)))
    live = jnp.arange(pass_len)[None, :] < own_len[:, None]
    terms = jnp.where(live[:, :, None], jnp.exp(similar / TAU), 0.0)
    denom = jnp.sum(terms, axis=1)
    scores = TAU * jnp.sum(jnp.log(denom).reshape(p_own, queries, q_len), axis=2)
    student = count * jnp.exp(scores)
    sums = jnp.stack([jnp.sum(student, axis=0), jnp.sum(teacher_mass * scores, axis=0)])
    sums = jnp.pad(sums.reshape(-1), (0, 1024 - 2 * queries)).reshape(8, 128)
    sums = total(sums).reshape(-1)[: 2 * queries].reshape(2, queries)
    student_sum = sums[0]
    loss = (teacher_dot - sums[1]) / teacher_sum - jnp.log(teacher_sum) + jnp.log(student_sum)
    query_loss = lax.dynamic_slice_in_dim(loss, my_block * q_dev, q_dev, 0)
    score_cot = student / student_sum - teacher_mass / teacher_sum
    scale = (score_cot[:, :, None] / denom.reshape(p_own, queries, q_len)).reshape(p_own, 1, -1)
    weights = (terms * scale).astype(BF16)
    cot_q = dot(weights, emb_p, ((0, 1), (0, 1))).astype(BF16)
    cot_p = dot(weights, q_all, ((2,), (0,)))
    uc_p = unit_cotangent(cot_p, unit_p, inv_p)

    pad_len = (pass_len + 15) // 16 * 16
    cot_q, uc_all = exchange_cot(
        cot_q.reshape(NC, NY, NZ, q_rows, emb),
        jnp.pad(uc_p, ((0, 0), (0, pad_len - pass_len), (0, 0))),
    )
    uc_q = unit_cotangent(cot_q, unit_q, inv_q)
    own_mixed = lax.dynamic_slice_in_dim(mixed_q, me_mp * q_own, q_own, 0)
    own_uc = lax.dynamic_slice_in_dim(uc_q, me_mp * q_own, q_own, 0)
    grad_proj = dot(mixed_p, uc_p, ((0, 1), (0, 1))) + dot(own_mixed, own_uc, ((0,), (0,)))
    uc_p = uc_all.reshape(p_dev, pad_len, emb)[:, :pass_len]

    def back(rows, pre, hid, uc):
        axes = tuple(range(rows.ndim - 1))
        last = (rows.ndim - 1,)
        mixed_cot = dot(uc, proj_weight, (last, (1,))).astype(BF16)
        down = dot(mixed_cot, hid, (axes, axes))
        hid_cot = dot(mixed_cot, down_weight, (last, (1,)))
        pre_cot = jax.vjp(jax.nn.gelu, pre)[1](hid_cot)[0].astype(BF16)
        return dot(rows, pre_cot, (axes, axes)), down

    up_p, down_p = back(passage_states, pre_p, hid_p, uc_p)
    up_q, down_q = back(rows_q, pre_q, hid_q, uc_q)
    grads = jnp.concatenate([up_p + up_q, down_p + down_q, grad_proj], axis=1).astype(BF16)
    rows = width // n_dp
    grads = jnp.pad(grads.reshape(NY, NZ, NC, rows, -1), ((0, 0),) * 3 + ((0, -rows % 16), (0, 0)))
    grads, grad_proj = exchange_grads(jnp.transpose(grads, (2, 0, 1, 3, 4)), emb)
    return (
        query_loss,
        grads[:rows, :hidden],
        grads[:rows, hidden:].T,
        grad_proj[:rows],
    )


def solution(mesh):
    return jax.shard_map(
        local,
        mesh=mesh,
        in_specs=(
            P("dp", None, None),
            P("dp", None, None),
            P(),
            P(),
            P("dp", "mp"),
            P("dp", "mp"),
            P(None, "mp"),
            P("mp", None),
            P(),
        ),
        out_specs=(P("dp"), P("dp", "mp"), P("mp", "dp"), P("dp", None)),
        check_vma=False,
    )
```

```python
import functools

import jax
import jax.numpy as jnp
from jax import lax
from jax.experimental import pallas as pl
from jax.experimental.pallas import tpu as pltpu
from jax.sharding import PartitionSpec as P

TAU = 0.05
EPS = 1e-06
F32 = jnp.float32
BF16 = jnp.bfloat16
NY, NZ, NC, NX = 4, 8, 2, 4
MESH = pl.DeviceIdType.MESH
VMEM = pl.BlockSpec(memory_space=pltpu.VMEM)


def dot(a, b, dims):
    return lax.dot_general(a, b, (dims, ((), ())), preferred_element_type=F32)


def place():
    dp, x = lax.axis_index("dp"), lax.axis_index("mp")
    return dp // (NZ * NC), (dp // NC) % NZ, dp % NC, x


def at(y, z, c, x):
    return ((y * NZ + z) * NC + c, x)


def peers(axis):
    y, z, c, x = place()
    out = []
    size = {"x": NX, "y": NY, "z": NZ, "c": NC}[axis]
    mine = {"x": x, "y": y, "z": z, "c": c}[axis]
    for k in range(1, size):
        to = (mine + k) % size
        frm = (mine + size - k) % size
        who = {"x": (y, z, c, to), "y": (to, z, c, x), "z": (y, to, c, x), "c": (y, z, to, x)}[axis]
        out.append((k, at(*who), to, frm))
    return out


def greet(axes):
    barrier = pltpu.get_barrier_semaphore()
    total = 0
    for axis in axes:
        for _, who, _, _ in peers(axis):
            pl.semaphore_signal(barrier, inc=1, device_id=who, device_id_type=MESH)
            total += 1
    pl.semaphore_wait(barrier, total)


class Stage:
    def __init__(self, axis, send_sem, recv_sem):
        self.axis, self.send_sem, self.recv_sem = axis, send_sem, recv_sem
        self.sent = []

    def start(self, src, dst):
        for k, who, to, _ in peers(self.axis):
            copy = pltpu.make_async_remote_copy(
                src_ref=src(to),
                dst_ref=dst(k),
                send_sem=self.send_sem.at[k - 1],
                recv_sem=self.recv_sem.at[k - 1],
                device_id=who,
                device_id_type=MESH,
            )
            copy.start()
            self.sent.append(copy)

    def arrive(self, dst):
        for k, who, _, frm in peers(self.axis):
            ref = dst(k, frm)
            pltpu.make_async_remote_copy(
                src_ref=ref,
                dst_ref=ref,
                send_sem=self.send_sem.at[k - 1],
                recv_sem=self.recv_sem.at[k - 1],
                device_id=who,
                device_id_type=MESH,
            ).wait_recv()

    def finish(self):
        for copy in self.sent:
            copy.wait_send()


def sems(n):
    return [pltpu.SemaphoreType.DMA((max(n, 1),)), pltpu.SemaphoreType.DMA((max(n, 1),))]


def call(kernel, outs, scratch, number, *args):
    return pl.pallas_call(
        kernel,
        out_shape=outs,
        in_specs=[VMEM] * len(args),
        out_specs=[VMEM] * len(outs),
        scratch_shapes=scratch,
        compiler_params=pltpu.CompilerParams(
            collective_id=number, has_side_effects=True, vmem_limit_bytes=56 * 2**20
        ),
        cost_estimate=pl.CostEstimate(flops=10**9, bytes_accessed=60 * 10**6, transcendentals=0),
    )(*args)


def gather_kernel(
    part, rows, proj, table, q_all, t_all, mixed, unit, inverse, pbuf, tbuf, *sem
):
    y, z, c, x = place()
    greet("xzyc")
    sx, tx = Stage("x", sem[0], sem[1]), Stage("x", sem[2], sem[3])
    sz, tz = Stage("z", sem[4], sem[5]), Stage("z", sem[6], sem[7])
    sy, ty = Stage("y", sem[8], sem[9]), Stage("y", sem[10], sem[11])
    sc, tc = Stage("c", sem[12], sem[13]), Stage("c", sem[14], sem[15])
    tx.start(lambda to: table, lambda k: tbuf.at[x])
    sx.start(lambda to: part, lambda k: pbuf.at[x])
    tbuf[x] = table[...]
    pbuf[x] = part[...]
    tx.arrive(lambda k, frm: tbuf.at[frm])
    merged = tbuf[0]
    for i in range(1, NX):
        merged = merged + tbuf[i]
    t_all[c, y, z] = merged
    tz.start(lambda to: t_all.at[c, y, z], lambda k: t_all.at[c, y, z])
    sx.arrive(lambda k, frm: pbuf.at[frm])
    ffn = pbuf[0].astype(F32)
    for i in range(1, NX):
        ffn = ffn + pbuf[i].astype(F32)
    blend = (rows[...].astype(F32) + ffn).astype(BF16)
    mixed[...] = blend
    projected = jnp.dot(blend, proj[...], preferred_element_type=F32)
    inv = lax.rsqrt(jnp.sum(projected * projected, axis=-1, keepdims=True) + EPS)
    inverse[...] = inv
    unit[...] = projected * inv
    q_all[c, y, z] = (projected * inv).astype(BF16)
    sz.start(lambda to: q_all.at[c, y, z], lambda k: q_all.at[c, y, z])
    tz.arrive(lambda k, frm: t_all.at[c, y, frm])
    ty.start(lambda to: t_all.at[c, y], lambda k: t_all.at[c, y])
    sz.arrive(lambda k, frm: q_all.at[c, y, frm])
    sy.start(lambda to: q_all.at[c, y], lambda k: q_all.at[c, y])
    ty.arrive(lambda k, frm: t_all.at[c, frm])
    tc.start(lambda to: t_all.at[c], lambda k: t_all.at[c])
    sy.arrive(lambda k, frm: q_all.at[c, frm])
    sc.start(lambda to: q_all.at[c], lambda k: q_all.at[c])
    tc.arrive(lambda k, frm: t_all.at[frm])
    sc.arrive(lambda k, frm: q_all.at[frm])
    for stage in (sx, tx, sz, tz, sy, ty, sc, tc):
        stage.finish()


def gather_queries(part, rows, proj, table):
    n, width = part.shape
    emb = proj.shape[1]
    shape = jax.ShapeDtypeStruct
    outs = [
        shape((NC, NY, NZ, n, emb), BF16),
        shape((NC, NY, NZ) + table.shape, F32),
        shape((n, width), BF16),
        shape((n, emb), F32),
        shape((n, 1), F32),
    ]
    scratch = [pltpu.VMEM((NX, n, width), BF16), pltpu.VMEM((NX,) + table.shape, F32)]
    for size in (NX, NX, NZ, NZ, NY, NY, NC, NC):
        scratch += sems(size - 1)
    return call(gather_kernel, outs, scratch, 1, part, rows, proj, table)


def total_kernel(vec, out, abuf, bbuf, *sem):
    y, z, c, x = place()
    barrier = pltpu.get_barrier_semaphore()
    groups = [
        (NY * NX, y * NX + x, lambda i: at(i // NX, z, c, i % NX)),
        (NZ * NC, z * NC + c, lambda i: at(y, i // NC, i % NC, x)),
    ]
    for size, mine, who in groups:
        for k in range(1, size):
            pl.semaphore_signal(
                barrier, inc=1, device_id=who((mine + k) % size), device_id_type=MESH
            )
    pl.semaphore_wait(barrier, NY * NX + NZ * NC - 2)
    held = vec
    for (size, mine, who), buf, send, recv in zip(
        groups, (abuf, bbuf), (sem[0], sem[2]), (sem[1], sem[3])
    ):
        copies = []
        buf[mine] = held[...]
        for k in range(1, size):
            copy = pltpu.make_async_remote_copy(
                src_ref=held,
                dst_ref=buf.at[mine],
                send_sem=send.at[k - 1],
                recv_sem=recv.at[k - 1],
                device_id=who((mine + k) % size),
                device_id_type=MESH,
            )
            copy.start()
            copies.append(copy)
        for k in range(1, size):
            ref = buf.at[(mine + size - k) % size]
            pltpu.make_async_remote_copy(
                src_ref=ref,
                dst_ref=ref,
                send_sem=send.at[k - 1],
                recv_sem=recv.at[k - 1],
                device_id=who((mine + k) % size),
                device_id_type=MESH,
            ).wait_recv()
        total = buf[0]
        for i in range(1, size):
            total = total + buf[i]
        for copy in copies:
            copy.wait_send()
        out[...] = total
        held = out


def total(vec):
    outs = [jax.ShapeDtypeStruct(vec.shape, F32)]
    scratch = [
        pltpu.VMEM((NY * NX,) + vec.shape, F32),
        pltpu.VMEM((NZ * NC,) + vec.shape, F32),
    ] + sems(NY * NX - 1) + sems(NZ * NC - 1)
    return call(total_kernel, outs, scratch, 2, vec)[0]


def add_into(dst, index, first, others):
    def body(i, carry):
        value = first(i).astype(F32)
        for other in others:
            value = value + other[i].astype(F32)
        dst[i] = value.astype(dst.dtype)
        return carry

    lax.fori_loop(0, index, body, 0)


def nt(a, b):
    return dot(a, b, ((1,), (1,)))


TILE = 256


def back_kernel(
    cot, uc, rows, hid, dgelu, mixed, rows_q, hid_q, dgelu_q, mixed_q, unit_q, inv_q, down, proj,
    projp, perm,
    out_up, out_down, out_proj,
    uc_all, cbuf, abuf, ybuf, bbuf, zbuf, xbuf, mc, mct, rowst, mixedt, mcq, mctq, rowstq, ucq,
    acc_up, acc_down, acc_proj,
    gd, gu, gp, cd, cu, cp, ad, au, ap, yd, yu, yp, fd, fu, fp, bd, bu, bp, zd, zu, zp, xp, *sem
):
    y, z, c, x = place()
    sem = list(sem)

    def stage(axis):
        send, recv = sem.pop(0), sem.pop(0)
        return Stage(axis, send, recv)

    greet("xzyc")
    sc, su, sy, sz, sx = (stage(a) for a in "cxyzx")
    sc.start(lambda to: cot.at[to], lambda k: cbuf)
    su.start(lambda to: uc, lambda k: uc_all.at[x])
    uc_all[x] = uc[...]
    width = down.shape[1]
    tiles = width // TILE

    def cut(j):
        return pl.ds(pl.multiple_of(j * TILE, TILE), TILE)

    def prepare(u, r, m, mt, rt):
        def body(j, carry):
            m[:, cut(j)] = nt(u[...], proj[cut(j), :]).astype(BF16)
            mt[cut(j), :] = nt(projp[cut(j), :], u[...]).astype(BF16)
            rt[cut(j), :] = nt(perm[cut(j), :], r[...]).astype(BF16)
            return carry

        lax.fori_loop(0, tiles, body, 0)

    def passages(g, first):
        u, r = uc_all.at[g], rows.at[g]
        prepare(u, r, mc, mct, rowst)

        def body(j, carry):
            term = jnp.dot(mct[...], hid[g, :, cut(j)], preferred_element_type=F32)
            back = nt(mc[...], down[cut(j), :])
            pre = (back * dgelu[g, :, cut(j)]).astype(BF16)
            up = jnp.dot(rowst[...], pre, preferred_element_type=F32)
            if first:
                acc_down[:, cut(j)] = term
                acc_up[:, cut(j)] = up
            else:
                acc_down[:, cut(j)] += term
                acc_up[:, cut(j)] += up
            return carry

        lax.fori_loop(0, tiles, body, 0)

    passages(x, True)

    def mix(j, carry):
        mixedt[cut(j), :] = nt(perm[cut(j), :], mixed[...]).astype(BF16)
        return carry

    lax.fori_loop(0, tiles, mix, 0)
    acc_proj[...] = jnp.dot(mixedt[...], uc[...], preferred_element_type=F32)

    sc.arrive(lambda k, frm: cbuf)
    for i in range(NY):
        add_into(abuf.at[i], NZ, lambda j: cot[c, i, j], [cbuf.at[i]])
    sy.start(lambda to: abuf.at[to], lambda k: ybuf.at[k - 1])
    su.arrive(lambda k, frm: uc_all.at[frm])
    passages(lax.rem(x + 3, NX), False)
    sy.arrive(lambda k, frm: ybuf.at[k - 1])
    add_into(bbuf, NZ, lambda j: abuf[y, j], [ybuf.at[i] for i in range(NY - 1)])
    sz.start(lambda to: bbuf.at[to], lambda k: zbuf.at[k - 1])
    passages(lax.rem(x + 1, NX), False)
    sz.arrive(lambda k, frm: zbuf.at[k - 1])
    value = bbuf[z].astype(F32)
    for i in range(NZ - 1):
        value = value + zbuf[i].astype(F32)
    xbuf[x] = value.astype(BF16)
    sx.start(lambda to: xbuf.at[x], lambda k: xbuf.at[x])
    passages(lax.rem(x + 2, NX), False)
    sx.arrive(lambda k, frm: xbuf.at[frm])
    g = xbuf[0].astype(F32)
    for i in range(1, NX):
        g = g + xbuf[i].astype(F32)
    along = jnp.sum(g * unit_q[...], axis=-1, keepdims=True)
    n = g.shape[0]
    ucq[...] = jnp.zeros(ucq.shape, BF16)
    ucq[0:n, :] = (inv_q[...] * (g - unit_q[...] * along)).astype(BF16)
    prepare(ucq, rows_q, mcq, mctq, rowstq)
    blocks = gd.shape[:3]

    def down_last(j, carry):
        term = acc_down[:, cut(j)] + jnp.dot(
            mctq[...], hid_q[:, cut(j)], preferred_element_type=F32
        )
        gd[:, :, :, cut(j)] = term.astype(BF16).reshape(blocks + (TILE,))
        return carry

    lax.fori_loop(0, tiles, down_last, 0)
    chunks = []
    for grads, near, total_a, far, f32_sum, padded, last in (
        (gd, cd, ad, yd, fd, bd, zd),
        (gp, cp, ap, yp, fp, bp, zp),
        (gu, cu, au, yu, fu, bu, zu),
    ):
        chunks.append((grads, near, total_a, far, f32_sum, padded, last) + tuple(stage(a) for a in "cyz"))

    def leave(chunk):
        chunk[7].start(lambda to: chunk[0].at[to], lambda k: chunk[1])

    leave(chunks[0])

    def mixq(j, carry):
        mctq[cut(j), :] = nt(perm[cut(j), :], mixed_q[...]).astype(BF16)
        return carry

    lax.fori_loop(0, tiles, mixq, 0)
    part = n // NX
    at_row = lax.broadcasted_iota(jnp.int32, ucq.shape, 0)
    mine = jnp.logical_and(at_row >= x * part, at_row < (x + 1) * part)
    own = jnp.where(mine, ucq[...].astype(F32), 0.0).astype(BF16)
    term = acc_proj[...] + jnp.dot(mctq[...], own, preferred_element_type=F32)
    gp[...] = term.astype(BF16).reshape(gp.shape)
    leave(chunks[1])

    def up_last(j, carry):
        back = nt(mcq[...], down[cut(j), :])
        pre = (back * dgelu_q[:, cut(j)]).astype(BF16)
        up = acc_up[:, cut(j)] + jnp.dot(rowstq[...], pre, preferred_element_type=F32)
        gu[:, :, :, cut(j)] = up.astype(BF16).reshape(blocks + (TILE,))
        return carry

    lax.fori_loop(0, tiles, up_last, 0)
    leave(chunks[2])

    for grads, near, total_a, far, f32_sum, padded, last, s1, s2, s3 in chunks:
        s1.arrive(lambda k, frm: near)
        add_into(total_a, NY, lambda j: grads[c, j], [near])
        s2.start(lambda to: total_a.at[to], lambda k: far.at[k - 1])
    per = width // (NY * NZ * NC)
    for grads, near, total_a, far, f32_sum, padded, last, s1, s2, s3 in chunks:
        s2.arrive(lambda k, frm: far.at[k - 1])
        value = total_a[y].astype(F32)
        for i in range(NY - 1):
            value = value + far[i].astype(F32)
        tall = value.shape[0]
        f32_sum[0:tall, :] = value
        f32_sum[tall : tall + 8, :] = jnp.zeros((8, value.shape[1]), F32)
        for i in range(NZ):
            padded[i] = f32_sum[i * per : i * per + 16, :].astype(BF16)
        s3.start(lambda to: padded.at[to], lambda k: last.at[k - 1])
    finals = []
    s4 = stage("x")
    for at_chunk in (1, 0, 2):
        grads, near, total_a, far, f32_sum, padded, last, s1, s2, s3 = chunks[at_chunk]
        s3.arrive(lambda k, frm: last.at[k - 1])
        value = padded[z].astype(F32)
        for i in range(NZ - 1):
            value = value + last[i].astype(F32)
        if at_chunk == 1:
            xp[x] = value
            s4.start(lambda to: xp.at[x], lambda k: xp.at[x])
        elif at_chunk == 0:
            out_down[...] = value
        else:
            out_up[...] = value
    s4.arrive(lambda k, frm: xp.at[frm])
    value = xp[0]
    for i in range(1, NX):
        value = value + xp[i]
    out_proj[...] = value
    for s in [sc, su, sy, sz, sx, s4] + [s for chunk in chunks for s in chunk[7:]]:
        s.finish()


def backward(*args):
    cot, uc, rows, hid, _, _, rows_q = args[:7]
    n, emb = cot.shape[-2:]
    many, width = rows.shape[1:]
    hidden = hid.shape[2]
    few = rows_q.shape[0]
    tall = width // (NC * NY)
    V = pltpu.VMEM
    outs = [jax.ShapeDtypeStruct((16, w), F32) for w in (hidden, hidden, emb)]
    scratch = [
        V((NX, many, emb), BF16),
        V((NY, NZ, n, emb), BF16),
        V((NY, NZ, n, emb), BF16),
        V((NY - 1, NZ, n, emb), BF16),
        V((NZ, n, emb), BF16),
        V((NZ - 1, n, emb), BF16),
        V((NX, n, emb), BF16),
        V((many, width), BF16),
        V((width, many), BF16),
        V((width, many), BF16),
        V((width, many), BF16),
        V((few, width), BF16),
        V((width, few), BF16),
        V((width, few), BF16),
        V((few, emb), BF16),
        V((width, hidden), F32),
        V((width, hidden), F32),
        V((width, emb), F32),
    ]
    wide = (hidden, hidden, emb)
    scratch += [V((NC, NY, tall, w), BF16) for w in wide]
    scratch += [V((NY, tall, w), BF16) for w in wide]
    scratch += [V((NY, tall, w), BF16) for w in wide]
    scratch += [V((NY - 1, tall, w), BF16) for w in wide]
    scratch += [V((tall + 8, w), F32) for w in wide]
    scratch += [V((NZ, 16, w), BF16) for w in wide]
    scratch += [V((NZ - 1, 16, w), BF16) for w in wide]
    scratch += [V((NX, 16, emb), F32)]
    for a in "cxyzx" + "cyz" * 3 + "x":
        scratch += sems({"x": NX, "y": NY, "z": NZ, "c": NC}[a] - 1)
    return call(back_kernel, outs, scratch, 3, *args)


def unit_cotangent(g, unit, inverse):
    along = jnp.sum(g * unit, axis=-1, keepdims=True)
    return (inverse * (g - unit * along)).astype(BF16)


def gelu_slope(v):
    return jax.vjp(jax.nn.gelu, v)[1](jnp.ones_like(v))[0]


def local(
    passage_states,
    query_states,
    lengths,
    owner_map,
    candidates,
    teacher_scores,
    up_weight,
    down_weight,
    proj_weight,
):
    p_dev, pass_len, width = passage_states.shape
    q_dev, q_len, _ = query_states.shape
    emb = proj_weight.shape[1]
    hidden = up_weight.shape[1]
    n_dp = NY * NZ * NC
    me_dp, me_mp = lax.axis_index("dp"), lax.axis_index("mp")
    y, z, c, _ = place()
    my_block = (c * NY + y) * NZ + z
    p_own = p_dev // NX
    q_rows = q_dev * q_len
    rows = width // n_dp
    queries = n_dp * q_dev
    cands = candidates.shape[1]
    all_cands = cands * NX

    pad_len = (pass_len + 15) // 16 * 16
    passage_states = jnp.pad(passage_states, ((0, 0), (0, pad_len - pass_len), (0, 0)))
    rows_q = query_states.reshape(q_rows, width)
    pre_q = dot(rows_q, up_weight, ((1,), (0,)))
    hid_q = jax.nn.gelu(pre_q).astype(BF16)
    part_q = dot(hid_q, down_weight, ((1,), (0,))).astype(BF16)
    pre_p = dot(passage_states, up_weight, ((2,), (0,)))
    hid_p = jax.nn.gelu(pre_p).astype(BF16)
    part_p = dot(hid_p, down_weight, ((2,), (0,))).astype(BF16)

    positions = jnp.take(owner_map, candidates).astype(F32)
    table = jnp.zeros((8, 2 * all_cands), F32)
    table = lax.dynamic_update_slice(table, positions, (0, me_mp * cands))
    table = lax.dynamic_update_slice(table, teacher_scores, (0, all_cands + me_mp * cands))

    part_p, part_q = lax.optimization_barrier((part_p, part_q))
    ffn_p = lax.psum_scatter(part_p, "mp", scatter_dimension=0, tiled=True)
    q_all, t_all, mixed_q, unit_q, inv_q = gather_queries(part_q, rows_q, proj_weight, table)
    q_all, pre_p, pre_q = lax.optimization_barrier((q_all, pre_p, pre_q))
    dgelu_p, dgelu_q = gelu_slope(pre_p), gelu_slope(pre_q)
    q_all = q_all.reshape(n_dp * q_rows, emb)
    table = t_all.reshape(n_dp, 8, 2 * all_cands)[:, :q_dev].reshape(queries, -1)
    pos_all, teacher = table[:, :all_cands], table[:, all_cands:]
    teacher_exp = jnp.exp(teacher)
    teacher_sum = jnp.sum(teacher_exp, axis=1)
    teacher_dot = jnp.sum(teacher_exp * teacher, axis=1)
    base = me_dp * p_dev + me_mp * p_own
    mine = base + jnp.arange(p_own)
    hit = pos_all[None] == mine[:, None, None].astype(F32)
    count = jnp.sum(hit.astype(F32), axis=2)
    teacher_mass = jnp.sum(jnp.where(hit, teacher_exp[None], 0.0), axis=2)

    own_p = lax.dynamic_slice_in_dim(passage_states, me_mp * p_own, p_own, 0)
    mixed_p = (own_p.astype(F32) + ffn_p.astype(F32)).astype(BF16)
    projected = dot(mixed_p, proj_weight, ((2,), (0,)))
    inv_p = lax.rsqrt(jnp.sum(projected * projected, axis=-1, keepdims=True) + EPS)
    unit_p = projected * inv_p
    emb_p = unit_p.astype(BF16)

    own_len = lax.dynamic_slice_in_dim(lengths, base, p_own, 0)
    similar = dot(emb_p, q_all, ((2,), (1,)))
    live = jnp.arange(pad_len)[None, :] < own_len[:, None]
    terms = jnp.where(live[:, :, None], jnp.exp(similar / TAU), 0.0)
    denom = jnp.sum(terms, axis=1)
    scores = TAU * jnp.sum(jnp.log(denom).reshape(p_own, queries, q_len), axis=2)
    student = count * jnp.exp(scores)
    sums = jnp.stack([jnp.sum(student, axis=0), jnp.sum(teacher_mass * scores, axis=0)])
    sums = jnp.pad(sums.reshape(-1), (0, 1024 - 2 * queries)).reshape(8, 128)
    sums = total(sums).reshape(-1)[: 2 * queries].reshape(2, queries)
    student_sum = sums[0]
    loss = (teacher_dot - sums[1]) / teacher_sum - jnp.log(teacher_sum) + jnp.log(student_sum)
    query_loss = lax.dynamic_slice_in_dim(loss, my_block * q_dev, q_dev, 0)
    score_cot = student / student_sum - teacher_mass / teacher_sum
    scale = (score_cot[:, :, None] / denom.reshape(p_own, queries, q_len)).reshape(p_own, 1, -1)
    weights = (terms * scale).astype(BF16)
    cot_q = dot(weights, emb_p, ((0, 1), (0, 1))).astype(BF16)
    cot_p = dot(weights, q_all, ((2,), (0,)))
    uc_p = unit_cotangent(cot_p, unit_p, inv_p)

    few = (q_rows + 127) // 128 * 128
    more = ((0, few - q_rows), (0, 0))
    order = jnp.arange(width).reshape(NC, NY, NZ, rows)
    order = (((order // (NZ * rows)) % NY * NZ + (order // rows) % NZ) * NC + order // (NY * NZ * rows)) * rows
    order = (order + jnp.arange(rows)).reshape(width)
    perm = (order[:, None] == jnp.arange(width)[None, :]).astype(BF16)
    proj_order = jnp.transpose(proj_weight.reshape(NY, NZ, NC, rows, emb), (2, 0, 1, 3, 4))
    up, down, grad_proj = backward(
        cot_q.reshape(NC, NY, NZ, q_rows, emb),
        uc_p.reshape(p_own * pad_len, emb),
        passage_states.reshape(NX, p_own * pad_len, width),
        hid_p.reshape(NX, p_own * pad_len, hidden),
        dgelu_p.reshape(NX, p_own * pad_len, hidden),
        mixed_p.reshape(p_own * pad_len, width),
        jnp.pad(rows_q, more),
        jnp.pad(hid_q, more),
        jnp.pad(dgelu_q, more),
        jnp.pad(mixed_q, more),
        unit_q,
        inv_q,
        down_weight,
        proj_weight,
        proj_order.reshape(width, emb),
        perm,
    )
    return query_loss, up[:rows], down[:rows].T, grad_proj[:rows]


def solution(mesh):
    return jax.shard_map(
        local,
        mesh=mesh,
        in_specs=(
            P("dp", None, None),
            P("dp", None, None),
            P(),
            P(),
            P("dp", "mp"),
            P("dp", "mp"),
            P(None, "mp"),
            P("mp", None),
            P(),
        ),
        out_specs=(P("dp"), P("dp", "mp"), P("mp", "dp"), P("dp", None)),
        check_vma=False,
    )
```

```python
import functools

import jax
import numpy as np
import jax.numpy as jnp
from jax import lax
from jax.experimental import pallas as pl
from jax.experimental.pallas import tpu as pltpu
from jax.sharding import PartitionSpec as P

TAU = 0.05
EPS = 1e-06
F32 = jnp.float32
BF16 = jnp.bfloat16
NY, NZ, NC, NX = 4, 8, 2, 4
MESH = pl.DeviceIdType.MESH
VMEM = pl.BlockSpec(memory_space=pltpu.VMEM)


def dot(a, b, dims):
    return lax.dot_general(a, b, (dims, ((), ())), preferred_element_type=F32)


def place():
    dp, x = lax.axis_index("dp"), lax.axis_index("mp")
    return dp // (NZ * NC), (dp // NC) % NZ, dp % NC, x


def at(y, z, c, x):
    return ((y * NZ + z) * NC + c, x)


def peers(axis):
    y, z, c, x = place()
    out = []
    size = {"x": NX, "y": NY, "z": NZ, "c": NC}[axis]
    mine = {"x": x, "y": y, "z": z, "c": c}[axis]
    for k in range(1, size):
        to = (mine + k) % size
        frm = (mine + size - k) % size
        who = {"x": (y, z, c, to), "y": (to, z, c, x), "z": (y, to, c, x), "c": (y, z, to, x)}[axis]
        out.append((k, at(*who), to, frm))
    return out


def greet(axes):
    barrier = pltpu.get_barrier_semaphore()
    total = 0
    for axis in axes:
        for _, who, _, _ in peers(axis):
            pl.semaphore_signal(barrier, inc=1, device_id=who, device_id_type=MESH)
            total += 1
    pl.semaphore_wait(barrier, total)


class Stage:
    def __init__(self, axis, send_sem, recv_sem):
        self.axis, self.send_sem, self.recv_sem = axis, send_sem, recv_sem
        self.sent = []

    def start(self, src, dst):
        for k, who, to, _ in peers(self.axis):
            copy = pltpu.make_async_remote_copy(
                src_ref=src(to),
                dst_ref=dst(k),
                send_sem=self.send_sem.at[k - 1],
                recv_sem=self.recv_sem.at[k - 1],
                device_id=who,
                device_id_type=MESH,
            )
            copy.start()
            self.sent.append(copy)

    def arrive(self, dst):
        for k, who, _, frm in peers(self.axis):
            ref = dst(k, frm)
            pltpu.make_async_remote_copy(
                src_ref=ref,
                dst_ref=ref,
                send_sem=self.send_sem.at[k - 1],
                recv_sem=self.recv_sem.at[k - 1],
                device_id=who,
                device_id_type=MESH,
            ).wait_recv()

    def finish(self):
        for copy in self.sent:
            copy.wait_send()


def sems(n):
    return [pltpu.SemaphoreType.DMA((max(n, 1),)), pltpu.SemaphoreType.DMA((max(n, 1),))]


def call(kernel, outs, scratch, number, *args, outer=((), ())):
    def spec(i, which):
        return pl.BlockSpec(memory_space=pl.ANY) if i in which else VMEM

    return pl.pallas_call(
        kernel,
        out_shape=outs,
        in_specs=[spec(i, outer[0]) for i in range(len(args))],
        out_specs=[spec(i, outer[1]) for i in range(len(outs))],
        scratch_shapes=scratch,
        compiler_params=pltpu.CompilerParams(
            collective_id=number, has_side_effects=True, vmem_limit_bytes=52 * 2**20
        ),
        cost_estimate=pl.CostEstimate(flops=10**9, bytes_accessed=60 * 10**6, transcendentals=0),
    )(*args)


TILE = 256
ROOT = (2.0 / np.pi) ** 0.5


def cut(j):
    return pl.ds(pl.multiple_of(j * TILE, TILE), TILE)


def nt(a, b):
    return dot(a, b, ((1,), (1,)))


def tiled(tiles, body):
    def step(j, carry):
        body(j)
        return carry

    lax.fori_loop(0, tiles, step, 0)


def encode_kernel(
    states, rows_q, up, down, proj, table, perm,
    rowst_out, hid_out, slope_out, mixedt, unit, inverse, q_all, t_all,
    rowstq, hid_q, slope_q, mixedtq, unit_q, inv_q, projp,
    rows, hid, slope, rowst, part, relay, onward, arrived, mixed, padq, partq, pbuf, tbuf,
    ring_send, ring_recv, save, *sem
):
    y, z, c, x = place()
    greet("xzyc")
    sx, tx = Stage("x", sem[0], sem[1]), Stage("x", sem[2], sem[3])
    sz, tz = Stage("z", sem[4], sem[5]), Stage("z", sem[6], sem[7])
    sy, ty = Stage("y", sem[8], sem[9]), Stage("y", sem[10], sem[11])
    sc, tc = Stage("c", sem[12], sem[13]), Stage("c", sem[14], sem[15])
    width = up.shape[0]
    tiles = width // TILE
    nq = rows_q.shape[0]
    own, length = states.shape[0] // NX, states.shape[1]
    many = rows.shape[1]
    each, half = many // own, many // 2
    right, left = at(y, z, c, lax.rem(x + 1, NX)), at(y, z, c, lax.rem(x + NX - 1, NX))
    ring, saves = [], []

    def ring_copy(i, src, dst, who):
        return pltpu.make_async_remote_copy(
            src_ref=src, dst_ref=dst, send_sem=ring_send.at[i], recv_sem=ring_recv.at[i],
            device_id=who, device_id_type=MESH,
        )

    def send(i, src, dst, who):
        copy = ring_copy(i, src, dst, who)
        copy.start()
        ring.append(copy)

    def keep(src, dst):
        copy = pltpu.make_async_copy(src, dst, save.at[len(saves)])
        copy.start()
        saves.append(copy)

    def feed(r, h, d, out):
        def first(j):
            v = jnp.dot(r[...], up[:, cut(j)], preferred_element_type=F32)
            v2 = v * v
            t = jnp.tanh(ROOT * v * (1.0 + 0.044715 * v2))
            h[:, cut(j)] = (0.5 * v * (1.0 + t)).astype(BF16)
            d[:, cut(j)] = 0.5 * (1.0 + t) + (0.5 * ROOT) * v * (1.0 - t * t) * (
                1.0 + (3 * 0.044715) * v2
            )

        tiled(tiles, first)

        def second(j):
            out[:, cut(j)] = jnp.dot(
                h[...], down[:, cut(j)], preferred_element_type=F32
            ).astype(BF16)

        tiled(tiles, second)

    def group(k):
        g = lax.rem(x + k, NX)
        for i in range(own):
            rows[g, each * (i + 1) - 16 : each * (i + 1), :] = jnp.zeros((16, width), BF16)
            rows[g, each * i : each * i + length, :] = states[g * own + i]
        feed(rows.at[g], hid.at[g], slope.at[g], part.at[k])
        keep(hid.at[g], hid_out.at[g])
        keep(slope.at[g], slope_out.at[g])

    lower, upper = pl.ds(0, half), pl.ds(half, half)
    tx.start(lambda to: table, lambda k: tbuf.at[x])
    tbuf[x] = table[...]
    padq[...] = jnp.zeros(padq.shape, BF16)
    padq[0:nq, :] = rows_q[...]
    feed(padq, hid_q, slope_q, partq)
    short = partq.at[pl.ds(0, nq)]
    sx.start(lambda to: short, lambda k: pbuf.at[x])
    pbuf[x] = partq[0:nq, :]
    group(2)
    send(0, part.at[2, lower], relay.at[0], right)
    send(1, part.at[2, upper], relay.at[1], left)
    tx.arrive(lambda k, frm: tbuf.at[frm])
    merged = tbuf[0]
    for i in range(1, NX):
        merged = merged + tbuf[i]
    t_all[c, y, z] = merged
    tz.start(lambda to: t_all.at[c, y, z], lambda k: t_all.at[c, y, z])
    group(1)
    send(2, part.at[1, upper], arrived.at[0, upper], right)
    sx.arrive(lambda k, frm: pbuf.at[frm])
    ffn = pbuf[0].astype(F32)
    for i in range(1, NX):
        ffn = ffn + pbuf[i].astype(F32)
    blend = (rows_q[...].astype(F32) + ffn).astype(BF16)
    projected = jnp.dot(blend, proj[...], preferred_element_type=F32)
    inv = lax.rsqrt(jnp.sum(projected * projected, axis=-1, keepdims=True) + EPS)
    inv_q[...] = inv
    unit_q[...] = projected * inv
    q_all[c, y, z] = (projected * inv).astype(BF16)
    sz.start(lambda to: q_all.at[c, y, z], lambda k: q_all.at[c, y, z])
    group(3)
    send(3, part.at[3, lower], arrived.at[1, lower], left)
    for i, k, rows_of, side, who in ((0, 1, lower, 0, right), (1, 3, upper, 1, left)):
        ring_copy(i, relay.at[i], relay.at[i], who).wait_recv()
        onward[i] = (part[k, rows_of, :].astype(F32) + relay[i].astype(F32)).astype(BF16)
        send(4 + i, onward.at[i], arrived.at[side, rows_of], who)
    tz.arrive(lambda k, frm: t_all.at[c, y, frm])
    ty.start(lambda to: t_all.at[c, y], lambda k: t_all.at[c, y])
    group(0)
    sz.arrive(lambda k, frm: q_all.at[c, y, frm])
    sy.start(lambda to: q_all.at[c, y], lambda k: q_all.at[c, y])
    ty.arrive(lambda k, frm: t_all.at[c, frm])
    tc.start(lambda to: t_all.at[c], lambda k: t_all.at[c])
    for k in range(NX):
        g = lax.rem(x + k, NX)

        def turn(j):
            rowst[g, cut(j), :] = nt(perm[cut(j), :], rows[g]).astype(BF16)

        tiled(tiles, turn)
        keep(rowst.at[g], rowst_out.at[g])

    def turn_q(j):
        rowstq[cut(j), :] = nt(perm[cut(j), :], padq[...]).astype(BF16)
        projp[cut(j), :] = jnp.dot(
            perm[cut(j), :], proj[...], preferred_element_type=F32
        ).astype(BF16)

    tiled(tiles, turn_q)
    padq[0:nq, :] = blend

    def turn_mixed_q(j):
        mixedtq[cut(j), :] = nt(perm[cut(j), :], padq[...]).astype(BF16)

    tiled(tiles, turn_mixed_q)
    sy.arrive(lambda k, frm: q_all.at[c, frm])
    sc.start(lambda to: q_all.at[c], lambda k: q_all.at[c])
    tc.arrive(lambda k, frm: t_all.at[frm])
    for i, side, rows_of, who in (
        (2, 0, upper, right), (3, 1, lower, left), (4, 0, lower, right), (5, 1, upper, left)
    ):
        ref = arrived.at[side, rows_of]
        ring_copy(i, ref, ref, who).wait_recv()
    step_rows = each

    def finish_rows(i):
        at_rows = pl.ds(pl.multiple_of(i * step_rows, 16), step_rows)
        ffn = part[0, at_rows, :].astype(F32)
        ffn = ffn + arrived[0, at_rows, :].astype(F32) + arrived[1, at_rows, :].astype(F32)
        blend = (rows[x, at_rows, :].astype(F32) + ffn).astype(BF16)
        mixed[at_rows, :] = blend
        projected = jnp.dot(blend, proj[...], preferred_element_type=F32)
        inv = lax.rsqrt(jnp.sum(projected * projected, axis=-1, keepdims=True) + EPS)
        inverse[at_rows, :] = inv
        unit[at_rows, :] = projected * inv

    tiled(own, finish_rows)

    def turn_mixed(j):
        mixedt[cut(j), :] = nt(perm[cut(j), :], mixed[...]).astype(BF16)

    tiled(tiles, turn_mixed)
    sc.arrive(lambda k, frm: q_all.at[frm])
    for stage in (sx, tx, sz, tz, sy, ty, sc, tc):
        stage.finish()
    for copy in ring:
        copy.wait_send()
    for copy in saves:
        copy.wait()


def encode(states, rows_q, up, down, proj, table, perm):
    nq, width = rows_q.shape
    hidden, emb = up.shape[1], proj.shape[1]
    own = states.shape[0] // NX
    many = own * ((states.shape[1] + 15) // 16 * 16)
    few = (nq + 127) // 128 * 128
    shape, V = jax.ShapeDtypeStruct, pltpu.VMEM
    outs = [
        shape((NX, width, many), BF16),
        shape((NX, many, hidden), BF16),
        shape((NX, many, hidden), F32),
        shape((width, many), BF16),
        shape((many, emb), F32),
        shape((many, 1), F32),
        shape((NC, NY, NZ, nq, emb), BF16),
        shape((NC, NY, NZ) + table.shape, F32),
        shape((width, few), BF16),
        shape((few, hidden), BF16),
        shape((few, hidden), F32),
        shape((width, few), BF16),
        shape((nq, emb), F32),
        shape((nq, 1), F32),
        shape((width, emb), BF16),
    ]
    scratch = [
        V((NX, many, width), BF16),
        V((NX, many, hidden), BF16),
        V((NX, many, hidden), F32),
        V((NX, width, many), BF16),
        V((NX, many, width), BF16),
        V((2, many // 2, width), BF16),
        V((2, many // 2, width), BF16),
        V((2, many, width), BF16),
        V((many, width), BF16),
        V((few, width), BF16),
        V((few, width), BF16),
        V((NX, nq, width), BF16),
        V((NX,) + table.shape, F32),
    ] + sems(6) + [pltpu.SemaphoreType.DMA((3 * NX,))]
    for size in (NX, NX, NZ, NZ, NY, NY, NC, NC):
        scratch += sems(size - 1)
    args = (states, rows_q, up, down, proj, table, perm)
    return call(encode_kernel, outs, scratch, 1, *args, outer=([], [0, 1, 2]))


def total_kernel(vec, out, abuf, bbuf, *sem):
    y, z, c, x = place()
    barrier = pltpu.get_barrier_semaphore()
    groups = [
        (NY * NX, y * NX + x, lambda i: at(i // NX, z, c, i % NX)),
        (NZ * NC, z * NC + c, lambda i: at(y, i // NC, i % NC, x)),
    ]
    for size, mine, who in groups:
        for k in range(1, size):
            pl.semaphore_signal(
                barrier, inc=1, device_id=who((mine + k) % size), device_id_type=MESH
            )
    pl.semaphore_wait(barrier, NY * NX + NZ * NC - 2)
    held = vec
    for (size, mine, who), buf, send, recv in zip(
        groups, (abuf, bbuf), (sem[0], sem[2]), (sem[1], sem[3])
    ):
        copies = []
        buf[mine] = held[...]
        for k in range(1, size):
            copy = pltpu.make_async_remote_copy(
                src_ref=held,
                dst_ref=buf.at[mine],
                send_sem=send.at[k - 1],
                recv_sem=recv.at[k - 1],
                device_id=who((mine + k) % size),
                device_id_type=MESH,
            )
            copy.start()
            copies.append(copy)
        for k in range(1, size):
            ref = buf.at[(mine + size - k) % size]
            pltpu.make_async_remote_copy(
                src_ref=ref,
                dst_ref=ref,
                send_sem=send.at[k - 1],
                recv_sem=recv.at[k - 1],
                device_id=who((mine + k) % size),
                device_id_type=MESH,
            ).wait_recv()
        total = buf[0]
        for i in range(1, size):
            total = total + buf[i]
        for copy in copies:
            copy.wait_send()
        out[...] = total
        held = out


def total(vec):
    outs = [jax.ShapeDtypeStruct(vec.shape, F32)]
    scratch = [
        pltpu.VMEM((NY * NX,) + vec.shape, F32),
        pltpu.VMEM((NZ * NC,) + vec.shape, F32),
    ] + sems(NY * NX - 1) + sems(NZ * NC - 1)
    return call(total_kernel, outs, scratch, 2, vec)[0]


def add_into(dst, index, first, others):
    def body(i, carry):
        value = first(i).astype(F32)
        for other in others:
            value = value + other[i].astype(F32)
        dst[i] = value.astype(dst.dtype)
        return carry

    lax.fori_loop(0, index, body, 0)


def back_kernel(
    cot, uc, rowst_in, hid_in, slope_in, mixedt, rowstq, hid_q, dgelu_q, mixedtq, unit_q, inv_q,
    down, proj, projp,
    out_up, out_down, out_proj,
    uc_all, cbuf, abuf, ybuf, bbuf, zbuf, xbuf, mc, mct, mcq, mctq, ucq, rowst, hid, dgelu,
    acc_up, acc_down, acc_proj,
    gd, gu, gp, cd, cu, cp, ad, au, ap, yd, yu, yp, fd, fu, fp, bd, bu, bp, zd, zu, zp, xp, load, *sem
):
    y, z, c, x = place()
    sem = list(sem)

    def stage(axis):
        send, recv = sem.pop(0), sem.pop(0)
        return Stage(axis, send, recv)

    greet("xzyc")
    sc, su, sy, sz, sx = (stage(a) for a in "cxyzx")
    sc.start(lambda to: cot.at[to], lambda k: cbuf)
    su.start(lambda to: uc, lambda k: uc_all.at[x])
    uc_all[x] = uc[...]
    width = down.shape[1]
    tiles = width // TILE

    loads = {}
    for i, k in enumerate((0, 3, 1, 2)):
        g = lax.rem(x + k, NX)
        loads[k] = [
            pltpu.make_async_copy(src.at[g], dst.at[g], load.at[3 * i + n])
            for n, (src, dst) in enumerate(((hid_in, hid), (slope_in, dgelu), (rowst_in, rowst)))
        ]
        for copy in loads[k]:
            copy.start()

    def prepare(u, m, mt):
        def body(j, carry):
            m[:, cut(j)] = nt(u[...], proj[cut(j), :]).astype(BF16)
            mt[cut(j), :] = nt(projp[cut(j), :], u[...]).astype(BF16)
            return carry

        lax.fori_loop(0, tiles, body, 0)

    def passages(k, first):
        g = lax.rem(x + k, NX)
        prepare(uc_all.at[g], mc, mct)
        for copy in loads[k]:
            copy.wait()

        def body(j, carry):
            term = jnp.dot(mct[...], hid[g, :, cut(j)], preferred_element_type=F32)
            back = nt(mc[...], down[cut(j), :])
            pre = (back * dgelu[g, :, cut(j)]).astype(BF16)
            up = jnp.dot(rowst[g], pre, preferred_element_type=F32)
            if first:
                acc_down[:, cut(j)] = term
                acc_up[:, cut(j)] = up
            else:
                acc_down[:, cut(j)] += term
                acc_up[:, cut(j)] += up
            return carry

        lax.fori_loop(0, tiles, body, 0)

    passages(0, True)
    acc_proj[...] = jnp.dot(mixedt[...], uc[...], preferred_element_type=F32)

    sc.arrive(lambda k, frm: cbuf)
    for i in range(NY):
        add_into(abuf.at[i], NZ, lambda j: cot[c, i, j], [cbuf.at[i]])
    sy.start(lambda to: abuf.at[to], lambda k: ybuf.at[k - 1])
    su.arrive(lambda k, frm: uc_all.at[frm])
    passages(3, False)
    sy.arrive(lambda k, frm: ybuf.at[k - 1])
    add_into(bbuf, NZ, lambda j: abuf[y, j], [ybuf.at[i] for i in range(NY - 1)])
    sz.start(lambda to: bbuf.at[to], lambda k: zbuf.at[k - 1])
    passages(1, False)
    sz.arrive(lambda k, frm: zbuf.at[k - 1])
    value = bbuf[z].astype(F32)
    for i in range(NZ - 1):
        value = value + zbuf[i].astype(F32)
    xbuf[x] = value.astype(BF16)
    sx.start(lambda to: xbuf.at[x], lambda k: xbuf.at[x])
    passages(2, False)
    sx.arrive(lambda k, frm: xbuf.at[frm])
    g = xbuf[0].astype(F32)
    for i in range(1, NX):
        g = g + xbuf[i].astype(F32)
    along = jnp.sum(g * unit_q[...], axis=-1, keepdims=True)
    n = g.shape[0]
    ucq[...] = jnp.zeros(ucq.shape, BF16)
    ucq[0:n, :] = (inv_q[...] * (g - unit_q[...] * along)).astype(BF16)
    prepare(ucq, mcq, mctq)
    blocks = gd.shape[:3]

    def down_last(j, carry):
        term = acc_down[:, cut(j)] + jnp.dot(
            mctq[...], hid_q[:, cut(j)], preferred_element_type=F32
        )
        gd[:, :, :, cut(j)] = term.astype(BF16).reshape(blocks + (TILE,))
        return carry

    lax.fori_loop(0, tiles, down_last, 0)
    chunks = []
    for grads, near, total_a, far, f32_sum, padded, last in (
        (gd, cd, ad, yd, fd, bd, zd),
        (gp, cp, ap, yp, fp, bp, zp),
        (gu, cu, au, yu, fu, bu, zu),
    ):
        chunks.append((grads, near, total_a, far, f32_sum, padded, last) + tuple(stage(a) for a in "cyz"))

    def leave(chunk):
        chunk[7].start(lambda to: chunk[0].at[to], lambda k: chunk[1])

    leave(chunks[0])

    part = n // NX
    at_row = lax.broadcasted_iota(jnp.int32, ucq.shape, 0)
    mine = jnp.logical_and(at_row >= x * part, at_row < (x + 1) * part)
    own = jnp.where(mine, ucq[...].astype(F32), 0.0).astype(BF16)
    term = acc_proj[...] + jnp.dot(mixedtq[...], own, preferred_element_type=F32)
    gp[...] = term.astype(BF16).reshape(gp.shape)
    leave(chunks[1])

    def up_last(j, carry):
        back = nt(mcq[...], down[cut(j), :])
        pre = (back * dgelu_q[:, cut(j)]).astype(BF16)
        up = acc_up[:, cut(j)] + jnp.dot(rowstq[...], pre, preferred_element_type=F32)
        gu[:, :, :, cut(j)] = up.astype(BF16).reshape(blocks + (TILE,))
        return carry

    lax.fori_loop(0, tiles, up_last, 0)
    leave(chunks[2])

    for grads, near, total_a, far, f32_sum, padded, last, s1, s2, s3 in chunks:
        s1.arrive(lambda k, frm: near)
        add_into(total_a, NY, lambda j: grads[c, j], [near])
        s2.start(lambda to: total_a.at[to], lambda k: far.at[k - 1])
    per = width // (NY * NZ * NC)
    for grads, near, total_a, far, f32_sum, padded, last, s1, s2, s3 in chunks:
        s2.arrive(lambda k, frm: far.at[k - 1])
        value = total_a[y].astype(F32)
        for i in range(NY - 1):
            value = value + far[i].astype(F32)
        tall = value.shape[0]
        f32_sum[0:tall, :] = value
        f32_sum[tall : tall + 8, :] = jnp.zeros((8, value.shape[1]), F32)
        for i in range(NZ):
            padded[i] = f32_sum[i * per : i * per + 16, :].astype(BF16)
        s3.start(lambda to: padded.at[to], lambda k: last.at[k - 1])
    finals = []
    s4 = stage("x")
    for at_chunk in (1, 0, 2):
        grads, near, total_a, far, f32_sum, padded, last, s1, s2, s3 = chunks[at_chunk]
        s3.arrive(lambda k, frm: last.at[k - 1])
        value = padded[z].astype(F32)
        for i in range(NZ - 1):
            value = value + last[i].astype(F32)
        if at_chunk == 1:
            xp[x] = value
            s4.start(lambda to: xp.at[x], lambda k: xp.at[x])
        elif at_chunk == 0:
            out_down[...] = value
        else:
            out_up[...] = value
    s4.arrive(lambda k, frm: xp.at[frm])
    value = xp[0]
    for i in range(1, NX):
        value = value + xp[i]
    out_proj[...] = value
    for s in [sc, su, sy, sz, sx, s4] + [s for chunk in chunks for s in chunk[7:]]:
        s.finish()


def backward(*args):
    cot, uc, rowst, hid, _, _, rowstq = args[:7]
    n, emb = cot.shape[-2:]
    width, many = rowst.shape[1:]
    hidden = hid.shape[2]
    few = rowstq.shape[1]
    tall = width // (NC * NY)
    V = pltpu.VMEM
    outs = [jax.ShapeDtypeStruct((16, w), F32) for w in (hidden, hidden, emb)]
    scratch = [
        V((NX, many, emb), BF16),
        V((NY, NZ, n, emb), BF16),
        V((NY, NZ, n, emb), BF16),
        V((NY - 1, NZ, n, emb), BF16),
        V((NZ, n, emb), BF16),
        V((NZ - 1, n, emb), BF16),
        V((NX, n, emb), BF16),
        V((many, width), BF16),
        V((width, many), BF16),
        V((few, width), BF16),
        V((width, few), BF16),
        V((few, emb), BF16),
        V((NX, width, many), BF16),
        V((NX, many, hidden), BF16),
        V((NX, many, hidden), F32),
        V((width, hidden), F32),
        V((width, hidden), F32),
        V((width, emb), F32),
    ]
    wide = (hidden, hidden, emb)
    scratch += [V((NC, NY, tall, w), BF16) for w in wide]
    scratch += [V((NY, tall, w), BF16) for w in wide]
    scratch += [V((NY, tall, w), BF16) for w in wide]
    scratch += [V((NY - 1, tall, w), BF16) for w in wide]
    scratch += [V((tall + 8, w), F32) for w in wide]
    scratch += [V((NZ, 16, w), BF16) for w in wide]
    scratch += [V((NZ - 1, 16, w), BF16) for w in wide]
    scratch += [V((NX, 16, emb), F32), pltpu.SemaphoreType.DMA((3 * NX,))]
    for a in "cxyzx" + "cyz" * 3 + "x":
        scratch += sems({"x": NX, "y": NY, "z": NZ, "c": NC}[a] - 1)
    return call(back_kernel, outs, scratch, 3, *args, outer=([2, 3, 4], ()))


def unit_cotangent(g, unit, inverse):
    along = jnp.sum(g * unit, axis=-1, keepdims=True)
    return (inverse * (g - unit * along)).astype(BF16)


def local(
    passage_states,
    query_states,
    lengths,
    owner_map,
    candidates,
    teacher_scores,
    up_weight,
    down_weight,
    proj_weight,
):
    p_dev, pass_len, width = passage_states.shape
    q_dev, q_len, _ = query_states.shape
    emb = proj_weight.shape[1]
    n_dp = NY * NZ * NC
    me_dp, me_mp = lax.axis_index("dp"), lax.axis_index("mp")
    y, z, c, _ = place()
    my_block = (c * NY + y) * NZ + z
    p_own = p_dev // NX
    q_rows = q_dev * q_len
    rows = width // n_dp
    queries = n_dp * q_dev
    cands = candidates.shape[1]
    all_cands = cands * NX

    pad_len = (pass_len + 15) // 16 * 16

    positions = jnp.take(owner_map, candidates).astype(F32)
    table = jnp.zeros((8, 2 * all_cands), F32)
    table = lax.dynamic_update_slice(table, positions, (0, me_mp * cands))
    table = lax.dynamic_update_slice(table, teacher_scores, (0, all_cands + me_mp * cands))

    order = np.arange(width).reshape(NY, NZ, NC, rows).transpose(2, 0, 1, 3).reshape(-1)
    perm = jnp.asarray(np.eye(width)[order], BF16)
    (
        rowst, hid_p, slope_p, mixedt, unit_p, inv_p, q_all, t_all,
        rowstq, hid_q, slope_q, mixedtq, unit_q, inv_q, projp,
    ) = encode(
        passage_states, query_states.reshape(q_rows, width), up_weight, down_weight,
        proj_weight, table, perm,
    )
    q_all = q_all.reshape(n_dp * q_rows, emb)
    table = t_all.reshape(n_dp, 8, 2 * all_cands)[:, :q_dev].reshape(queries, -1)
    pos_all, teacher = table[:, :all_cands], table[:, all_cands:]
    teacher_exp = jnp.exp(teacher)
    teacher_sum = jnp.sum(teacher_exp, axis=1)
    teacher_dot = jnp.sum(teacher_exp * teacher, axis=1)
    base = me_dp * p_dev + me_mp * p_own
    mine = base + jnp.arange(p_own)
    hit = pos_all[None] == mine[:, None, None].astype(F32)
    count = jnp.sum(hit.astype(F32), axis=2)
    teacher_mass = jnp.sum(jnp.where(hit, teacher_exp[None], 0.0), axis=2)

    unit_p = unit_p.reshape(p_own, pad_len, emb)
    inv_p = inv_p.reshape(p_own, pad_len, 1)
    emb_p = unit_p.astype(BF16)

    own_len = lax.dynamic_slice_in_dim(lengths, base, p_own, 0)
    similar = dot(emb_p, q_all, ((2,), (1,)))
    live = jnp.arange(pad_len)[None, :] < own_len[:, None]
    terms = jnp.where(live[:, :, None], jnp.exp(similar / TAU), 0.0)
    denom = jnp.sum(terms, axis=1)
    scores = TAU * jnp.sum(jnp.log(denom).reshape(p_own, queries, q_len), axis=2)
    student = count * jnp.exp(scores)
    sums = jnp.stack([jnp.sum(student, axis=0), jnp.sum(teacher_mass * scores, axis=0)])
    sums = jnp.pad(sums.reshape(-1), (0, 1024 - 2 * queries)).reshape(8, 128)
    sums = total(sums).reshape(-1)[: 2 * queries].reshape(2, queries)
    student_sum = sums[0]
    loss = (teacher_dot - sums[1]) / teacher_sum - jnp.log(teacher_sum) + jnp.log(student_sum)
    query_loss = lax.dynamic_slice_in_dim(loss, my_block * q_dev, q_dev, 0)
    score_cot = student / student_sum - teacher_mass / teacher_sum
    scale = (score_cot[:, :, None] / denom.reshape(p_own, queries, q_len)).reshape(p_own, 1, -1)
    weights = (terms * scale).astype(BF16)
    cot_q = dot(weights, emb_p, ((0, 1), (0, 1))).astype(BF16)
    cot_p = dot(weights, q_all, ((2,), (0,)))
    uc_p = unit_cotangent(cot_p, unit_p, inv_p)

    up, down, grad_proj = backward(
        cot_q.reshape(NC, NY, NZ, q_rows, emb),
        uc_p.reshape(p_own * pad_len, emb),
        rowst, hid_p, slope_p, mixedt, rowstq, hid_q, slope_q, mixedtq, unit_q, inv_q,
        down_weight, proj_weight, projp,
    )
    return query_loss, up[:rows], down[:rows].T, grad_proj[:rows]


def solution(mesh):
    return jax.shard_map(
        local,
        mesh=mesh,
        in_specs=(
            P("dp", None, None),
            P("dp", None, None),
            P(),
            P(),
            P("dp", "mp"),
            P("dp", "mp"),
            P(None, "mp"),
            P("mp", None),
            P(),
        ),
        out_specs=(P("dp"), P("dp", "mp"), P("mp", "dp"), P("dp", None)),
        check_vma=False,
    )
```

```python
import functools

import jax
import numpy as np
import jax.numpy as jnp
from jax import lax
from jax.experimental import pallas as pl
from jax.experimental.pallas import tpu as pltpu
from jax.sharding import PartitionSpec as P

TAU = 0.05
EPS = 1e-06
F32 = jnp.float32
BF16 = jnp.bfloat16
NY, NZ, NC, NX = 4, 8, 2, 4
MESH = pl.DeviceIdType.MESH
VMEM = pl.BlockSpec(memory_space=pltpu.VMEM)


def dot(a, b, dims):
    return lax.dot_general(a, b, (dims, ((), ())), preferred_element_type=F32)


def place():
    dp, x = lax.axis_index("dp"), lax.axis_index("mp")
    return dp // (NZ * NC), (dp // NC) % NZ, dp % NC, x


def at(y, z, c, x):
    return ((y * NZ + z) * NC + c, x)


def peers(axis):
    y, z, c, x = place()
    out = []
    size = {"x": NX, "y": NY, "z": NZ, "c": NC}[axis]
    mine = {"x": x, "y": y, "z": z, "c": c}[axis]
    for k in range(1, size):
        to = (mine + k) % size
        frm = (mine + size - k) % size
        who = {"x": (y, z, c, to), "y": (to, z, c, x), "z": (y, to, c, x), "c": (y, z, to, x)}[axis]
        out.append((k, at(*who), to, frm))
    return out


def greet(axes):
    barrier = pltpu.get_barrier_semaphore()
    total = 0
    for axis in axes:
        for _, who, _, _ in peers(axis):
            pl.semaphore_signal(barrier, inc=1, device_id=who, device_id_type=MESH)
            total += 1
    pl.semaphore_wait(barrier, total)


class Stage:
    def __init__(self, axis, send_sem, recv_sem):
        self.axis, self.send_sem, self.recv_sem = axis, send_sem, recv_sem
        self.sent = []

    def start(self, src, dst):
        for k, who, to, _ in peers(self.axis):
            copy = pltpu.make_async_remote_copy(
                src_ref=src(to),
                dst_ref=dst(k),
                send_sem=self.send_sem.at[k - 1],
                recv_sem=self.recv_sem.at[k - 1],
                device_id=who,
                device_id_type=MESH,
            )
            copy.start()
            self.sent.append(copy)

    def arrive(self, dst):
        for k, who, _, frm in peers(self.axis):
            ref = dst(k, frm)
            pltpu.make_async_remote_copy(
                src_ref=ref,
                dst_ref=ref,
                send_sem=self.send_sem.at[k - 1],
                recv_sem=self.recv_sem.at[k - 1],
                device_id=who,
                device_id_type=MESH,
            ).wait_recv()

    def finish(self):
        for copy in self.sent:
            copy.wait_send()


def sems(n):
    return [pltpu.SemaphoreType.DMA((max(n, 1),)), pltpu.SemaphoreType.DMA((max(n, 1),))]


def call(kernel, outs, scratch, number, *args, outer=((), ()), scalars=()):
    def spec(i, which, small=()):
        if i in small:
            return pl.BlockSpec(memory_space=pltpu.SMEM)
        return pl.BlockSpec(memory_space=pl.ANY) if i in which else VMEM

    return pl.pallas_call(
        kernel,
        out_shape=outs,
        in_specs=[spec(i, outer[0], scalars) for i in range(len(args))],
        out_specs=[spec(i, outer[1]) for i in range(len(outs))],
        scratch_shapes=scratch,
        compiler_params=pltpu.CompilerParams(
            collective_id=number, has_side_effects=True, vmem_limit_bytes=58 * 2**20
        ),
        cost_estimate=pl.CostEstimate(flops=10**9, bytes_accessed=60 * 10**6, transcendentals=0),
    )(*args)


TILE = 256
ROOT = (2.0 / np.pi) ** 0.5


def cut(j):
    return pl.ds(pl.multiple_of(j * TILE, TILE), TILE)


def nt(a, b):
    return dot(a, b, ((1,), (1,)))


def tiled(tiles, body):
    def step(j, carry):
        body(j)
        return carry

    lax.fori_loop(0, tiles, step, 0)


def encode_kernel(
    states, rows_q, up, down, proj, perm, owner_map, candidates, teacher,
    rowst_out, hid_out, slope_out, mixedt, unit, inverse, q_all, t_all,
    rowstq, hid_q, slope_q, mixedtq, unit_q, inv_q, projp,
    rows, hid, slope, rowst, part, relay, onward, arrived, mixed, padq, partq, pbuf, tbuf, table,
    ring_send, ring_recv, save, *sem
):
    y, z, c, x = place()
    greet("xzyc")
    sx, tx = Stage("x", sem[0], sem[1]), Stage("x", sem[2], sem[3])
    sz, tz = Stage("z", sem[4], sem[5]), Stage("z", sem[6], sem[7])
    sy, ty = Stage("y", sem[8], sem[9]), Stage("y", sem[10], sem[11])
    sc, tc = Stage("c", sem[12], sem[13]), Stage("c", sem[14], sem[15])
    width = up.shape[0]
    tiles = width // TILE
    nq = rows_q.shape[0]
    own, length = states.shape[0] // NX, states.shape[1]
    many = rows.shape[1]
    each, half = many // own, many // 2
    right, left = at(y, z, c, lax.rem(x + 1, NX)), at(y, z, c, lax.rem(x + NX - 1, NX))
    ring, saves = [], []

    def ring_copy(i, src, dst, who):
        return pltpu.make_async_remote_copy(
            src_ref=src, dst_ref=dst, send_sem=ring_send.at[i], recv_sem=ring_recv.at[i],
            device_id=who, device_id_type=MESH,
        )

    def send(i, src, dst, who):
        copy = ring_copy(i, src, dst, who)
        copy.start()
        ring.append(copy)

    def keep(src, dst):
        copy = pltpu.make_async_copy(src, dst, save.at[len(saves)])
        copy.start()
        saves.append(copy)

    def feed(r, h, d, out):
        def first(j):
            v = jnp.dot(r[...], up[:, cut(j)], preferred_element_type=F32)
            v2 = v * v
            t = jnp.tanh(ROOT * v * (1.0 + 0.044715 * v2))
            h[:, cut(j)] = (0.5 * v * (1.0 + t)).astype(BF16)
            d[:, cut(j)] = 0.5 * (1.0 + t) + (0.5 * ROOT) * v * (1.0 - t * t) * (
                1.0 + (3 * 0.044715) * v2
            )

        tiled(tiles, first)

        def second(j):
            out[:, cut(j)] = jnp.dot(
                h[...], down[:, cut(j)], preferred_element_type=F32
            ).astype(BF16)

        tiled(tiles, second)

    def group(k):
        g = lax.rem(x + k, NX)
        for i in range(own):
            rows[g, each * (i + 1) - 16 : each * (i + 1), :] = jnp.zeros((16, width), BF16)
            rows[g, each * i : each * i + length, :] = states[g * own + i]
        feed(rows.at[g], hid.at[g], slope.at[g], part.at[k])
        keep(hid.at[g], hid_out.at[g])
        keep(slope.at[g], slope_out.at[g])

    lower, upper = pl.ds(0, half), pl.ds(half, half)
    row = lax.broadcasted_iota(jnp.int32, table.shape, 0)
    lane = lax.broadcasted_iota(jnp.int32, table.shape, 1)
    value = jnp.zeros(table.shape, F32)
    few_c = candidates.shape[1]
    for b in range(few_c):
        at_b = jnp.logical_and(lane % (few_c * NX) == x * few_c + b, row < candidates.shape[0])
        for a in range(candidates.shape[0]):
            here = jnp.logical_and(at_b, row == a)
            position = owner_map[candidates[a, b]].astype(F32)
            value = jnp.where(here, jnp.where(lane < few_c * NX, position, teacher[a, b]), value)
    table[...] = value
    tx.start(lambda to: table, lambda k: tbuf.at[x])
    tbuf[x] = table[...]
    padq[...] = jnp.zeros(padq.shape, BF16)
    padq[0:nq, :] = rows_q[...]
    feed(padq, hid_q, slope_q, partq)
    short = partq.at[pl.ds(0, nq)]
    sx.start(lambda to: short, lambda k: pbuf.at[x])
    pbuf[x] = partq[0:nq, :]
    group(2)
    send(0, part.at[2, lower], relay.at[0], right)
    send(1, part.at[2, upper], relay.at[1], left)
    tx.arrive(lambda k, frm: tbuf.at[frm])
    merged = tbuf[0]
    for i in range(1, NX):
        merged = merged + tbuf[i]
    t_all[c, y, z] = merged
    tz.start(lambda to: t_all.at[c, y, z], lambda k: t_all.at[c, y, z])
    group(1)
    send(2, part.at[1, upper], arrived.at[0, upper], right)
    sx.arrive(lambda k, frm: pbuf.at[frm])
    ffn = pbuf[0].astype(F32)
    for i in range(1, NX):
        ffn = ffn + pbuf[i].astype(F32)
    blend = (rows_q[...].astype(F32) + ffn).astype(BF16)
    projected = jnp.dot(blend, proj[...], preferred_element_type=F32)
    inv = lax.rsqrt(jnp.sum(projected * projected, axis=-1, keepdims=True) + EPS)
    inv_q[...] = inv
    unit_q[...] = projected * inv
    q_all[c, y, z] = (projected * inv).astype(BF16)
    sz.start(lambda to: q_all.at[c, y, z], lambda k: q_all.at[c, y, z])
    group(3)
    send(3, part.at[3, lower], arrived.at[1, lower], left)
    for i, k, rows_of, side, who in ((0, 1, lower, 0, right), (1, 3, upper, 1, left)):
        ring_copy(i, relay.at[i], relay.at[i], who).wait_recv()
        onward[i] = (part[k, rows_of, :].astype(F32) + relay[i].astype(F32)).astype(BF16)
        send(4 + i, onward.at[i], arrived.at[side, rows_of], who)
    tz.arrive(lambda k, frm: t_all.at[c, y, frm])
    ty.start(lambda to: t_all.at[c, y], lambda k: t_all.at[c, y])
    group(0)
    sz.arrive(lambda k, frm: q_all.at[c, y, frm])
    sy.start(lambda to: q_all.at[c, y], lambda k: q_all.at[c, y])
    ty.arrive(lambda k, frm: t_all.at[c, frm])
    tc.start(lambda to: t_all.at[c], lambda k: t_all.at[c])
    for k in range(NX):
        g = lax.rem(x + k, NX)

        def turn(j):
            rowst[g, cut(j), :] = nt(perm[cut(j), :], rows[g]).astype(BF16)

        tiled(tiles, turn)
        keep(rowst.at[g], rowst_out.at[g])

    def turn_q(j):
        rowstq[cut(j), :] = nt(perm[cut(j), :], padq[...]).astype(BF16)
        projp[cut(j), :] = jnp.dot(
            perm[cut(j), :], proj[...], preferred_element_type=F32
        ).astype(BF16)

    tiled(tiles, turn_q)
    padq[0:nq, :] = blend

    def turn_mixed_q(j):
        mixedtq[cut(j), :] = nt(perm[cut(j), :], padq[...]).astype(BF16)

    tiled(tiles, turn_mixed_q)
    sy.arrive(lambda k, frm: q_all.at[c, frm])
    sc.start(lambda to: q_all.at[c], lambda k: q_all.at[c])
    tc.arrive(lambda k, frm: t_all.at[frm])
    for i, side, rows_of, who in (
        (2, 0, upper, right), (3, 1, lower, left), (4, 0, lower, right), (5, 1, upper, left)
    ):
        ref = arrived.at[side, rows_of]
        ring_copy(i, ref, ref, who).wait_recv()
    step_rows = each

    def finish_rows(i):
        at_rows = pl.ds(pl.multiple_of(i * step_rows, 16), step_rows)
        ffn = part[0, at_rows, :].astype(F32)
        ffn = ffn + arrived[0, at_rows, :].astype(F32) + arrived[1, at_rows, :].astype(F32)
        blend = (rows[x, at_rows, :].astype(F32) + ffn).astype(BF16)
        mixed[at_rows, :] = blend
        projected = jnp.dot(blend, proj[...], preferred_element_type=F32)
        inv = lax.rsqrt(jnp.sum(projected * projected, axis=-1, keepdims=True) + EPS)
        inverse[at_rows, :] = inv
        unit[at_rows, :] = projected * inv

    tiled(own, finish_rows)

    def turn_mixed(j):
        mixedt[cut(j), :] = nt(perm[cut(j), :], mixed[...]).astype(BF16)

    tiled(tiles, turn_mixed)
    sc.arrive(lambda k, frm: q_all.at[frm])
    for stage in (sx, tx, sz, tz, sy, ty, sc, tc):
        stage.finish()
    for copy in ring:
        copy.wait_send()
    for copy in saves:
        copy.wait()


def encode(states, rows_q, up, down, proj, perm, owner_map, candidates, teacher):
    nq, width = rows_q.shape
    hidden, emb = up.shape[1], proj.shape[1]
    own = states.shape[0] // NX
    many = own * ((states.shape[1] + 15) // 16 * 16)
    few = (nq + 127) // 128 * 128
    shape, V = jax.ShapeDtypeStruct, pltpu.VMEM
    table = (8, 2 * NX * candidates.shape[1])
    outs = [
        shape((NX, width, many), BF16),
        shape((NX, many, hidden), BF16),
        shape((NX, many, hidden), F32),
        shape((width, many), BF16),
        shape((many, emb), F32),
        shape((many, 1), F32),
        shape((NC, NY, NZ, nq, emb), BF16),
        shape((NC, NY, NZ) + table, F32),
        shape((width, few), BF16),
        shape((few, hidden), BF16),
        shape((few, hidden), F32),
        shape((width, few), BF16),
        shape((nq, emb), F32),
        shape((nq, 1), F32),
        shape((width, emb), BF16),
    ]
    scratch = [
        V((NX, many, width), BF16),
        V((NX, many, hidden), BF16),
        V((NX, many, hidden), F32),
        V((NX, width, many), BF16),
        V((NX, many, width), BF16),
        V((2, many // 2, width), BF16),
        V((2, many // 2, width), BF16),
        V((2, many, width), BF16),
        V((many, width), BF16),
        V((few, width), BF16),
        V((few, width), BF16),
        V((NX, nq, width), BF16),
        V((NX,) + table, F32),
        V(table, F32),
    ] + sems(6) + [pltpu.SemaphoreType.DMA((3 * NX,))]
    for size in (NX, NX, NZ, NZ, NY, NY, NC, NC):
        scratch += sems(size - 1)
    args = (states, rows_q, up, down, proj, perm, owner_map, candidates, teacher)
    return call(encode_kernel, outs, scratch, 1, *args, outer=([], [0, 1, 2]), scalars=[6, 7, 8])


def circles(y, z, c, x):
    return (
        (NY * NX, y * NX + x, lambda i: at(i // NX, z, c, i % NX)),
        (NZ * NC, z * NC + c, lambda i: at(y, i // NC, i % NC, x)),
    )


def circle_sum(group, held, buf, out, send, recv):
    size, mine, who = group
    copies = []
    buf[mine] = held[...]
    for k in range(1, size):
        copy = pltpu.make_async_remote_copy(
            src_ref=held, dst_ref=buf.at[mine], send_sem=send.at[k - 1], recv_sem=recv.at[k - 1],
            device_id=who((mine + k) % size), device_id_type=MESH,
        )
        copy.start()
        copies.append(copy)
    for k in range(1, size):
        ref = buf.at[(mine + size - k) % size]
        pltpu.make_async_remote_copy(
            src_ref=ref, dst_ref=ref, send_sem=send.at[k - 1], recv_sem=recv.at[k - 1],
            device_id=who((mine + k) % size), device_id_type=MESH,
        ).wait_recv()
    total = buf[0]
    for i in range(1, size):
        total = total + buf[i]
    out[...] = total
    return copies


def spread_sum(v, span):
    lane = lax.broadcasted_iota(jnp.int32, v.shape, 1)
    width = v.shape[1]
    k = 1
    while k < span:
        other = jnp.where((lane & k) != 0, pltpu.roll(v, k, 1), pltpu.roll(v, width - k, 1))
        v = v + other
        k *= 2
    return v


def add_into(dst, index, first, others):
    def body(i, carry):
        value = first(i).astype(F32)
        for other in others:
            value = value + other[i].astype(F32)
        dst[i] = value.astype(dst.dtype)
        return carry

    lax.fori_loop(0, index, body, 0)


CHUNK = 512


def back_kernel(
    P_OWN, Q_LEN,
    q_all, unit_p, inv_p, side, lens, rowst_in, hid_in, slope_in, mixedt, rowstq, hid_q, dgelu_q,
    mixedtq, unit_q, inv_q, down, proj, projp,
    out_up, out_down, out_proj, out_loss,
    terms, emb_p, den, scale, cot_p, held, summed, totals, near_sums, far_sums, cot, uc,
    uc_all, cbuf, abuf, ybuf, bbuf, zbuf, xbuf, mc, mct, mcq, mctq, ucq, rowst, hid, dgelu,
    acc_up, acc_down, acc_proj,
    gd, gu, gp, cd, cu, cp, ad, au, ap, yd, yu, yp, fd, fu, fp, bd, bu, bp, zd, zu, zp, xp, load, *sem
):
    y, z, c, x = place()
    sem = list(sem)

    def stage(axis):
        send, recv = sem.pop(0), sem.pop(0)
        return Stage(axis, send, recv)

    barrier = pltpu.get_barrier_semaphore()
    groups = circles(y, z, c, x)
    for size, mine, who in groups:
        for k in range(1, size):
            pl.semaphore_signal(
                barrier, inc=1, device_id=who((mine + k) % size), device_id_type=MESH
            )
    width = down.shape[1]
    tiles = width // TILE

    loads = {}
    for i, k in enumerate((0, 3, 1, 2)):
        g = lax.rem(x + k, NX)
        loads[k] = [
            pltpu.make_async_copy(src.at[g], dst.at[g], load.at[3 * i + n])
            for n, (src, dst) in enumerate(((hid_in, hid), (slope_in, dgelu), (rowst_in, rowst)))
        ]
        for copy in loads[k]:
            copy.start()

    many = unit_p.shape[0]
    many_q, emb = q_all.shape
    own = P_OWN
    each = many // own
    n = unit_q.shape[0]
    half = many_q // NC
    base = ((y * NZ + z) * NC + c) * (own * NX) + x * own
    emb_p[...] = unit_p[...].astype(BF16)
    den[...] = jnp.ones(den.shape, F32)

    def score(j, carry):
        at_q = pl.ds(pl.multiple_of(j * CHUNK, CHUNK), CHUNK)
        row = lax.broadcasted_iota(jnp.int32, (each, CHUNK), 0)
        for k in range(own):
            rows_k = slice(k * each, (k + 1) * each)
            similar = nt(emb_p[rows_k, :], q_all[at_q, :])
            value = jnp.where(row < lens[base + k], jnp.exp(similar * (1.0 / TAU)), 0.0)
            terms[rows_k, at_q] = value
            den[k : k + 1, at_q] = jnp.sum(value, axis=0, keepdims=True)
        return carry

    lax.fori_loop(0, many_q // CHUNK, score, 0)
    scores = TAU * spread_sum(jnp.log(den[...]), Q_LEN)
    student = side[0] * jnp.exp(scores)
    scale[...] = student
    first = jnp.sum(student, axis=0, keepdims=True)
    second = jnp.sum(side[1] * scores, axis=0, keepdims=True)
    lane = lax.broadcasted_iota(jnp.int32, (1, 128), 1) % Q_LEN
    for r, line in enumerate((first, second)):
        for u in range(held.shape[1] // 128):
            packed = jnp.zeros((1, 128), F32)
            for j in range(min(Q_LEN, many_q // 128 - u * Q_LEN)):
                v = u * Q_LEN + j
                packed = jnp.where(lane == j, line[:, v * 128 : (v + 1) * 128], packed)
            held[r : r + 1, u * 128 : (u + 1) * 128] = packed
    held[2:8, :] = jnp.zeros((6, held.shape[1]), F32)
    pl.semaphore_wait(barrier, NY * NX + NZ * NC - 2)
    sum_sems = [sem.pop(0) for _ in range(4)]
    copies = circle_sum(groups[0], held, near_sums, summed, sum_sems[0], sum_sems[1])
    copies += circle_sum(groups[1], summed, far_sums, totals, sum_sems[2], sum_sems[3])
    lane = lax.broadcasted_iota(jnp.int32, (8, 128), 1) % Q_LEN
    got = totals[...]
    for v in range(many_q // 128):
        u, j = v // Q_LEN, v % Q_LEN
        at_v = slice(v * 128, (v + 1) * 128)
        here = jnp.where(lane == j, got[:, u * 128 : (u + 1) * 128], 0.0)
        here = spread_sum(here, Q_LEN)
        student_sum, cross = here[0:1, :], here[1:2, :]
        teacher_sum, teacher_dot = side[2, 0:1, at_v], side[2, 1:2, at_v]
        out_loss[:, at_v] = (
            (teacher_dot - cross) / teacher_sum - jnp.log(teacher_sum) + jnp.log(student_sum)
        )
        cotangent = scale[:, at_v] / student_sum - side[1, :, at_v] / teacher_sum
        scale[:, at_v] = cotangent / den[:, at_v]
    cot_p[...] = jnp.zeros(cot_p.shape, F32)

    def spread(side_of):
        def body(j, carry):
            inside = pl.ds(pl.multiple_of(j * CHUNK, CHUNK), CHUNK)
            at_q = pl.ds(pl.multiple_of(side_of * half + j * CHUNK, CHUNK), CHUNK)
            weights = jnp.concatenate(
                [
                    (terms[k * each : (k + 1) * each, at_q] * scale[k : k + 1, at_q]).astype(BF16)
                    for k in range(own)
                ],
                axis=0,
            )
            cot[side_of, inside, :] = dot(weights, emb_p[...], ((0,), (0,))).astype(BF16)
            cot_p[...] += jnp.dot(weights, q_all[at_q, :], preferred_element_type=F32)
            return carry

        lax.fori_loop(0, half // CHUNK, body, 0)

    sc, su, sy, sz, sx = (stage(a) for a in "cxyzx")
    spread(1 - c)
    sc.start(lambda to: cot.at[to], lambda k: cbuf)
    spread(c)
    g = cot_p[...]
    along = jnp.sum(g * unit_p[...], axis=-1, keepdims=True)
    uc[...] = (inv_p[...] * (g - unit_p[...] * along)).astype(BF16)
    su.start(lambda to: uc, lambda k: uc_all.at[x])
    uc_all[x] = uc[...]

    def prepare(u, m, mt):
        def body(j, carry):
            m[:, cut(j)] = nt(u[...], proj[cut(j), :]).astype(BF16)
            mt[cut(j), :] = nt(projp[cut(j), :], u[...]).astype(BF16)
            return carry

        lax.fori_loop(0, tiles, body, 0)

    def passages(k, first):
        g = lax.rem(x + k, NX)
        prepare(uc_all.at[g], mc, mct)
        for copy in loads[k]:
            copy.wait()

        def body(j, carry):
            term = jnp.dot(mct[...], hid[g, :, cut(j)], preferred_element_type=F32)
            back = nt(mc[...], down[cut(j), :])
            pre = (back * dgelu[g, :, cut(j)]).astype(BF16)
            up = jnp.dot(rowst[g], pre, preferred_element_type=F32)
            if first:
                acc_down[:, cut(j)] = term
                acc_up[:, cut(j)] = up
            else:
                acc_down[:, cut(j)] += term
                acc_up[:, cut(j)] += up
            return carry

        lax.fori_loop(0, tiles, body, 0)

    passages(0, True)
    acc_proj[...] = jnp.dot(mixedt[...], uc[...], preferred_element_type=F32)

    sc.arrive(lambda k, frm: cbuf)
    for i in range(NY):
        def block(ref, j):
            return ref[pl.ds(pl.multiple_of((i * NZ + j) * n, 16), n), :]

        def near(j, carry):
            value = block(cot.at[c], j).astype(F32) + block(cbuf, j).astype(F32)
            abuf[i, j] = value.astype(BF16)
            return carry

        lax.fori_loop(0, NZ, near, 0)
    sy.start(lambda to: abuf.at[to], lambda k: ybuf.at[k - 1])
    su.arrive(lambda k, frm: uc_all.at[frm])
    passages(3, False)
    sy.arrive(lambda k, frm: ybuf.at[k - 1])
    add_into(bbuf, NZ, lambda j: abuf[y, j], [ybuf.at[i] for i in range(NY - 1)])
    sz.start(lambda to: bbuf.at[to], lambda k: zbuf.at[k - 1])
    passages(1, False)
    sz.arrive(lambda k, frm: zbuf.at[k - 1])
    value = bbuf[z].astype(F32)
    for i in range(NZ - 1):
        value = value + zbuf[i].astype(F32)
    xbuf[x] = value.astype(BF16)
    sx.start(lambda to: xbuf.at[x], lambda k: xbuf.at[x])
    passages(2, False)
    sx.arrive(lambda k, frm: xbuf.at[frm])
    g = xbuf[0].astype(F32)
    for i in range(1, NX):
        g = g + xbuf[i].astype(F32)
    along = jnp.sum(g * unit_q[...], axis=-1, keepdims=True)
    ucq[...] = jnp.zeros(ucq.shape, BF16)
    ucq[0:n, :] = (inv_q[...] * (g - unit_q[...] * along)).astype(BF16)
    prepare(ucq, mcq, mctq)
    blocks = gd.shape[:3]

    def down_last(j, carry):
        term = acc_down[:, cut(j)] + jnp.dot(
            mctq[...], hid_q[:, cut(j)], preferred_element_type=F32
        )
        gd[:, :, :, cut(j)] = term.astype(BF16).reshape(blocks + (TILE,))
        return carry

    lax.fori_loop(0, tiles, down_last, 0)
    chunks = []
    for grads, near, total_a, far, f32_sum, padded, last in (
        (gd, cd, ad, yd, fd, bd, zd),
        (gp, cp, ap, yp, fp, bp, zp),
        (gu, cu, au, yu, fu, bu, zu),
    ):
        chunks.append((grads, near, total_a, far, f32_sum, padded, last) + tuple(stage(a) for a in "cyz"))

    def leave(chunk):
        chunk[7].start(lambda to: chunk[0].at[to], lambda k: chunk[1])

    leave(chunks[0])

    part = n // NX
    at_row = lax.broadcasted_iota(jnp.int32, ucq.shape, 0)
    mine = jnp.logical_and(at_row >= x * part, at_row < (x + 1) * part)
    own = jnp.where(mine, ucq[...].astype(F32), 0.0).astype(BF16)
    term = acc_proj[...] + jnp.dot(mixedtq[...], own, preferred_element_type=F32)
    gp[...] = term.astype(BF16).reshape(gp.shape)
    leave(chunks[1])

    def up_last(j, carry):
        back = nt(mcq[...], down[cut(j), :])
        pre = (back * dgelu_q[:, cut(j)]).astype(BF16)
        up = acc_up[:, cut(j)] + jnp.dot(rowstq[...], pre, preferred_element_type=F32)
        gu[:, :, :, cut(j)] = up.astype(BF16).reshape(blocks + (TILE,))
        return carry

    lax.fori_loop(0, tiles, up_last, 0)
    leave(chunks[2])

    for grads, near, total_a, far, f32_sum, padded, last, s1, s2, s3 in chunks:
        s1.arrive(lambda k, frm: near)
        add_into(total_a, NY, lambda j: grads[c, j], [near])
        s2.start(lambda to: total_a.at[to], lambda k: far.at[k - 1])
    per = width // (NY * NZ * NC)
    for grads, near, total_a, far, f32_sum, padded, last, s1, s2, s3 in chunks:
        s2.arrive(lambda k, frm: far.at[k - 1])
        value = total_a[y].astype(F32)
        for i in range(NY - 1):
            value = value + far[i].astype(F32)
        tall = value.shape[0]
        f32_sum[0:tall, :] = value
        f32_sum[tall : tall + 8, :] = jnp.zeros((8, value.shape[1]), F32)
        for i in range(NZ):
            padded[i] = f32_sum[i * per : i * per + 16, :].astype(BF16)
        s3.start(lambda to: padded.at[to], lambda k: last.at[k - 1])
    finals = []
    s4 = stage("x")
    for at_chunk in (1, 0, 2):
        grads, near, total_a, far, f32_sum, padded, last, s1, s2, s3 = chunks[at_chunk]
        s3.arrive(lambda k, frm: last.at[k - 1])
        value = padded[z].astype(F32)
        for i in range(NZ - 1):
            value = value + last[i].astype(F32)
        if at_chunk == 1:
            xp[x] = value
            s4.start(lambda to: xp.at[x], lambda k: xp.at[x])
        elif at_chunk == 0:
            out_down[...] = value
        else:
            out_up[...] = value
    s4.arrive(lambda k, frm: xp.at[frm])
    value = xp[0]
    for i in range(1, NX):
        value = value + xp[i]
    out_proj[...] = value
    for copy in copies:
        copy.wait_send()
    for s in [sc, su, sy, sz, sx, s4] + [s for chunk in chunks for s in chunk[7:]]:
        s.finish()


def backward(own, q_len, *args):
    q_all, rowst, hid, rowstq, unit_q = args[0], args[5], args[6], args[9], args[13]
    n, emb = unit_q.shape
    many_q = q_all.shape[0]
    width, many = rowst.shape[1:]
    hidden = hid.shape[2]
    few = rowstq.shape[1]
    tall = width // (NC * NY)
    V = pltpu.VMEM
    outs = [jax.ShapeDtypeStruct((16, w), F32) for w in (hidden, hidden, emb)]
    outs.append(jax.ShapeDtypeStruct((1, many_q), F32))
    packed = (8, -(-many_q // (128 * q_len)) * 128)
    scratch = [
        V((many, many_q), F32),
        V((many, emb), BF16),
        V((8, many_q), F32),
        V((8, many_q), F32),
        V((many, emb), F32),
        V(packed, F32),
        V(packed, F32),
        V(packed, F32),
        V((NY * NX,) + packed, F32),
        V((NZ * NC,) + packed, F32),
        V((NC, many_q // NC, emb), BF16),
        V((many, emb), BF16),
        V((NX, many, emb), BF16),
        V((many_q // NC, emb), BF16),
        V((NY, NZ, n, emb), BF16),
        V((NY - 1, NZ, n, emb), BF16),
        V((NZ, n, emb), BF16),
        V((NZ - 1, n, emb), BF16),
        V((NX, n, emb), BF16),
        V((many, width), BF16),
        V((width, many), BF16),
        V((few, width), BF16),
        V((width, few), BF16),
        V((few, emb), BF16),
        V((NX, width, many), BF16),
        V((NX, many, hidden), BF16),
        V((NX, many, hidden), F32),
        V((width, hidden), F32),
        V((width, hidden), F32),
        V((width, emb), F32),
    ]
    wide = (hidden, hidden, emb)
    scratch += [V((NC, NY, tall, w), BF16) for w in wide]
    scratch += [V((NY, tall, w), BF16) for w in wide]
    scratch += [V((NY, tall, w), BF16) for w in wide]
    scratch += [V((NY - 1, tall, w), BF16) for w in wide]
    scratch += [V((tall + 8, w), F32) for w in wide]
    scratch += [V((NZ, 16, w), BF16) for w in wide]
    scratch += [V((NZ - 1, 16, w), BF16) for w in wide]
    scratch += [V((NX, 16, emb), F32), pltpu.SemaphoreType.DMA((3 * NX,))]
    scratch += sems(NY * NX - 1) + sems(NZ * NC - 1)
    for a in "cxyzx" + "cyz" * 3 + "x":
        scratch += sems({"x": NX, "y": NY, "z": NZ, "c": NC}[a] - 1)
    kernel = functools.partial(back_kernel, own, q_len)
    return call(kernel, outs, scratch, 3, *args, outer=([5, 6, 7], ()), scalars=[4])


def local(
    passage_states,
    query_states,
    lengths,
    owner_map,
    candidates,
    teacher_scores,
    up_weight,
    down_weight,
    proj_weight,
):
    p_dev, pass_len, width = passage_states.shape
    q_dev, q_len, _ = query_states.shape
    emb = proj_weight.shape[1]
    n_dp = NY * NZ * NC
    me_dp, me_mp = lax.axis_index("dp"), lax.axis_index("mp")
    y, z, c, _ = place()
    my_block = (c * NY + y) * NZ + z
    p_own = p_dev // NX
    q_rows = q_dev * q_len
    rows = width // n_dp
    queries = n_dp * q_dev
    cands = candidates.shape[1]
    all_cands = cands * NX

    order = np.arange(width).reshape(NY, NZ, NC, rows).transpose(2, 0, 1, 3).reshape(-1)
    perm = jnp.asarray(np.eye(width)[order], BF16)
    (
        rowst, hid_p, slope_p, mixedt, unit_p, inv_p, q_all, t_all,
        rowstq, hid_q, slope_q, mixedtq, unit_q, inv_q, projp,
    ) = encode(
        passage_states, query_states.reshape(q_rows, width), up_weight, down_weight,
        proj_weight, perm, owner_map, candidates, teacher_scores,
    )
    q_all = q_all.reshape(n_dp * q_rows, emb)
    table = t_all.reshape(n_dp, 8, 2 * all_cands)[:, :q_dev].reshape(queries, -1)
    pos_all, teacher = table[:, :all_cands], table[:, all_cands:]
    teacher_exp = jnp.exp(teacher)
    teacher_sum = jnp.sum(teacher_exp, axis=1)
    teacher_dot = jnp.sum(teacher_exp * teacher, axis=1)
    base = me_dp * p_dev + me_mp * p_own
    mine = base + jnp.arange(p_own)
    hit = pos_all[None] == mine[:, None, None].astype(F32)
    count = jnp.sum(hit.astype(F32), axis=2)
    teacher_mass = jnp.sum(jnp.where(hit, teacher_exp[None], 0.0), axis=2)

    def rows8(*lines):
        lines = jnp.concatenate([line.reshape(-1, queries) for line in lines], axis=0)
        return jnp.pad(lines, ((0, 8 - lines.shape[0]), (0, 0)))

    side = jnp.stack([rows8(count), rows8(teacher_mass), rows8(teacher_sum, teacher_dot)])
    side = jnp.broadcast_to(side[..., None], side.shape + (q_len,)).reshape(3, 8, -1)
    up, down, grad_proj, loss = backward(
        p_own, q_len, q_all, unit_p, inv_p, side, lengths,
        rowst, hid_p, slope_p, mixedt, rowstq, hid_q, slope_q, mixedtq, unit_q, inv_q,
        down_weight, proj_weight, projp,
    )
    loss = lax.dynamic_slice_in_dim(loss.reshape(-1), my_block * q_rows, q_rows, 0)
    query_loss = loss.reshape(q_dev, q_len)[:, 0]
    return query_loss, up[:rows], down[:rows].T, grad_proj[:rows]


def solution(mesh):
    return jax.shard_map(
        local,
        mesh=mesh,
        in_specs=(
            P("dp", None, None),
            P("dp", None, None),
            P(),
            P(),
            P("dp", "mp"),
            P("dp", "mp"),
            P(None, "mp"),
            P("mp", None),
            P(),
        ),
        out_specs=(P("dp"), P("dp", "mp"), P("mp", "dp"), P("dp", None)),
        check_vma=False,
    )
```

```python
import functools

import jax
import numpy as np
import jax.numpy as jnp
from jax import lax
from jax.experimental import pallas as pl
from jax.experimental.pallas import tpu as pltpu
from jax.sharding import PartitionSpec as P

TAU = 0.05
EPS = 1e-06
F32 = jnp.float32
BF16 = jnp.bfloat16
NY, NZ, NC, NX = 4, 8, 2, 4
MESH = pl.DeviceIdType.MESH
VMEM = pl.BlockSpec(memory_space=pltpu.VMEM)


def dot(a, b, dims):
    return lax.dot_general(a, b, (dims, ((), ())), preferred_element_type=F32)


def place():
    dp, x = lax.axis_index("dp"), lax.axis_index("mp")
    return dp // (NZ * NC), (dp // NC) % NZ, dp % NC, x


def at(y, z, c, x):
    return ((y * NZ + z) * NC + c, x)


def peers(axis):
    y, z, c, x = place()
    out = []
    size = {"x": NX, "y": NY, "z": NZ, "c": NC}[axis]
    mine = {"x": x, "y": y, "z": z, "c": c}[axis]
    for k in range(1, size):
        to = (mine + k) % size
        frm = (mine + size - k) % size
        who = {"x": (y, z, c, to), "y": (to, z, c, x), "z": (y, to, c, x), "c": (y, z, to, x)}[axis]
        out.append((k, at(*who), to, frm))
    return out


def greet(axes):
    barrier = pltpu.get_barrier_semaphore()
    total = 0
    for axis in axes:
        for _, who, _, _ in peers(axis):
            pl.semaphore_signal(barrier, inc=1, device_id=who, device_id_type=MESH)
            total += 1
    pl.semaphore_wait(barrier, total)


class Stage:
    def __init__(self, axis, send_sem, recv_sem):
        self.axis, self.send_sem, self.recv_sem = axis, send_sem, recv_sem
        self.sent = []

    def start(self, src, dst):
        for k, who, to, _ in peers(self.axis):
            copy = pltpu.make_async_remote_copy(
                src_ref=src(to),
                dst_ref=dst(k),
                send_sem=self.send_sem.at[k - 1],
                recv_sem=self.recv_sem.at[k - 1],
                device_id=who,
                device_id_type=MESH,
            )
            copy.start()
            self.sent.append(copy)

    def arrive(self, dst):
        for k, who, _, frm in peers(self.axis):
            ref = dst(k, frm)
            pltpu.make_async_remote_copy(
                src_ref=ref,
                dst_ref=ref,
                send_sem=self.send_sem.at[k - 1],
                recv_sem=self.recv_sem.at[k - 1],
                device_id=who,
                device_id_type=MESH,
            ).wait_recv()

    def finish(self):
        for copy in self.sent:
            copy.wait_send()


def sems(n):
    return [pltpu.SemaphoreType.DMA((max(n, 1),)), pltpu.SemaphoreType.DMA((max(n, 1),))]


def call(kernel, outs, scratch, number, *args, outer=((), ()), scalars=()):
    def spec(i, which, small=()):
        if i in small:
            return pl.BlockSpec(memory_space=pltpu.SMEM)
        return pl.BlockSpec(memory_space=pl.ANY) if i in which else VMEM

    return pl.pallas_call(
        kernel,
        out_shape=outs,
        in_specs=[spec(i, outer[0], scalars) for i in range(len(args))],
        out_specs=[spec(i, outer[1]) for i in range(len(outs))],
        scratch_shapes=scratch,
        compiler_params=pltpu.CompilerParams(
            collective_id=number, has_side_effects=True, vmem_limit_bytes=58 * 2**20
        ),
        cost_estimate=pl.CostEstimate(flops=10**9, bytes_accessed=60 * 10**6, transcendentals=0),
    )(*args)


TILE = 256
ROOT = (2.0 / np.pi) ** 0.5


def cut(j):
    return pl.ds(pl.multiple_of(j * TILE, TILE), TILE)


def nt(a, b):
    return dot(a, b, ((1,), (1,)))


def tiled(tiles, body):
    def step(j, carry):
        body(j)
        return carry

    lax.fori_loop(0, tiles, step, 0)


def encode_kernel(
    q_len, states, rows_q, up, down, proj, perm, owner_map, candidates, teacher,
    rowst_out, hid_out, slope_out, mixedt, unit, inverse, q_all, side,
    rowstq, hid_q, slope_q, mixedtq, unit_q, inv_q, projp,
    rows, hid, slope, rowst, part, relay, onward, arrived, mixed, padq, partq, pbuf, tbuf, table, t_all,
    ring_send, ring_recv, save, *sem
):
    y, z, c, x = place()
    greet("xzyc")
    sx, tx = Stage("x", sem[0], sem[1]), Stage("x", sem[2], sem[3])
    sz, tz = Stage("z", sem[4], sem[5]), Stage("z", sem[6], sem[7])
    sy, ty = Stage("y", sem[8], sem[9]), Stage("y", sem[10], sem[11])
    sc, tc = Stage("c", sem[12], sem[13]), Stage("c", sem[14], sem[15])
    width = up.shape[0]
    tiles = width // TILE
    nq = rows_q.shape[0]
    own, length = states.shape[0] // NX, states.shape[1]
    many = rows.shape[1]
    each, half = many // own, many // 2
    right, left = at(y, z, c, lax.rem(x + 1, NX)), at(y, z, c, lax.rem(x + NX - 1, NX))
    ring, saves = [], []

    def ring_copy(i, src, dst, who):
        return pltpu.make_async_remote_copy(
            src_ref=src, dst_ref=dst, send_sem=ring_send.at[i], recv_sem=ring_recv.at[i],
            device_id=who, device_id_type=MESH,
        )

    def send(i, src, dst, who):
        copy = ring_copy(i, src, dst, who)
        copy.start()
        ring.append(copy)

    def keep(src, dst):
        copy = pltpu.make_async_copy(src, dst, save.at[len(saves)])
        copy.start()
        saves.append(copy)

    def feed(r, h, d, out):
        def first(j):
            v = jnp.dot(r[...], up[:, cut(j)], preferred_element_type=F32)
            v2 = v * v
            t = jnp.tanh(ROOT * v * (1.0 + 0.044715 * v2))
            h[:, cut(j)] = (0.5 * v * (1.0 + t)).astype(BF16)
            d[:, cut(j)] = 0.5 * (1.0 + t) + (0.5 * ROOT) * v * (1.0 - t * t) * (
                1.0 + (3 * 0.044715) * v2
            )

        tiled(tiles, first)

        def second(j):
            out[:, cut(j)] = jnp.dot(
                h[...], down[:, cut(j)], preferred_element_type=F32
            ).astype(BF16)

        tiled(tiles, second)

    def group(k):
        g = lax.rem(x + k, NX)
        for i in range(own):
            rows[g, each * (i + 1) - 16 : each * (i + 1), :] = jnp.zeros((16, width), BF16)
            rows[g, each * i : each * i + length, :] = states[g * own + i]
        feed(rows.at[g], hid.at[g], slope.at[g], part.at[k])
        keep(hid.at[g], hid_out.at[g])
        keep(slope.at[g], slope_out.at[g])

    lower, upper = pl.ds(0, half), pl.ds(half, half)
    row = lax.broadcasted_iota(jnp.int32, table.shape, 0)
    lane = lax.broadcasted_iota(jnp.int32, table.shape, 1)
    value = jnp.zeros(table.shape, F32)
    few_c = candidates.shape[1]
    for b in range(few_c):
        at_b = jnp.logical_and(lane % (few_c * NX) == x * few_c + b, row < candidates.shape[0])
        for a in range(candidates.shape[0]):
            here = jnp.logical_and(at_b, row == a)
            position = owner_map[candidates[a, b]].astype(F32)
            value = jnp.where(here, jnp.where(lane < few_c * NX, position, teacher[a, b]), value)
    table[...] = value
    tx.start(lambda to: table, lambda k: tbuf.at[x])
    tbuf[x] = table[...]
    padq[...] = jnp.zeros(padq.shape, BF16)
    padq[0:nq, :] = rows_q[...]
    feed(padq, hid_q, slope_q, partq)
    short = partq.at[pl.ds(0, nq)]
    sx.start(lambda to: short, lambda k: pbuf.at[x])
    pbuf[x] = partq[0:nq, :]
    group(2)
    send(0, part.at[2, lower], relay.at[0], right)
    send(1, part.at[2, upper], relay.at[1], left)
    tx.arrive(lambda k, frm: tbuf.at[frm])
    merged = tbuf[0]
    for i in range(1, NX):
        merged = merged + tbuf[i]
    t_all[c, y, z] = merged
    tz.start(lambda to: t_all.at[c, y, z], lambda k: t_all.at[c, y, z])
    group(1)
    send(2, part.at[1, upper], arrived.at[0, upper], right)
    sx.arrive(lambda k, frm: pbuf.at[frm])
    ffn = pbuf[0].astype(F32)
    for i in range(1, NX):
        ffn = ffn + pbuf[i].astype(F32)
    blend = (rows_q[...].astype(F32) + ffn).astype(BF16)
    projected = jnp.dot(blend, proj[...], preferred_element_type=F32)
    inv = lax.rsqrt(jnp.sum(projected * projected, axis=-1, keepdims=True) + EPS)
    inv_q[...] = inv
    unit_q[...] = projected * inv
    q_all[c, y, z] = (projected * inv).astype(BF16)
    sz.start(lambda to: q_all.at[c, y, z], lambda k: q_all.at[c, y, z])
    group(3)
    send(3, part.at[3, lower], arrived.at[1, lower], left)
    for i, k, rows_of, way, who in ((0, 1, lower, 0, right), (1, 3, upper, 1, left)):
        ring_copy(i, relay.at[i], relay.at[i], who).wait_recv()
        onward[i] = (part[k, rows_of, :].astype(F32) + relay[i].astype(F32)).astype(BF16)
        send(4 + i, onward.at[i], arrived.at[way, rows_of], who)
    tz.arrive(lambda k, frm: t_all.at[c, y, frm])
    ty.start(lambda to: t_all.at[c, y], lambda k: t_all.at[c, y])
    group(0)
    sz.arrive(lambda k, frm: q_all.at[c, y, frm])
    sy.start(lambda to: q_all.at[c, y], lambda k: q_all.at[c, y])
    ty.arrive(lambda k, frm: t_all.at[c, frm])
    tc.start(lambda to: t_all.at[c], lambda k: t_all.at[c])
    for k in range(NX):
        g = lax.rem(x + k, NX)

        def turn(j):
            rowst[g, cut(j), :] = nt(perm[cut(j), :], rows[g]).astype(BF16)

        tiled(tiles, turn)
        keep(rowst.at[g], rowst_out.at[g])

    def turn_q(j):
        rowstq[cut(j), :] = nt(perm[cut(j), :], padq[...]).astype(BF16)
        projp[cut(j), :] = jnp.dot(
            perm[cut(j), :], proj[...], preferred_element_type=F32
        ).astype(BF16)

    tiled(tiles, turn_q)
    padq[0:nq, :] = blend

    def turn_mixed_q(j):
        mixedtq[cut(j), :] = nt(perm[cut(j), :], padq[...]).astype(BF16)

    tiled(tiles, turn_mixed_q)
    sy.arrive(lambda k, frm: q_all.at[c, frm])
    sc.start(lambda to: q_all.at[c], lambda k: q_all.at[c])
    tc.arrive(lambda k, frm: t_all.at[frm])

    side[...] = jnp.zeros(side.shape, F32)
    base = ((y * NZ + z) * NC + c) * (own * NX) + x * own
    rows4, span = 4 * t_all.shape[3], 4 * nq
    all_c = few_c * NX
    r = lax.broadcasted_iota(jnp.int32, (rows4, span), 0)
    start = (r // 8) * nq + (r % 8) * q_len
    token = lax.broadcasted_iota(jnp.int32, (rows4, span), 1)
    spread = jnp.logical_and(token >= start, token < start + q_len)
    spread = jnp.logical_and(spread, r % 8 < candidates.shape[0]).astype(F32)
    left_half = lax.broadcasted_iota(jnp.int32, (rows4, 2 * all_c), 1) < all_c

    def tally(b):
        per_y = NZ // 4
        got = t_all[b // (NY * per_y), (b // per_y) % NY, pl.ds((b % per_y) * 4, 4)]
        got = got.reshape(rows4, 2 * all_c)
        scores = jnp.where(left_half, pltpu.roll(got, all_c, 1), 0.0)
        mass = jnp.where(left_half, jnp.exp(scores), 0.0)
        tokens = pl.ds(pl.multiple_of(b * span, 128), span)

        def put(i, k, column):
            line = jnp.sum(jnp.sum(column, axis=1, keepdims=True) * spread, axis=0, keepdims=True)
            side[i, k : k + 1, tokens] = line

        for k in range(own):
            hit = jnp.logical_and(left_half, got == (base + k).astype(F32))
            put(0, k, jnp.where(hit, 1.0, 0.0))
            put(1, k, jnp.where(hit, mass, 0.0))
        put(2, 0, mass)
        put(2, 1, mass * scores)

    tiled(NC * NY * NZ // 4, tally)
    for i, way, rows_of, who in (
        (2, 0, upper, right), (3, 1, lower, left), (4, 0, lower, right), (5, 1, upper, left)
    ):
        ref = arrived.at[way, rows_of]
        ring_copy(i, ref, ref, who).wait_recv()
    step_rows = each

    def finish_rows(i):
        at_rows = pl.ds(pl.multiple_of(i * step_rows, 16), step_rows)
        ffn = part[0, at_rows, :].astype(F32)
        ffn = ffn + arrived[0, at_rows, :].astype(F32) + arrived[1, at_rows, :].astype(F32)
        blend = (rows[x, at_rows, :].astype(F32) + ffn).astype(BF16)
        mixed[at_rows, :] = blend
        projected = jnp.dot(blend, proj[...], preferred_element_type=F32)
        inv = lax.rsqrt(jnp.sum(projected * projected, axis=-1, keepdims=True) + EPS)
        inverse[at_rows, :] = inv
        unit[at_rows, :] = projected * inv

    tiled(own, finish_rows)

    def turn_mixed(j):
        mixedt[cut(j), :] = nt(perm[cut(j), :], mixed[...]).astype(BF16)

    tiled(tiles, turn_mixed)
    sc.arrive(lambda k, frm: q_all.at[frm])
    for stage in (sx, tx, sz, tz, sy, ty, sc, tc):
        stage.finish()
    for copy in ring:
        copy.wait_send()
    for copy in saves:
        copy.wait()


def encode(states, rows_q, up, down, proj, perm, owner_map, candidates, teacher):
    nq, width = rows_q.shape
    hidden, emb = up.shape[1], proj.shape[1]
    own = states.shape[0] // NX
    many = own * ((states.shape[1] + 15) // 16 * 16)
    few = (nq + 127) // 128 * 128
    shape, V = jax.ShapeDtypeStruct, pltpu.VMEM
    table = (8, 2 * NX * candidates.shape[1])
    outs = [
        shape((NX, width, many), BF16),
        shape((NX, many, hidden), BF16),
        shape((NX, many, hidden), F32),
        shape((width, many), BF16),
        shape((many, emb), F32),
        shape((many, 1), F32),
        shape((NC, NY, NZ, nq, emb), BF16),
        shape((3, 8, NC * NY * NZ * nq), F32),
        shape((width, few), BF16),
        shape((few, hidden), BF16),
        shape((few, hidden), F32),
        shape((width, few), BF16),
        shape((nq, emb), F32),
        shape((nq, 1), F32),
        shape((width, emb), BF16),
    ]
    scratch = [
        V((NX, many, width), BF16),
        V((NX, many, hidden), BF16),
        V((NX, many, hidden), F32),
        V((NX, width, many), BF16),
        V((NX, many, width), BF16),
        V((2, many // 2, width), BF16),
        V((2, many // 2, width), BF16),
        V((2, many, width), BF16),
        V((many, width), BF16),
        V((few, width), BF16),
        V((few, width), BF16),
        V((NX, nq, width), BF16),
        V((NX,) + table, F32),
        V(table, F32),
        V((NC, NY, NZ) + table, F32),
    ] + sems(6) + [pltpu.SemaphoreType.DMA((3 * NX,))]
    for size in (NX, NX, NZ, NZ, NY, NY, NC, NC):
        scratch += sems(size - 1)
    args = (states, rows_q, up, down, proj, perm, owner_map, candidates, teacher)
    kernel = functools.partial(encode_kernel, nq // candidates.shape[0])
    return call(kernel, outs, scratch, 1, *args, outer=([], [0, 1, 2]), scalars=[6, 7, 8])


def circles(y, z, c, x):
    return (
        (NY * NX, y * NX + x, lambda i: at(i // NX, z, c, i % NX)),
        (NZ * NC, z * NC + c, lambda i: at(y, i // NC, i % NC, x)),
    )


def circle_sum(group, held, buf, out, send, recv):
    size, mine, who = group
    copies = []
    buf[mine] = held[...]
    for k in range(1, size):
        copy = pltpu.make_async_remote_copy(
            src_ref=held, dst_ref=buf.at[mine], send_sem=send.at[k - 1], recv_sem=recv.at[k - 1],
            device_id=who((mine + k) % size), device_id_type=MESH,
        )
        copy.start()
        copies.append(copy)
    for k in range(1, size):
        ref = buf.at[(mine + size - k) % size]
        pltpu.make_async_remote_copy(
            src_ref=ref, dst_ref=ref, send_sem=send.at[k - 1], recv_sem=recv.at[k - 1],
            device_id=who((mine + k) % size), device_id_type=MESH,
        ).wait_recv()
    total = buf[0]
    for i in range(1, size):
        total = total + buf[i]
    out[...] = total
    return copies


def spread_sum(v, span):
    lane = lax.broadcasted_iota(jnp.int32, v.shape, 1)
    width = v.shape[1]
    k = 1
    while k < span:
        other = jnp.where((lane & k) != 0, pltpu.roll(v, k, 1), pltpu.roll(v, width - k, 1))
        v = v + other
        k *= 2
    return v


def add_into(dst, index, first, others):
    def body(i, carry):
        value = first(i).astype(F32)
        for other in others:
            value = value + other[i].astype(F32)
        dst[i] = value.astype(dst.dtype)
        return carry

    lax.fori_loop(0, index, body, 0)


CHUNK = 512


def back_kernel(
    P_OWN, Q_LEN,
    q_all, unit_p, inv_p, side, lens, rowst_in, hid_in, slope_in, mixedt, rowstq, hid_q, dgelu_q,
    mixedtq, unit_q, inv_q, down, proj, projp,
    out_up, out_down, out_proj, out_loss,
    terms, emb_p, den, scale, cot_p, held, summed, totals, near_sums, far_sums, cot, uc,
    uc_all, cbuf, abuf, ybuf, bbuf, zbuf, xbuf, mc, mct, mcq, mctq, ucq, rowst, hid, dgelu,
    acc_up, acc_down, acc_proj,
    gd, gu, gp, cd, cu, cp, ad, au, ap, yd, yu, yp, fd, fu, fp, bd, bu, bp, zd, zu, zp, xp, load, *sem
):
    y, z, c, x = place()
    sem = list(sem)

    def stage(axis):
        send, recv = sem.pop(0), sem.pop(0)
        return Stage(axis, send, recv)

    barrier = pltpu.get_barrier_semaphore()
    groups = circles(y, z, c, x)
    for size, mine, who in groups:
        for k in range(1, size):
            pl.semaphore_signal(
                barrier, inc=1, device_id=who((mine + k) % size), device_id_type=MESH
            )
    width = down.shape[1]
    tiles = width // TILE

    loads = {}
    for i, k in enumerate((0, 3, 1, 2)):
        g = lax.rem(x + k, NX)
        loads[k] = [
            pltpu.make_async_copy(src.at[g], dst.at[g], load.at[3 * i + n])
            for n, (src, dst) in enumerate(((hid_in, hid), (slope_in, dgelu), (rowst_in, rowst)))
        ]
        for copy in loads[k]:
            copy.start()

    many = unit_p.shape[0]
    many_q, emb = q_all.shape
    own = P_OWN
    each = many // own
    n = unit_q.shape[0]
    half = many_q // NC
    base = ((y * NZ + z) * NC + c) * (own * NX) + x * own
    emb_p[...] = unit_p[...].astype(BF16)
    den[...] = jnp.ones(den.shape, F32)

    def score(j, carry):
        at_q = pl.ds(pl.multiple_of(j * CHUNK, CHUNK), CHUNK)
        row = lax.broadcasted_iota(jnp.int32, (each, CHUNK), 0)
        for k in range(own):
            rows_k = slice(k * each, (k + 1) * each)
            similar = nt(emb_p[rows_k, :], q_all[at_q, :])
            value = jnp.where(row < lens[base + k], jnp.exp(similar * (1.0 / TAU)), 0.0)
            terms[rows_k, at_q] = value
            den[k : k + 1, at_q] = jnp.sum(value, axis=0, keepdims=True)
        return carry

    lax.fori_loop(0, many_q // CHUNK, score, 0)
    scores = TAU * spread_sum(jnp.log(den[...]), Q_LEN)
    student = side[0] * jnp.exp(scores)
    scale[...] = student
    first = jnp.sum(student, axis=0, keepdims=True)
    second = jnp.sum(side[1] * scores, axis=0, keepdims=True)
    lane = lax.broadcasted_iota(jnp.int32, (1, 128), 1) % Q_LEN
    for r, line in enumerate((first, second)):
        for u in range(held.shape[1] // 128):
            packed = jnp.zeros((1, 128), F32)
            for j in range(min(Q_LEN, many_q // 128 - u * Q_LEN)):
                v = u * Q_LEN + j
                packed = jnp.where(lane == j, line[:, v * 128 : (v + 1) * 128], packed)
            held[r : r + 1, u * 128 : (u + 1) * 128] = packed
    held[2:8, :] = jnp.zeros((6, held.shape[1]), F32)
    pl.semaphore_wait(barrier, NY * NX + NZ * NC - 2)
    sum_sems = [sem.pop(0) for _ in range(4)]
    copies = circle_sum(groups[0], held, near_sums, summed, sum_sems[0], sum_sems[1])
    copies += circle_sum(groups[1], summed, far_sums, totals, sum_sems[2], sum_sems[3])
    lane = lax.broadcasted_iota(jnp.int32, (8, 128), 1) % Q_LEN
    got = totals[...]
    lane_1 = lax.broadcasted_iota(jnp.int32, (1, 128), 1)
    first_token = ((c * NY + y) * NZ + z) * n
    picks = [jnp.zeros((1, 128), F32)] * (n // Q_LEN)
    for v in range(many_q // 128):
        u, j = v // Q_LEN, v % Q_LEN
        at_v = slice(v * 128, (v + 1) * 128)
        here = jnp.where(lane == j, got[:, u * 128 : (u + 1) * 128], 0.0)
        here = spread_sum(here, Q_LEN)
        student_sum, cross = here[0:1, :], here[1:2, :]
        teacher_sum, teacher_dot = side[2, 0:1, at_v], side[2, 1:2, at_v]
        loss = (teacher_dot - cross) / teacher_sum - jnp.log(teacher_sum) + jnp.log(student_sum)
        picks = [
            jnp.where(lane_1 == first_token + (a * Q_LEN - v * 128), loss, pick)
            for a, pick in enumerate(picks)
        ]
        cotangent = scale[:, at_v] / student_sum - side[1, :, at_v] / teacher_sum
        scale[:, at_v] = cotangent / den[:, at_v]
    line = jnp.zeros((1, 128), F32)
    for a, pick in enumerate(picks):
        line = jnp.where(lane_1 == a, jnp.sum(pick, axis=1, keepdims=True), line)
    out_loss[...] = line
    cot_p[...] = jnp.zeros(cot_p.shape, F32)

    def spread(side_of):
        def body(j, carry):
            inside = pl.ds(pl.multiple_of(j * CHUNK, CHUNK), CHUNK)
            at_q = pl.ds(pl.multiple_of(side_of * half + j * CHUNK, CHUNK), CHUNK)
            weights = jnp.concatenate(
                [
                    (terms[k * each : (k + 1) * each, at_q] * scale[k : k + 1, at_q]).astype(BF16)
                    for k in range(own)
                ],
                axis=0,
            )
            cot[side_of, inside, :] = dot(weights, emb_p[...], ((0,), (0,))).astype(BF16)
            cot_p[...] += jnp.dot(weights, q_all[at_q, :], preferred_element_type=F32)
            return carry

        lax.fori_loop(0, half // CHUNK, body, 0)

    sc, su, sy, sz, sx = (stage(a) for a in "cxyzx")
    spread(1 - c)
    sc.start(lambda to: cot.at[to], lambda k: cbuf)
    spread(c)
    g = cot_p[...]
    along = jnp.sum(g * unit_p[...], axis=-1, keepdims=True)
    uc[...] = (inv_p[...] * (g - unit_p[...] * along)).astype(BF16)
    su.start(lambda to: uc, lambda k: uc_all.at[x])
    uc_all[x] = uc[...]

    def prepare(u, m, mt):
        def body(j, carry):
            m[:, cut(j)] = nt(u[...], proj[cut(j), :]).astype(BF16)
            mt[cut(j), :] = nt(projp[cut(j), :], u[...]).astype(BF16)
            return carry

        lax.fori_loop(0, tiles, body, 0)

    def passages(k, first):
        g = lax.rem(x + k, NX)
        prepare(uc_all.at[g], mc, mct)
        for copy in loads[k]:
            copy.wait()

        def body(j, carry):
            term = jnp.dot(mct[...], hid[g, :, cut(j)], preferred_element_type=F32)
            back = nt(mc[...], down[cut(j), :])
            pre = (back * dgelu[g, :, cut(j)]).astype(BF16)
            up = jnp.dot(rowst[g], pre, preferred_element_type=F32)
            if first:
                acc_down[:, cut(j)] = term
                acc_up[:, cut(j)] = up
            else:
                acc_down[:, cut(j)] += term
                acc_up[:, cut(j)] += up
            return carry

        lax.fori_loop(0, tiles, body, 0)

    passages(0, True)
    acc_proj[...] = jnp.dot(mixedt[...], uc[...], preferred_element_type=F32)

    sc.arrive(lambda k, frm: cbuf)
    for i in range(NY):
        def block(ref, j):
            return ref[pl.ds(pl.multiple_of((i * NZ + j) * n, 16), n), :]

        def near(j, carry):
            value = block(cot.at[c], j).astype(F32) + block(cbuf, j).astype(F32)
            abuf[i, j] = value.astype(BF16)
            return carry

        lax.fori_loop(0, NZ, near, 0)
    sy.start(lambda to: abuf.at[to], lambda k: ybuf.at[k - 1])
    su.arrive(lambda k, frm: uc_all.at[frm])
    passages(3, False)
    sy.arrive(lambda k, frm: ybuf.at[k - 1])
    add_into(bbuf, NZ, lambda j: abuf[y, j], [ybuf.at[i] for i in range(NY - 1)])
    sz.start(lambda to: bbuf.at[to], lambda k: zbuf.at[k - 1])
    passages(1, False)
    sz.arrive(lambda k, frm: zbuf.at[k - 1])
    value = bbuf[z].astype(F32)
    for i in range(NZ - 1):
        value = value + zbuf[i].astype(F32)
    xbuf[x] = value.astype(BF16)
    sx.start(lambda to: xbuf.at[x], lambda k: xbuf.at[x])
    passages(2, False)
    sx.arrive(lambda k, frm: xbuf.at[frm])
    g = xbuf[0].astype(F32)
    for i in range(1, NX):
        g = g + xbuf[i].astype(F32)
    along = jnp.sum(g * unit_q[...], axis=-1, keepdims=True)
    ucq[...] = jnp.zeros(ucq.shape, BF16)
    ucq[0:n, :] = (inv_q[...] * (g - unit_q[...] * along)).astype(BF16)
    prepare(ucq, mcq, mctq)
    blocks = gd.shape[:3]

    def down_last(j, carry):
        term = acc_down[:, cut(j)] + jnp.dot(
            mctq[...], hid_q[:, cut(j)], preferred_element_type=F32
        )
        gd[:, :, :, cut(j)] = term.astype(BF16).reshape(blocks + (TILE,))
        return carry

    lax.fori_loop(0, tiles, down_last, 0)
    chunks = []
    for grads, near, total_a, far, f32_sum, padded, last in (
        (gd, cd, ad, yd, fd, bd, zd),
        (gp, cp, ap, yp, fp, bp, zp),
        (gu, cu, au, yu, fu, bu, zu),
    ):
        chunks.append((grads, near, total_a, far, f32_sum, padded, last) + tuple(stage(a) for a in "cyz"))

    def leave(chunk):
        chunk[7].start(lambda to: chunk[0].at[to], lambda k: chunk[1])

    leave(chunks[0])

    part = n // NX
    at_row = lax.broadcasted_iota(jnp.int32, ucq.shape, 0)
    mine = jnp.logical_and(at_row >= x * part, at_row < (x + 1) * part)
    own = jnp.where(mine, ucq[...].astype(F32), 0.0).astype(BF16)
    term = acc_proj[...] + jnp.dot(mixedtq[...], own, preferred_element_type=F32)
    gp[...] = term.astype(BF16).reshape(gp.shape)
    leave(chunks[1])

    def up_last(j, carry):
        back = nt(mcq[...], down[cut(j), :])
        pre = (back * dgelu_q[:, cut(j)]).astype(BF16)
        up = acc_up[:, cut(j)] + jnp.dot(rowstq[...], pre, preferred_element_type=F32)
        gu[:, :, :, cut(j)] = up.astype(BF16).reshape(blocks + (TILE,))
        return carry

    lax.fori_loop(0, tiles, up_last, 0)
    leave(chunks[2])

    for grads, near, total_a, far, f32_sum, padded, last, s1, s2, s3 in chunks:
        s1.arrive(lambda k, frm: near)
        add_into(total_a, NY, lambda j: grads[c, j], [near])
        s2.start(lambda to: total_a.at[to], lambda k: far.at[k - 1])
    per = width // (NY * NZ * NC)
    for grads, near, total_a, far, f32_sum, padded, last, s1, s2, s3 in chunks:
        s2.arrive(lambda k, frm: far.at[k - 1])
        value = total_a[y].astype(F32)
        for i in range(NY - 1):
            value = value + far[i].astype(F32)
        tall = value.shape[0]
        f32_sum[0:tall, :] = value
        f32_sum[tall : tall + 8, :] = jnp.zeros((8, value.shape[1]), F32)
        for i in range(NZ):
            padded[i] = f32_sum[i * per : i * per + 16, :].astype(BF16)
        s3.start(lambda to: padded.at[to], lambda k: last.at[k - 1])
    finals = []
    s4 = stage("x")
    for at_chunk in (1, 0, 2):
        grads, near, total_a, far, f32_sum, padded, last, s1, s2, s3 = chunks[at_chunk]
        s3.arrive(lambda k, frm: last.at[k - 1])
        value = padded[z].astype(F32)
        for i in range(NZ - 1):
            value = value + last[i].astype(F32)
        if at_chunk == 1:
            xp[x] = value
            s4.start(lambda to: xp.at[x], lambda k: xp.at[x])
        elif at_chunk == 0:
            out_down[...] = value
        else:
            out_up[...] = value
    s4.arrive(lambda k, frm: xp.at[frm])
    value = xp[0]
    for i in range(1, NX):
        value = value + xp[i]
    out_proj[...] = value
    for copy in copies:
        copy.wait_send()
    for s in [sc, su, sy, sz, sx, s4] + [s for chunk in chunks for s in chunk[7:]]:
        s.finish()


def backward(own, q_len, *args):
    q_all, rowst, hid, rowstq, unit_q = args[0], args[5], args[6], args[9], args[13]
    n, emb = unit_q.shape
    many_q = q_all.shape[0]
    width, many = rowst.shape[1:]
    hidden = hid.shape[2]
    few = rowstq.shape[1]
    tall = width // (NC * NY)
    V = pltpu.VMEM
    outs = [jax.ShapeDtypeStruct((16, w), F32) for w in (hidden, hidden, emb)]
    outs.append(jax.ShapeDtypeStruct((1, 128), F32))
    packed = (8, -(-many_q // (128 * q_len)) * 128)
    scratch = [
        V((many, many_q), F32),
        V((many, emb), BF16),
        V((8, many_q), F32),
        V((8, many_q), F32),
        V((many, emb), F32),
        V(packed, F32),
        V(packed, F32),
        V(packed, F32),
        V((NY * NX,) + packed, F32),
        V((NZ * NC,) + packed, F32),
        V((NC, many_q // NC, emb), BF16),
        V((many, emb), BF16),
        V((NX, many, emb), BF16),
        V((many_q // NC, emb), BF16),
        V((NY, NZ, n, emb), BF16),
        V((NY - 1, NZ, n, emb), BF16),
        V((NZ, n, emb), BF16),
        V((NZ - 1, n, emb), BF16),
        V((NX, n, emb), BF16),
        V((many, width), BF16),
        V((width, many), BF16),
        V((few, width), BF16),
        V((width, few), BF16),
        V((few, emb), BF16),
        V((NX, width, many), BF16),
        V((NX, many, hidden), BF16),
        V((NX, many, hidden), F32),
        V((width, hidden), F32),
        V((width, hidden), F32),
        V((width, emb), F32),
    ]
    wide = (hidden, hidden, emb)
    scratch += [V((NC, NY, tall, w), BF16) for w in wide]
    scratch += [V((NY, tall, w), BF16) for w in wide]
    scratch += [V((NY, tall, w), BF16) for w in wide]
    scratch += [V((NY - 1, tall, w), BF16) for w in wide]
    scratch += [V((tall + 8, w), F32) for w in wide]
    scratch += [V((NZ, 16, w), BF16) for w in wide]
    scratch += [V((NZ - 1, 16, w), BF16) for w in wide]
    scratch += [V((NX, 16, emb), F32), pltpu.SemaphoreType.DMA((3 * NX,))]
    scratch += sems(NY * NX - 1) + sems(NZ * NC - 1)
    for a in "cxyzx" + "cyz" * 3 + "x":
        scratch += sems({"x": NX, "y": NY, "z": NZ, "c": NC}[a] - 1)
    kernel = functools.partial(back_kernel, own, q_len)
    return call(kernel, outs, scratch, 3, *args, outer=([5, 6, 7], ()), scalars=[4])


def trim_kernel(n, *refs):
    half = len(refs) // 2
    for src, dst in zip(refs[:half], refs[half:]):
        dst[...] = src[0:n, :]


def trim(n, *arrays):
    return pl.pallas_call(
        functools.partial(trim_kernel, n),
        out_shape=[jax.ShapeDtypeStruct((n, a.shape[1]), a.dtype) for a in arrays],
        in_specs=[VMEM] * len(arrays),
        out_specs=[VMEM] * len(arrays),
    )(*arrays)


def local(
    passage_states,
    query_states,
    lengths,
    owner_map,
    candidates,
    teacher_scores,
    up_weight,
    down_weight,
    proj_weight,
):
    p_dev, pass_len, width = passage_states.shape
    q_dev, q_len, _ = query_states.shape
    emb = proj_weight.shape[1]
    n_dp = NY * NZ * NC
    p_own = p_dev // NX
    q_rows = q_dev * q_len
    rows = width // n_dp

    order = np.arange(width).reshape(NY, NZ, NC, rows).transpose(2, 0, 1, 3).reshape(-1)
    perm = jnp.asarray(np.eye(width)[order], BF16)
    (
        rowst, hid_p, slope_p, mixedt, unit_p, inv_p, q_all, side,
        rowstq, hid_q, slope_q, mixedtq, unit_q, inv_q, projp,
    ) = encode(
        passage_states, query_states.reshape(q_rows, width), up_weight, down_weight,
        proj_weight, perm, owner_map, candidates, teacher_scores,
    )
    q_all = q_all.reshape(n_dp * q_rows, emb)
    up, down, grad_proj, loss = backward(
        p_own, q_len, q_all, unit_p, inv_p, side, lengths,
        rowst, hid_p, slope_p, mixedt, rowstq, hid_q, slope_q, mixedtq, unit_q, inv_q,
        down_weight, proj_weight, projp,
    )
    up, down, grad_proj = trim(rows, up, down, grad_proj)
    return loss[0, :q_dev], up, down.T, grad_proj


def solution(mesh):
    return jax.shard_map(
        local,
        mesh=mesh,
        in_specs=(
            P("dp", None, None),
            P("dp", None, None),
            P(),
            P(),
            P("dp", "mp"),
            P("dp", "mp"),
            P(None, "mp"),
            P("mp", None),
            P(),
        ),
        out_specs=(P("dp"), P("dp", "mp"), P("mp", "dp"), P("dp", None)),
        check_vma=False,
    )
```

```python
import functools

import jax
import numpy as np
import jax.numpy as jnp
from jax import lax
from jax.experimental import pallas as pl
from jax.experimental.pallas import tpu as pltpu
from jax.sharding import PartitionSpec as P

TAU = 0.05
EPS = 1e-06
F32 = jnp.float32
BF16 = jnp.bfloat16
NY, NZ, NC, NX = 4, 8, 2, 4
MESH = pl.DeviceIdType.MESH
VMEM = pl.BlockSpec(memory_space=pltpu.VMEM)


def dot(a, b, dims):
    return lax.dot_general(a, b, (dims, ((), ())), preferred_element_type=F32)


def place():
    dp, x = lax.axis_index("dp"), lax.axis_index("mp")
    return dp // (NZ * NC), (dp // NC) % NZ, dp % NC, x


def at(y, z, c, x):
    return ((y * NZ + z) * NC + c, x)


def peers(axis):
    y, z, c, x = place()
    out = []
    size = {"x": NX, "y": NY, "z": NZ, "c": NC}[axis]
    mine = {"x": x, "y": y, "z": z, "c": c}[axis]
    for k in range(1, size):
        to = (mine + k) % size
        frm = (mine + size - k) % size
        who = {"x": (y, z, c, to), "y": (to, z, c, x), "z": (y, to, c, x), "c": (y, z, to, x)}[axis]
        out.append((k, at(*who), to, frm))
    return out


def greet(axes):
    barrier = pltpu.get_barrier_semaphore()
    total = 0
    for axis in axes:
        for _, who, _, _ in peers(axis):
            pl.semaphore_signal(barrier, inc=1, device_id=who, device_id_type=MESH)
            total += 1
    pl.semaphore_wait(barrier, total)


class Stage:
    def __init__(self, axis, send_sem, recv_sem):
        self.axis, self.send_sem, self.recv_sem = axis, send_sem, recv_sem
        self.sent = []

    def start(self, src, dst):
        for k, who, to, _ in peers(self.axis):
            copy = pltpu.make_async_remote_copy(
                src_ref=src(to),
                dst_ref=dst(k),
                send_sem=self.send_sem.at[k - 1],
                recv_sem=self.recv_sem.at[k - 1],
                device_id=who,
                device_id_type=MESH,
            )
            copy.start()
            self.sent.append(copy)

    def arrive(self, dst):
        for k, who, _, frm in peers(self.axis):
            ref = dst(k, frm)
            pltpu.make_async_remote_copy(
                src_ref=ref,
                dst_ref=ref,
                send_sem=self.send_sem.at[k - 1],
                recv_sem=self.recv_sem.at[k - 1],
                device_id=who,
                device_id_type=MESH,
            ).wait_recv()

    def finish(self):
        for copy in self.sent:
            copy.wait_send()


def sems(n):
    return [pltpu.SemaphoreType.DMA((max(n, 1),)), pltpu.SemaphoreType.DMA((max(n, 1),))]


def call(kernel, outs, scratch, number, *args, outer=((), ()), scalars=()):
    def spec(i, which, small=()):
        if i in small:
            return pl.BlockSpec(memory_space=pltpu.SMEM)
        return pl.BlockSpec(memory_space=pl.ANY) if i in which else VMEM

    return pl.pallas_call(
        kernel,
        out_shape=outs,
        in_specs=[spec(i, outer[0], scalars) for i in range(len(args))],
        out_specs=[spec(i, outer[1]) for i in range(len(outs))],
        scratch_shapes=scratch,
        compiler_params=pltpu.CompilerParams(
            collective_id=number, has_side_effects=True, vmem_limit_bytes=58 * 2**20
        ),
        cost_estimate=pl.CostEstimate(flops=10**9, bytes_accessed=60 * 10**6, transcendentals=0),
    )(*args)


TILE = 256
ROOT = (2.0 / np.pi) ** 0.5


def cut(j):
    return pl.ds(pl.multiple_of(j * TILE, TILE), TILE)


def nt(a, b):
    return dot(a, b, ((1,), (1,)))


def tiled(tiles, body):
    def step(j, carry):
        body(j)
        return carry

    lax.fori_loop(0, tiles, step, 0)


def encode_kernel(
    q_len, states, rows_q, up, down, proj, perm, owner_map, candidates, teacher,
    rowst_out, hid_out, slope_out, downt, unit, inverse, q_all, side,
    rowstq, hid_q, slope_q, unit_q, inv_q, projp,
    rows, hid, slope, rowst, part, sent, arrived, padq, partq, sent_q, pbuf, tbuf, table, t_all,
    ring_send, ring_recv, save, *sem
):
    y, z, c, x = place()
    greet("xzyc")
    sx, tx = Stage("x", sem[0], sem[1]), Stage("x", sem[2], sem[3])
    sz, tz = Stage("z", sem[4], sem[5]), Stage("z", sem[6], sem[7])
    sy, ty = Stage("y", sem[8], sem[9]), Stage("y", sem[10], sem[11])
    sc, tc = Stage("c", sem[12], sem[13]), Stage("c", sem[14], sem[15])
    width = up.shape[0]
    tiles = width // TILE
    nq = rows_q.shape[0]
    own, length = states.shape[0] // NX, states.shape[1]
    many = rows.shape[1]
    each = many // own
    ring, saves = [], []

    def ring_copy(i, src, dst, who):
        return pltpu.make_async_remote_copy(
            src_ref=src, dst_ref=dst, send_sem=ring_send.at[i], recv_sem=ring_recv.at[i],
            device_id=who, device_id_type=MESH,
        )

    def send(i, src, dst, who):
        copy = ring_copy(i, src, dst, who)
        copy.start()
        ring.append(copy)

    def keep(src, dst):
        copy = pltpu.make_async_copy(src, dst, save.at[len(saves)])
        copy.start()
        saves.append(copy)

    def feed(r, h, d, out):
        def first(j):
            v = jnp.dot(r[...], up[:, cut(j)], preferred_element_type=F32)
            v2 = v * v
            t = jnp.tanh(ROOT * v * (1.0 + 0.044715 * v2))
            h[:, cut(j)] = (0.5 * v * (1.0 + t)).astype(BF16)
            d[:, cut(j)] = 0.5 * (1.0 + t) + (0.5 * ROOT) * v * (1.0 - t * t) * (
                1.0 + (3 * 0.044715) * v2
            )

        tiled(tiles, first)

        def second(j):
            out[:, cut(j)] = jnp.dot(
                h[...], down[:, cut(j)], preferred_element_type=F32
            ).astype(BF16)

        tiled(tiles, second)

    def group(k):
        g = lax.rem(x + k, NX)
        for i in range(own):
            rows[g, each * (i + 1) - 16 : each * (i + 1), :] = jnp.zeros((16, width), BF16)
            rows[g, each * i : each * i + length, :] = states[g * own + i]
        feed(rows.at[g], hid.at[g], slope.at[g], part)
        sent[k] = jnp.dot(part[...], proj[...], preferred_element_type=F32)
        if k:
            send(k - 1, sent.at[k], arrived.at[k - 1], at(y, z, c, g))
        keep(hid.at[g], hid_out.at[g])
        keep(slope.at[g], slope_out.at[g])

    row = lax.broadcasted_iota(jnp.int32, table.shape, 0)
    lane = lax.broadcasted_iota(jnp.int32, table.shape, 1)
    value = jnp.zeros(table.shape, F32)
    few_c = candidates.shape[1]
    for b in range(few_c):
        at_b = jnp.logical_and(lane % (few_c * NX) == x * few_c + b, row < candidates.shape[0])
        for a in range(candidates.shape[0]):
            here = jnp.logical_and(at_b, row == a)
            position = owner_map[candidates[a, b]].astype(F32)
            value = jnp.where(here, jnp.where(lane < few_c * NX, position, teacher[a, b]), value)
    table[...] = value
    tx.start(lambda to: table, lambda k: tbuf.at[x])
    tbuf[x] = table[...]
    padq[...] = jnp.zeros(padq.shape, BF16)
    padq[0:nq, :] = rows_q[...]
    feed(padq, hid_q, slope_q, partq)
    sent_q[...] = jnp.dot(partq[0:nq, :], proj[...], preferred_element_type=F32)
    sx.start(lambda to: sent_q, lambda k: pbuf.at[x])
    pbuf[x] = sent_q[...]
    group(2)
    tx.arrive(lambda k, frm: tbuf.at[frm])
    merged = tbuf[0]
    for i in range(1, NX):
        merged = merged + tbuf[i]
    t_all[c, y, z] = merged
    tz.start(lambda to: t_all.at[c, y, z], lambda k: t_all.at[c, y, z])
    sx.arrive(lambda k, frm: pbuf.at[frm])
    projected = jnp.dot(rows_q[...], proj[...], preferred_element_type=F32)
    for i in range(NX):
        projected = projected + pbuf[i]
    inv = lax.rsqrt(jnp.sum(projected * projected, axis=-1, keepdims=True) + EPS)
    inv_q[...] = inv
    unit_q[...] = projected * inv
    q_all[c, y, z] = (projected * inv).astype(BF16)
    sz.start(lambda to: q_all.at[c, y, z], lambda k: q_all.at[c, y, z])
    group(1)
    tz.arrive(lambda k, frm: t_all.at[c, y, frm])
    ty.start(lambda to: t_all.at[c, y], lambda k: t_all.at[c, y])
    group(3)
    sz.arrive(lambda k, frm: q_all.at[c, y, frm])
    sy.start(lambda to: q_all.at[c, y], lambda k: q_all.at[c, y])
    ty.arrive(lambda k, frm: t_all.at[c, frm])
    tc.start(lambda to: t_all.at[c], lambda k: t_all.at[c])
    group(0)
    for k in range(NX):
        g = lax.rem(x + k, NX)

        def turn(j):
            rowst[g, cut(j), :] = nt(perm[cut(j), :], rows[g]).astype(BF16)

        tiled(tiles, turn)
        keep(rowst.at[g], rowst_out.at[g])

    def turn_q(j):
        rowstq[cut(j), :] = nt(perm[cut(j), :], padq[...]).astype(BF16)
        projp[cut(j), :] = jnp.dot(
            perm[cut(j), :], proj[...], preferred_element_type=F32
        ).astype(BF16)

    tiled(tiles, turn_q)

    def turn_down(j):
        downt[cut(j), :] = nt(perm[cut(j), :], down[...]).astype(BF16)

    tiled(tiles, turn_down)
    sy.arrive(lambda k, frm: q_all.at[c, frm])
    sc.start(lambda to: q_all.at[c], lambda k: q_all.at[c])
    tc.arrive(lambda k, frm: t_all.at[frm])

    side[...] = jnp.zeros(side.shape, F32)
    base = ((y * NZ + z) * NC + c) * (own * NX) + x * own
    rows4, span = 4 * t_all.shape[3], 4 * nq
    all_c = few_c * NX
    r = lax.broadcasted_iota(jnp.int32, (rows4, span), 0)
    start = (r // 8) * nq + (r % 8) * q_len
    token = lax.broadcasted_iota(jnp.int32, (rows4, span), 1)
    spread = jnp.logical_and(token >= start, token < start + q_len)
    spread = jnp.logical_and(spread, r % 8 < candidates.shape[0]).astype(F32)
    left_half = lax.broadcasted_iota(jnp.int32, (rows4, 2 * all_c), 1) < all_c

    def tally(b):
        per_y = NZ // 4
        got = t_all[b // (NY * per_y), (b // per_y) % NY, pl.ds((b % per_y) * 4, 4)]
        got = got.reshape(rows4, 2 * all_c)
        scores = jnp.where(left_half, pltpu.roll(got, all_c, 1), 0.0)
        mass = jnp.where(left_half, jnp.exp(scores), 0.0)
        tokens = pl.ds(pl.multiple_of(b * span, 128), span)

        def put(i, k, column):
            line = jnp.sum(jnp.sum(column, axis=1, keepdims=True) * spread, axis=0, keepdims=True)
            side[i, k : k + 1, tokens] = line

        for k in range(own):
            hit = jnp.logical_and(left_half, got == (base + k).astype(F32))
            put(0, k, jnp.where(hit, 1.0, 0.0))
            put(1, k, jnp.where(hit, mass, 0.0))
        put(2, 0, mass)
        put(2, 1, mass * scores)

    tiled(NC * NY * NZ // 4, tally)
    for i in range(NX - 1):
        ring_copy(i, arrived.at[i], arrived.at[i], at(y, z, c, x)).wait_recv()

    def finish_rows(i):
        at_rows = pl.ds(pl.multiple_of(i * each, 16), each)
        projected = jnp.dot(rows[x, at_rows, :], proj[...], preferred_element_type=F32)
        projected = projected + sent[0, at_rows, :]
        for k in range(NX - 1):
            projected = projected + arrived[k, at_rows, :]
        inv = lax.rsqrt(jnp.sum(projected * projected, axis=-1, keepdims=True) + EPS)
        inverse[at_rows, :] = inv
        unit[at_rows, :] = projected * inv

    tiled(own, finish_rows)
    sc.arrive(lambda k, frm: q_all.at[frm])
    for stage in (sx, tx, sz, tz, sy, ty, sc, tc):
        stage.finish()
    for copy in ring:
        copy.wait_send()
    for copy in saves:
        copy.wait()


def encode(states, rows_q, up, down, proj, perm, owner_map, candidates, teacher):
    nq, width = rows_q.shape
    hidden, emb = up.shape[1], proj.shape[1]
    own = states.shape[0] // NX
    many = own * ((states.shape[1] + 15) // 16 * 16)
    few = (nq + 127) // 128 * 128
    shape, V = jax.ShapeDtypeStruct, pltpu.VMEM
    table = (8, 2 * NX * candidates.shape[1])
    outs = [
        shape((NX, width, many), BF16),
        shape((NX, many, hidden), BF16),
        shape((NX, many, hidden), F32),
        shape((width, hidden), BF16),
        shape((many, emb), F32),
        shape((many, 1), F32),
        shape((NC, NY, NZ, nq, emb), BF16),
        shape((3, 8, NC * NY * NZ * nq), F32),
        shape((width, few), BF16),
        shape((few, hidden), BF16),
        shape((few, hidden), F32),
        shape((nq, emb), F32),
        shape((nq, 1), F32),
        shape((width, emb), BF16),
    ]
    scratch = [
        V((NX, many, width), BF16),
        V((NX, many, hidden), BF16),
        V((NX, many, hidden), F32),
        V((NX, width, many), BF16),
        V((many, width), BF16),
        V((NX, many, emb), F32),
        V((NX - 1, many, emb), F32),
        V((few, width), BF16),
        V((few, width), BF16),
        V((nq, emb), F32),
        V((NX, nq, emb), F32),
        V((NX,) + table, F32),
        V(table, F32),
        V((NC, NY, NZ) + table, F32),
    ] + sems(NX - 1) + [pltpu.SemaphoreType.DMA((3 * NX,))]
    for size in (NX, NX, NZ, NZ, NY, NY, NC, NC):
        scratch += sems(size - 1)
    args = (states, rows_q, up, down, proj, perm, owner_map, candidates, teacher)
    kernel = functools.partial(encode_kernel, nq // candidates.shape[0])
    return call(kernel, outs, scratch, 1, *args, outer=([], [0, 1, 2]), scalars=[6, 7, 8])


def circles(y, z, c, x):
    return (
        (NY * NX, y * NX + x, lambda i: at(i // NX, z, c, i % NX)),
        (NZ * NC, z * NC + c, lambda i: at(y, i // NC, i % NC, x)),
    )


def circle_sum(group, held, buf, out, send, recv):
    size, mine, who = group
    copies = []
    buf[mine] = held[...]
    for k in range(1, size):
        copy = pltpu.make_async_remote_copy(
            src_ref=held, dst_ref=buf.at[mine], send_sem=send.at[k - 1], recv_sem=recv.at[k - 1],
            device_id=who((mine + k) % size), device_id_type=MESH,
        )
        copy.start()
        copies.append(copy)
    for k in range(1, size):
        ref = buf.at[(mine + size - k) % size]
        pltpu.make_async_remote_copy(
            src_ref=ref, dst_ref=ref, send_sem=send.at[k - 1], recv_sem=recv.at[k - 1],
            device_id=who((mine + k) % size), device_id_type=MESH,
        ).wait_recv()
    total = buf[0]
    for i in range(1, size):
        total = total + buf[i]
    out[...] = total
    return copies


def spread_sum(v, span):
    lane = lax.broadcasted_iota(jnp.int32, v.shape, 1)
    width = v.shape[1]
    k = 1
    while k < span:
        other = jnp.where((lane & k) != 0, pltpu.roll(v, k, 1), pltpu.roll(v, width - k, 1))
        v = v + other
        k *= 2
    return v


def add_into(dst, index, first, others):
    def body(i, carry):
        value = first(i).astype(F32)
        for other in others:
            value = value + other[i].astype(F32)
        dst[i] = value.astype(dst.dtype)
        return carry

    lax.fori_loop(0, index, body, 0)


CHUNK = 512


def back_kernel(
    P_OWN, Q_LEN,
    q_all, unit_p, inv_p, side, lens, rowst_in, hid_in, slope_in, downt, rowstq, hid_q, dgelu_q,
    unit_q, inv_q, down, proj, projp,
    out_up, out_down, out_proj, out_loss,
    terms, emb_p, den, scale, cot_p, held, summed, totals, near_sums, far_sums, cot, uc,
    uc_all, cbuf, abuf, ybuf, bbuf, zbuf, xbuf, mc, mct, mcq, mctq, ucq, rowst, hid, dgelu, turned,
    acc_up, acc_down, acc_proj,
    gd, gu, gp, cd, cu, cp, ad, au, ap, yd, yu, yp, fd, fu, fp, bd, bu, bp, zd, zu, zp, xp, load, *sem
):
    y, z, c, x = place()
    sem = list(sem)

    def stage(axis):
        send, recv = sem.pop(0), sem.pop(0)
        return Stage(axis, send, recv)

    barrier = pltpu.get_barrier_semaphore()
    groups = circles(y, z, c, x)
    for size, mine, who in groups:
        for k in range(1, size):
            pl.semaphore_signal(
                barrier, inc=1, device_id=who((mine + k) % size), device_id_type=MESH
            )
    width = down.shape[1]
    tiles = width // TILE

    loads = {}
    for i, k in enumerate((0, 3, 1, 2)):
        g = lax.rem(x + k, NX)
        loads[k] = [
            pltpu.make_async_copy(src.at[g], dst.at[g], load.at[3 * i + n])
            for n, (src, dst) in enumerate(((hid_in, hid), (slope_in, dgelu), (rowst_in, rowst)))
        ]
        for copy in loads[k]:
            copy.start()

    many = unit_p.shape[0]
    many_q, emb = q_all.shape
    own = P_OWN
    each = many // own
    n = unit_q.shape[0]
    half = many_q // NC
    base = ((y * NZ + z) * NC + c) * (own * NX) + x * own
    emb_p[...] = unit_p[...].astype(BF16)
    den[...] = jnp.ones(den.shape, F32)

    def score(j, carry):
        at_q = pl.ds(pl.multiple_of(j * CHUNK, CHUNK), CHUNK)
        row = lax.broadcasted_iota(jnp.int32, (each, CHUNK), 0)
        for k in range(own):
            rows_k = slice(k * each, (k + 1) * each)
            similar = nt(emb_p[rows_k, :], q_all[at_q, :])
            value = jnp.where(row < lens[base + k], jnp.exp(similar * (1.0 / TAU)), 0.0)
            terms[rows_k, at_q] = value
            den[k : k + 1, at_q] = jnp.sum(value, axis=0, keepdims=True)
        return carry

    lax.fori_loop(0, many_q // CHUNK, score, 0)
    scores = TAU * spread_sum(jnp.log(den[...]), Q_LEN)
    student = side[0] * jnp.exp(scores)
    scale[...] = student
    first = jnp.sum(student, axis=0, keepdims=True)
    second = jnp.sum(side[1] * scores, axis=0, keepdims=True)
    lane = lax.broadcasted_iota(jnp.int32, (1, 128), 1) % Q_LEN
    for r, line in enumerate((first, second)):
        for u in range(held.shape[1] // 128):
            packed = jnp.zeros((1, 128), F32)
            for j in range(min(Q_LEN, many_q // 128 - u * Q_LEN)):
                v = u * Q_LEN + j
                packed = jnp.where(lane == j, line[:, v * 128 : (v + 1) * 128], packed)
            held[r : r + 1, u * 128 : (u + 1) * 128] = packed
    held[2:8, :] = jnp.zeros((6, held.shape[1]), F32)
    pl.semaphore_wait(barrier, NY * NX + NZ * NC - 2)
    sum_sems = [sem.pop(0) for _ in range(4)]
    copies = circle_sum(groups[0], held, near_sums, summed, sum_sems[0], sum_sems[1])
    copies += circle_sum(groups[1], summed, far_sums, totals, sum_sems[2], sum_sems[3])
    lane = lax.broadcasted_iota(jnp.int32, (8, 128), 1) % Q_LEN
    got = totals[...]
    lane_1 = lax.broadcasted_iota(jnp.int32, (1, 128), 1)
    first_token = ((c * NY + y) * NZ + z) * n
    picks = [jnp.zeros((1, 128), F32)] * (n // Q_LEN)
    for v in range(many_q // 128):
        u, j = v // Q_LEN, v % Q_LEN
        at_v = slice(v * 128, (v + 1) * 128)
        here = jnp.where(lane == j, got[:, u * 128 : (u + 1) * 128], 0.0)
        here = spread_sum(here, Q_LEN)
        student_sum, cross = here[0:1, :], here[1:2, :]
        teacher_sum, teacher_dot = side[2, 0:1, at_v], side[2, 1:2, at_v]
        loss = (teacher_dot - cross) / teacher_sum - jnp.log(teacher_sum) + jnp.log(student_sum)
        picks = [
            jnp.where(lane_1 == first_token + (a * Q_LEN - v * 128), loss, pick)
            for a, pick in enumerate(picks)
        ]
        cotangent = scale[:, at_v] / student_sum - side[1, :, at_v] / teacher_sum
        scale[:, at_v] = cotangent / den[:, at_v]
    line = jnp.zeros((1, 128), F32)
    for a, pick in enumerate(picks):
        line = jnp.where(lane_1 == a, jnp.sum(pick, axis=1, keepdims=True), line)
    out_loss[...] = line
    cot_p[...] = jnp.zeros(cot_p.shape, F32)

    def spread(side_of):
        def body(j, carry):
            inside = pl.ds(pl.multiple_of(j * CHUNK, CHUNK), CHUNK)
            at_q = pl.ds(pl.multiple_of(side_of * half + j * CHUNK, CHUNK), CHUNK)
            weights = jnp.concatenate(
                [
                    (terms[k * each : (k + 1) * each, at_q] * scale[k : k + 1, at_q]).astype(BF16)
                    for k in range(own)
                ],
                axis=0,
            )
            cot[side_of, inside, :] = dot(weights, emb_p[...], ((0,), (0,))).astype(BF16)
            cot_p[...] += jnp.dot(weights, q_all[at_q, :], preferred_element_type=F32)
            return carry

        lax.fori_loop(0, half // CHUNK, body, 0)

    sc, su, sy, sz, sx = (stage(a) for a in "cxyzx")
    spread(1 - c)
    sc.start(lambda to: cot.at[to], lambda k: cbuf)
    spread(c)
    g = cot_p[...]
    along = jnp.sum(g * unit_p[...], axis=-1, keepdims=True)
    uc[...] = (inv_p[...] * (g - unit_p[...] * along)).astype(BF16)
    su.start(lambda to: uc, lambda k: uc_all.at[x])
    uc_all[x] = uc[...]

    def prepare(u, m, mt):
        def body(j, carry):
            m[:, cut(j)] = nt(u[...], proj[cut(j), :]).astype(BF16)
            mt[cut(j), :] = nt(projp[cut(j), :], u[...]).astype(BF16)
            return carry

        lax.fori_loop(0, tiles, body, 0)

    unit_matrix = lax.broadcasted_iota(jnp.int32, (emb, emb), 0)
    unit_matrix = unit_matrix == lax.broadcasted_iota(jnp.int32, (emb, emb), 1)
    unit_matrix = jnp.where(unit_matrix, 1.0, 0.0).astype(BF16)

    def passages(k, first):
        g = lax.rem(x + k, NX)
        prepare(uc_all.at[g], mc, mct)
        for copy in loads[k]:
            copy.wait()
        uct = nt(unit_matrix, uc_all[g]).astype(BF16)
        cot_hid = jnp.dot(uct, hid[g], preferred_element_type=F32)
        if first:
            turned[...] = cot_hid
        else:
            turned[...] += cot_hid

        def body(j, carry):
            term = jnp.dot(mct[...], hid[g, :, cut(j)], preferred_element_type=F32)
            back = nt(mc[...], down[cut(j), :])
            pre = (back * dgelu[g, :, cut(j)]).astype(BF16)
            up = jnp.dot(rowst[g], pre, preferred_element_type=F32)
            if first:
                acc_down[:, cut(j)] = term
                acc_up[:, cut(j)] = up
            else:
                acc_down[:, cut(j)] += term
                acc_up[:, cut(j)] += up
            return carry

        lax.fori_loop(0, tiles, body, 0)

    passages(0, True)
    acc_proj[...] = jnp.dot(rowst[x], uc[...], preferred_element_type=F32)

    sc.arrive(lambda k, frm: cbuf)
    for i in range(NY):
        def block(ref, j):
            return ref[pl.ds(pl.multiple_of((i * NZ + j) * n, 16), n), :]

        def near(j, carry):
            value = block(cot.at[c], j).astype(F32) + block(cbuf, j).astype(F32)
            abuf[i, j] = value.astype(BF16)
            return carry

        lax.fori_loop(0, NZ, near, 0)
    sy.start(lambda to: abuf.at[to], lambda k: ybuf.at[k - 1])
    su.arrive(lambda k, frm: uc_all.at[frm])
    passages(3, False)
    sy.arrive(lambda k, frm: ybuf.at[k - 1])
    add_into(bbuf, NZ, lambda j: abuf[y, j], [ybuf.at[i] for i in range(NY - 1)])
    sz.start(lambda to: bbuf.at[to], lambda k: zbuf.at[k - 1])
    passages(1, False)
    sz.arrive(lambda k, frm: zbuf.at[k - 1])
    value = bbuf[z].astype(F32)
    for i in range(NZ - 1):
        value = value + zbuf[i].astype(F32)
    xbuf[x] = value.astype(BF16)
    sx.start(lambda to: xbuf.at[x], lambda k: xbuf.at[x])
    passages(2, False)
    sx.arrive(lambda k, frm: xbuf.at[frm])
    g = xbuf[0].astype(F32)
    for i in range(1, NX):
        g = g + xbuf[i].astype(F32)
    along = jnp.sum(g * unit_q[...], axis=-1, keepdims=True)
    ucq[...] = jnp.zeros(ucq.shape, BF16)
    ucq[0:n, :] = (inv_q[...] * (g - unit_q[...] * along)).astype(BF16)
    prepare(ucq, mcq, mctq)
    blocks = gd.shape[:3]

    def down_last(j, carry):
        term = acc_down[:, cut(j)] + jnp.dot(
            mctq[...], hid_q[:, cut(j)], preferred_element_type=F32
        )
        gd[:, :, :, cut(j)] = term.astype(BF16).reshape(blocks + (TILE,))
        return carry

    lax.fori_loop(0, tiles, down_last, 0)
    chunks = []
    for grads, near, total_a, far, f32_sum, padded, last in (
        (gd, cd, ad, yd, fd, bd, zd),
        (gp, cp, ap, yp, fp, bp, zp),
        (gu, cu, au, yu, fu, bu, zu),
    ):
        chunks.append((grads, near, total_a, far, f32_sum, padded, last) + tuple(stage(a) for a in "cyz"))

    def leave(chunk):
        chunk[7].start(lambda to: chunk[0].at[to], lambda k: chunk[1])

    leave(chunks[0])

    part = n // NX
    at_row = lax.broadcasted_iota(jnp.int32, ucq.shape, 0)
    mine = jnp.logical_and(at_row >= x * part, at_row < (x + 1) * part)
    own = jnp.where(mine, ucq[...].astype(F32), 0.0).astype(BF16)
    term = acc_proj[...] + jnp.dot(rowstq[...], own, preferred_element_type=F32)
    cot_hid = turned[...] + jnp.dot(
        nt(unit_matrix, ucq[...]).astype(BF16), hid_q[...], preferred_element_type=F32
    )
    high = cot_hid.astype(BF16)
    low = (cot_hid - high.astype(F32)).astype(BF16)
    term = term + nt(downt[...], high) + nt(downt[...], low)
    gp[...] = term.astype(BF16).reshape(gp.shape)
    leave(chunks[1])

    def up_last(j, carry):
        back = nt(mcq[...], down[cut(j), :])
        pre = (back * dgelu_q[:, cut(j)]).astype(BF16)
        up = acc_up[:, cut(j)] + jnp.dot(rowstq[...], pre, preferred_element_type=F32)
        gu[:, :, :, cut(j)] = up.astype(BF16).reshape(blocks + (TILE,))
        return carry

    lax.fori_loop(0, tiles, up_last, 0)
    leave(chunks[2])

    for grads, near, total_a, far, f32_sum, padded, last, s1, s2, s3 in chunks:
        s1.arrive(lambda k, frm: near)
        add_into(total_a, NY, lambda j: grads[c, j], [near])
        s2.start(lambda to: total_a.at[to], lambda k: far.at[k - 1])
    per = width // (NY * NZ * NC)
    for grads, near, total_a, far, f32_sum, padded, last, s1, s2, s3 in chunks:
        s2.arrive(lambda k, frm: far.at[k - 1])
        value = total_a[y].astype(F32)
        for i in range(NY - 1):
            value = value + far[i].astype(F32)
        tall = value.shape[0]
        f32_sum[0:tall, :] = value
        f32_sum[tall : tall + 8, :] = jnp.zeros((8, value.shape[1]), F32)
        for i in range(NZ):
            padded[i] = f32_sum[i * per : i * per + 16, :].astype(BF16)
        s3.start(lambda to: padded.at[to], lambda k: last.at[k - 1])
    finals = []
    s4 = stage("x")
    for at_chunk in (1, 0, 2):
        grads, near, total_a, far, f32_sum, padded, last, s1, s2, s3 = chunks[at_chunk]
        s3.arrive(lambda k, frm: last.at[k - 1])
        value = padded[z].astype(F32)
        for i in range(NZ - 1):
            value = value + last[i].astype(F32)
        if at_chunk == 1:
            xp[x] = value
            s4.start(lambda to: xp.at[x], lambda k: xp.at[x])
        elif at_chunk == 0:
            out_down[...] = value
        else:
            out_up[...] = value
    s4.arrive(lambda k, frm: xp.at[frm])
    value = xp[0]
    for i in range(1, NX):
        value = value + xp[i]
    out_proj[...] = value
    for copy in copies:
        copy.wait_send()
    for s in [sc, su, sy, sz, sx, s4] + [s for chunk in chunks for s in chunk[7:]]:
        s.finish()


def backward(own, q_len, *args):
    q_all, rowst, hid, rowstq, unit_q = args[0], args[5], args[6], args[9], args[12]
    n, emb = unit_q.shape
    many_q = q_all.shape[0]
    width, many = rowst.shape[1:]
    hidden = hid.shape[2]
    few = rowstq.shape[1]
    tall = width // (NC * NY)
    V = pltpu.VMEM
    outs = [jax.ShapeDtypeStruct((16, w), F32) for w in (hidden, hidden, emb)]
    outs.append(jax.ShapeDtypeStruct((1, 128), F32))
    packed = (8, -(-many_q // (128 * q_len)) * 128)
    scratch = [
        V((many, many_q), F32),
        V((many, emb), BF16),
        V((8, many_q), F32),
        V((8, many_q), F32),
        V((many, emb), F32),
        V(packed, F32),
        V(packed, F32),
        V(packed, F32),
        V((NY * NX,) + packed, F32),
        V((NZ * NC,) + packed, F32),
        V((NC, many_q // NC, emb), BF16),
        V((many, emb), BF16),
        V((NX, many, emb), BF16),
        V((many_q // NC, emb), BF16),
        V((NY, NZ, n, emb), BF16),
        V((NY - 1, NZ, n, emb), BF16),
        V((NZ, n, emb), BF16),
        V((NZ - 1, n, emb), BF16),
        V((NX, n, emb), BF16),
        V((many, width), BF16),
        V((width, many), BF16),
        V((few, width), BF16),
        V((width, few), BF16),
        V((few, emb), BF16),
        V((NX, width, many), BF16),
        V((NX, many, hidden), BF16),
        V((NX, many, hidden), F32),
        V((emb, hidden), F32),
        V((width, hidden), F32),
        V((width, hidden), F32),
        V((width, emb), F32),
    ]
    wide = (hidden, hidden, emb)
    scratch += [V((NC, NY, tall, w), BF16) for w in wide]
    scratch += [V((NY, tall, w), BF16) for w in wide]
    scratch += [V((NY, tall, w), BF16) for w in wide]
    scratch += [V((NY - 1, tall, w), BF16) for w in wide]
    scratch += [V((tall + 8, w), F32) for w in wide]
    scratch += [V((NZ, 16, w), BF16) for w in wide]
    scratch += [V((NZ - 1, 16, w), BF16) for w in wide]
    scratch += [V((NX, 16, emb), F32), pltpu.SemaphoreType.DMA((3 * NX,))]
    scratch += sems(NY * NX - 1) + sems(NZ * NC - 1)
    for a in "cxyzx" + "cyz" * 3 + "x":
        scratch += sems({"x": NX, "y": NY, "z": NZ, "c": NC}[a] - 1)
    kernel = functools.partial(back_kernel, own, q_len)
    return call(kernel, outs, scratch, 3, *args, outer=([5, 6, 7], ()), scalars=[4])


def trim_kernel(n, *refs):
    half = len(refs) // 2
    for src, dst in zip(refs[:half], refs[half:]):
        dst[...] = src[0:n, :]


def trim(n, *arrays):
    return pl.pallas_call(
        functools.partial(trim_kernel, n),
        out_shape=[jax.ShapeDtypeStruct((n, a.shape[1]), a.dtype) for a in arrays],
        in_specs=[VMEM] * len(arrays),
        out_specs=[VMEM] * len(arrays),
    )(*arrays)


def local(
    passage_states,
    query_states,
    lengths,
    owner_map,
    candidates,
    teacher_scores,
    up_weight,
    down_weight,
    proj_weight,
):
    p_dev, pass_len, width = passage_states.shape
    q_dev, q_len, _ = query_states.shape
    emb = proj_weight.shape[1]
    n_dp = NY * NZ * NC
    p_own = p_dev // NX
    q_rows = q_dev * q_len
    rows = width // n_dp

    order = np.arange(width).reshape(NY, NZ, NC, rows).transpose(2, 0, 1, 3).reshape(-1)
    perm = jnp.asarray(np.eye(width)[order], BF16)
    (
        rowst, hid_p, slope_p, downt, unit_p, inv_p, q_all, side,
        rowstq, hid_q, slope_q, unit_q, inv_q, projp,
    ) = encode(
        passage_states, query_states.reshape(q_rows, width), up_weight, down_weight,
        proj_weight, perm, owner_map, candidates, teacher_scores,
    )
    q_all = q_all.reshape(n_dp * q_rows, emb)
    up, down, grad_proj, loss = backward(
        p_own, q_len, q_all, unit_p, inv_p, side, lengths,
        rowst, hid_p, slope_p, downt, rowstq, hid_q, slope_q, unit_q, inv_q,
        down_weight, proj_weight, projp,
    )
    up, down, grad_proj = trim(rows, up, down, grad_proj)
    return loss[0, :q_dev], up, down.T, grad_proj


def solution(mesh):
    return jax.shard_map(
        local,
        mesh=mesh,
        in_specs=(
            P("dp", None, None),
            P("dp", None, None),
            P(),
            P(),
            P("dp", "mp"),
            P("dp", "mp"),
            P(None, "mp"),
            P("mp", None),
            P(),
        ),
        out_specs=(P("dp"), P("dp", "mp"), P("mp", "dp"), P("dp", None)),
        check_vma=False,
    )
```

```python
import functools

import jax
import numpy as np
import jax.numpy as jnp
from jax import lax
from jax.experimental import pallas as pl
from jax.experimental.pallas import tpu as pltpu
from jax.sharding import PartitionSpec as P

TAU = 0.05
EPS = 1e-06
F32 = jnp.float32
BF16 = jnp.bfloat16
NY, NZ, NC, NX = 4, 8, 2, 4
MESH = pl.DeviceIdType.MESH
VMEM = pl.BlockSpec(memory_space=pltpu.VMEM)


def dot(a, b, dims):
    return lax.dot_general(a, b, (dims, ((), ())), preferred_element_type=F32)


def place():
    dp, x = lax.axis_index("dp"), lax.axis_index("mp")
    return dp // (NZ * NC), (dp // NC) % NZ, dp % NC, x


def at(y, z, c, x):
    return ((y * NZ + z) * NC + c, x)


def peers(axis):
    y, z, c, x = place()
    out = []
    size = {"x": NX, "y": NY, "z": NZ, "c": NC}[axis]
    mine = {"x": x, "y": y, "z": z, "c": c}[axis]
    for k in range(1, size):
        to = (mine + k) % size
        frm = (mine + size - k) % size
        who = {"x": (y, z, c, to), "y": (to, z, c, x), "z": (y, to, c, x), "c": (y, z, to, x)}[axis]
        out.append((k, at(*who), to, frm))
    return out


def greet(axes):
    barrier = pltpu.get_barrier_semaphore()
    total = 0
    for axis in axes:
        for _, who, _, _ in peers(axis):
            pl.semaphore_signal(barrier, inc=1, device_id=who, device_id_type=MESH)
            total += 1
    pl.semaphore_wait(barrier, total)


class Stage:
    def __init__(self, axis, send_sem, recv_sem):
        self.axis, self.send_sem, self.recv_sem = axis, send_sem, recv_sem
        self.sent = []

    def start(self, src, dst):
        for k, who, to, _ in peers(self.axis):
            copy = pltpu.make_async_remote_copy(
                src_ref=src(to),
                dst_ref=dst(k),
                send_sem=self.send_sem.at[k - 1],
                recv_sem=self.recv_sem.at[k - 1],
                device_id=who,
                device_id_type=MESH,
            )
            copy.start()
            self.sent.append(copy)

    def arrive(self, dst):
        for k, who, _, frm in peers(self.axis):
            ref = dst(k, frm)
            pltpu.make_async_remote_copy(
                src_ref=ref,
                dst_ref=ref,
                send_sem=self.send_sem.at[k - 1],
                recv_sem=self.recv_sem.at[k - 1],
                device_id=who,
                device_id_type=MESH,
            ).wait_recv()

    def finish(self):
        for copy in self.sent:
            copy.wait_send()


def sems(n):
    return [pltpu.SemaphoreType.DMA((max(n, 1),)), pltpu.SemaphoreType.DMA((max(n, 1),))]


def call(kernel, outs, scratch, number, *args, outer=((), ()), scalars=()):
    def spec(i, which, small=()):
        if i in small:
            return pl.BlockSpec(memory_space=pltpu.SMEM)
        return pl.BlockSpec(memory_space=pl.ANY) if i in which else VMEM

    return pl.pallas_call(
        kernel,
        out_shape=outs,
        in_specs=[spec(i, outer[0], scalars) for i in range(len(args))],
        out_specs=[spec(i, outer[1]) for i in range(len(outs))],
        scratch_shapes=scratch,
        compiler_params=pltpu.CompilerParams(
            collective_id=number, has_side_effects=True, vmem_limit_bytes=58 * 2**20
        ),
        cost_estimate=pl.CostEstimate(flops=10**9, bytes_accessed=60 * 10**6, transcendentals=0),
    )(*args)


TILE = 256
ROOT = (2.0 / np.pi) ** 0.5


def cut(j):
    return pl.ds(pl.multiple_of(j * TILE, TILE), TILE)


def nt(a, b):
    return dot(a, b, ((1,), (1,)))


def tiled(tiles, body):
    def step(j, carry):
        body(j)
        return carry

    lax.fori_loop(0, tiles, step, 0)


def encode_kernel(
    q_len, states, rows_q, up, down, proj, perm, owner_map, candidates, teacher,
    rowst_out, hid_out, slope_out, downt, unit, inverse, q_all, side,
    rowstq, hid_q, slope_q, unit_q, inv_q, projp,
    rows, hid, slope, rowst, part, sent, arrived, padq, partq, sent_q, pbuf, tbuf, table, t_all,
    ring_send, ring_recv, save, *sem
):
    y, z, c, x = place()
    greet("xzyc")
    sx, tx = Stage("x", sem[0], sem[1]), Stage("x", sem[2], sem[3])
    sz, tz = Stage("z", sem[4], sem[5]), Stage("z", sem[6], sem[7])
    sy, ty = Stage("y", sem[8], sem[9]), Stage("y", sem[10], sem[11])
    sc, tc = Stage("c", sem[12], sem[13]), Stage("c", sem[14], sem[15])
    width = up.shape[0]
    tiles = width // TILE
    nq = rows_q.shape[0]
    own, length = states.shape[0] // NX, states.shape[1]
    many = rows.shape[1]
    each = many // own
    ring, saves = [], []

    def ring_copy(i, src, dst, who):
        return pltpu.make_async_remote_copy(
            src_ref=src, dst_ref=dst, send_sem=ring_send.at[i], recv_sem=ring_recv.at[i],
            device_id=who, device_id_type=MESH,
        )

    def send(i, src, dst, who):
        copy = ring_copy(i, src, dst, who)
        copy.start()
        ring.append(copy)

    def keep(src, dst):
        copy = pltpu.make_async_copy(src, dst, save.at[len(saves)])
        copy.start()
        saves.append(copy)

    def feed(r, h, d, out):
        def first(j):
            v = jnp.dot(r[...], up[:, cut(j)], preferred_element_type=F32)
            v2 = v * v
            t = jnp.tanh(ROOT * v * (1.0 + 0.044715 * v2))
            h[:, cut(j)] = (0.5 * v * (1.0 + t)).astype(BF16)
            d[:, cut(j)] = 0.5 * (1.0 + t) + (0.5 * ROOT) * v * (1.0 - t * t) * (
                1.0 + (3 * 0.044715) * v2
            )

        tiled(tiles, first)

        def second(j):
            out[:, cut(j)] = jnp.dot(
                h[...], down[:, cut(j)], preferred_element_type=F32
            ).astype(BF16)

        tiled(tiles, second)

    def group(k):
        g = lax.rem(x + k, NX)
        for i in range(own):
            rows[g, each * (i + 1) - 16 : each * (i + 1), :] = jnp.zeros((16, width), BF16)
            rows[g, each * i : each * i + length, :] = states[g * own + i]
        feed(rows.at[g], hid.at[g], slope.at[g], part)
        sent[k] = jnp.dot(part[...], proj[...], preferred_element_type=F32)
        if k:
            send(k - 1, sent.at[k], arrived.at[k - 1], at(y, z, c, g))
        keep(hid.at[g], hid_out.at[g])
        keep(slope.at[g], slope_out.at[g])

    row = lax.broadcasted_iota(jnp.int32, table.shape, 0)
    lane = lax.broadcasted_iota(jnp.int32, table.shape, 1)
    value = jnp.zeros(table.shape, F32)
    few_c = candidates.shape[1]
    for b in range(few_c):
        at_b = jnp.logical_and(lane % (few_c * NX) == x * few_c + b, row < candidates.shape[0])
        for a in range(candidates.shape[0]):
            here = jnp.logical_and(at_b, row == a)
            position = owner_map[candidates[a, b]].astype(F32)
            value = jnp.where(here, jnp.where(lane < few_c * NX, position, teacher[a, b]), value)
    table[...] = value
    tx.start(lambda to: table, lambda k: tbuf.at[x])
    tbuf[x] = table[...]
    padq[...] = jnp.zeros(padq.shape, BF16)
    padq[0:nq, :] = rows_q[...]
    feed(padq, hid_q, slope_q, partq)
    sent_q[...] = jnp.dot(partq[0:nq, :], proj[...], preferred_element_type=F32)
    sx.start(lambda to: sent_q, lambda k: pbuf.at[x])
    pbuf[x] = sent_q[...]
    group(2)
    tx.arrive(lambda k, frm: tbuf.at[frm])
    merged = tbuf[0]
    for i in range(1, NX):
        merged = merged + tbuf[i]
    t_all[c, y, z] = merged
    tz.start(lambda to: t_all.at[c, y, z], lambda k: t_all.at[c, y, z])
    sx.arrive(lambda k, frm: pbuf.at[frm])
    projected = jnp.dot(rows_q[...], proj[...], preferred_element_type=F32)
    for i in range(NX):
        projected = projected + pbuf[i]
    inv = lax.rsqrt(jnp.sum(projected * projected, axis=-1, keepdims=True) + EPS)
    inv_q[...] = inv
    unit_q[...] = projected * inv
    q_all[c, y, z] = (projected * inv).astype(BF16)
    sz.start(lambda to: q_all.at[c, y, z], lambda k: q_all.at[c, y, z])
    group(1)
    tz.arrive(lambda k, frm: t_all.at[c, y, frm])
    ty.start(lambda to: t_all.at[c, y], lambda k: t_all.at[c, y])
    group(3)
    sz.arrive(lambda k, frm: q_all.at[c, y, frm])
    sy.start(lambda to: q_all.at[c, y], lambda k: q_all.at[c, y])
    ty.arrive(lambda k, frm: t_all.at[c, frm])
    tc.start(lambda to: t_all.at[c], lambda k: t_all.at[c])
    group(0)
    for k in range(NX):
        g = lax.rem(x + k, NX)

        def turn(j):
            rowst[g, cut(j), :] = nt(perm[cut(j), :], rows[g]).astype(BF16)

        tiled(tiles, turn)
        keep(rowst.at[g], rowst_out.at[g])

    def turn_q(j):
        rowstq[cut(j), :] = nt(perm[cut(j), :], padq[...]).astype(BF16)
        projp[cut(j), :] = jnp.dot(
            perm[cut(j), :], proj[...], preferred_element_type=F32
        ).astype(BF16)

    tiled(tiles, turn_q)

    def turn_down(j):
        downt[cut(j), :] = nt(perm[cut(j), :], down[...]).astype(BF16)

    tiled(tiles, turn_down)
    sy.arrive(lambda k, frm: q_all.at[c, frm])
    sc.start(lambda to: q_all.at[c], lambda k: q_all.at[c])
    tc.arrive(lambda k, frm: t_all.at[frm])

    side[...] = jnp.zeros(side.shape, F32)
    base = ((y * NZ + z) * NC + c) * (own * NX) + x * own
    rows4, span = 4 * t_all.shape[3], 4 * nq
    all_c = few_c * NX
    r = lax.broadcasted_iota(jnp.int32, (rows4, span), 0)
    start = (r // 8) * nq + (r % 8) * q_len
    token = lax.broadcasted_iota(jnp.int32, (rows4, span), 1)
    spread = jnp.logical_and(token >= start, token < start + q_len)
    spread = jnp.logical_and(spread, r % 8 < candidates.shape[0]).astype(F32)
    left_half = lax.broadcasted_iota(jnp.int32, (rows4, 2 * all_c), 1) < all_c

    def tally(b):
        per_y = NZ // 4
        got = t_all[b // (NY * per_y), (b // per_y) % NY, pl.ds((b % per_y) * 4, 4)]
        got = got.reshape(rows4, 2 * all_c)
        scores = jnp.where(left_half, pltpu.roll(got, all_c, 1), 0.0)
        mass = jnp.where(left_half, jnp.exp(scores), 0.0)
        tokens = pl.ds(pl.multiple_of(b * span, 128), span)

        def put(i, k, column):
            line = jnp.sum(jnp.sum(column, axis=1, keepdims=True) * spread, axis=0, keepdims=True)
            side[i, k : k + 1, tokens] = line

        for k in range(own):
            hit = jnp.logical_and(left_half, got == (base + k).astype(F32))
            put(0, k, jnp.where(hit, 1.0, 0.0))
            put(1, k, jnp.where(hit, mass, 0.0))
        put(2, 0, mass)
        put(2, 1, mass * scores)

    tiled(NC * NY * NZ // 4, tally)
    for i in range(NX - 1):
        ring_copy(i, arrived.at[i], arrived.at[i], at(y, z, c, x)).wait_recv()

    def finish_rows(i):
        at_rows = pl.ds(pl.multiple_of(i * each, 16), each)
        projected = jnp.dot(rows[x, at_rows, :], proj[...], preferred_element_type=F32)
        projected = projected + sent[0, at_rows, :]
        for k in range(NX - 1):
            projected = projected + arrived[k, at_rows, :]
        inv = lax.rsqrt(jnp.sum(projected * projected, axis=-1, keepdims=True) + EPS)
        inverse[at_rows, :] = inv
        unit[at_rows, :] = projected * inv

    tiled(own, finish_rows)
    sc.arrive(lambda k, frm: q_all.at[frm])
    for stage in (sx, tx, sz, tz, sy, ty, sc, tc):
        stage.finish()
    for copy in ring:
        copy.wait_send()
    for copy in saves:
        copy.wait()


def encode(states, rows_q, up, down, proj, perm, owner_map, candidates, teacher):
    nq, width = rows_q.shape
    hidden, emb = up.shape[1], proj.shape[1]
    own = states.shape[0] // NX
    many = own * ((states.shape[1] + 15) // 16 * 16)
    few = (nq + 127) // 128 * 128
    shape, V = jax.ShapeDtypeStruct, pltpu.VMEM
    table = (8, 2 * NX * candidates.shape[1])
    outs = [
        shape((NX, width, many), BF16),
        shape((NX, many, hidden), BF16),
        shape((NX, many, hidden), F32),
        shape((width, hidden), BF16),
        shape((many, emb), F32),
        shape((many, 1), F32),
        shape((NC, NY, NZ, nq, emb), BF16),
        shape((3, 8, NC * NY * NZ * nq), F32),
        shape((width, few), BF16),
        shape((few, hidden), BF16),
        shape((few, hidden), F32),
        shape((nq, emb), F32),
        shape((nq, 1), F32),
        shape((width, emb), BF16),
    ]
    scratch = [
        V((NX, many, width), BF16),
        V((NX, many, hidden), BF16),
        V((NX, many, hidden), F32),
        V((NX, width, many), BF16),
        V((many, width), BF16),
        V((NX, many, emb), F32),
        V((NX - 1, many, emb), F32),
        V((few, width), BF16),
        V((few, width), BF16),
        V((nq, emb), F32),
        V((NX, nq, emb), F32),
        V((NX,) + table, F32),
        V(table, F32),
        V((NC, NY, NZ) + table, F32),
    ] + sems(NX - 1) + [pltpu.SemaphoreType.DMA((3 * NX,))]
    for size in (NX, NX, NZ, NZ, NY, NY, NC, NC):
        scratch += sems(size - 1)
    args = (states, rows_q, up, down, proj, perm, owner_map, candidates, teacher)
    kernel = functools.partial(encode_kernel, nq // candidates.shape[0])
    return call(kernel, outs, scratch, 1, *args, outer=([], [0, 1, 2]), scalars=[6, 7, 8])


def circles(y, z, c, x):
    return (
        (NY * NX, y * NX + x, lambda i: at(i // NX, z, c, i % NX)),
        (NZ * NC, z * NC + c, lambda i: at(y, i // NC, i % NC, x)),
    )


def circle_sum(group, held, buf, out, send, recv):
    size, mine, who = group
    copies = []
    buf[mine] = held[...]
    for k in range(1, size):
        copy = pltpu.make_async_remote_copy(
            src_ref=held, dst_ref=buf.at[mine], send_sem=send.at[k - 1], recv_sem=recv.at[k - 1],
            device_id=who((mine + k) % size), device_id_type=MESH,
        )
        copy.start()
        copies.append(copy)
    for k in range(1, size):
        ref = buf.at[(mine + size - k) % size]
        pltpu.make_async_remote_copy(
            src_ref=ref, dst_ref=ref, send_sem=send.at[k - 1], recv_sem=recv.at[k - 1],
            device_id=who((mine + k) % size), device_id_type=MESH,
        ).wait_recv()
    total = buf[0]
    for i in range(1, size):
        total = total + buf[i]
    out[...] = total
    return copies


def spread_sum(v, span):
    lane = lax.broadcasted_iota(jnp.int32, v.shape, 1)
    width = v.shape[1]
    k = 1
    while k < span:
        other = jnp.where((lane & k) != 0, pltpu.roll(v, k, 1), pltpu.roll(v, width - k, 1))
        v = v + other
        k *= 2
    return v


def add_into(dst, index, first, others):
    def body(i, carry):
        value = first(i).astype(F32)
        for other in others:
            value = value + other[i].astype(F32)
        dst[i] = value.astype(dst.dtype)
        return carry

    lax.fori_loop(0, index, body, 0)


CHUNK = 512


def back_kernel(
    P_OWN, Q_LEN,
    q_all, unit_p, inv_p, side, lens, rowst_in, hid_in, slope_in, downt, rowstq, hid_q, dgelu_q,
    unit_q, inv_q, down, proj, projp,
    out_up, out_down, out_proj, out_loss,
    terms, emb_p, den, scale, cot_p, held, summed, totals, near_sums, far_sums, cot, uc,
    uc_all, cbuf, abuf, ybuf, bbuf, zbuf, xbuf, mc, mct, mcq, mctq, ucq, rowst, hid, dgelu, turned,
    acc_up, acc_down, acc_proj,
    gp, cp, ap, yp, fp, bp, zp, xp, load, *rest
):
    y, z, c, x = place()
    tiles = down.shape[1] // TILE
    parts = 2 * tiles
    bufs = [rest[i * parts : (i + 1) * parts] for i in range(7)]
    sem = list(rest[7 * parts :])

    def stage(axis):
        send, recv = sem.pop(0), sem.pop(0)
        return Stage(axis, send, recv)

    barrier = pltpu.get_barrier_semaphore()
    groups = circles(y, z, c, x)
    for size, mine, who in groups:
        for k in range(1, size):
            pl.semaphore_signal(
                barrier, inc=1, device_id=who((mine + k) % size), device_id_type=MESH
            )
    width = down.shape[1]

    loads = {}
    for i, k in enumerate((0, 3, 1, 2)):
        g = lax.rem(x + k, NX)
        loads[k] = [
            pltpu.make_async_copy(src.at[g], dst.at[g], load.at[3 * i + n])
            for n, (src, dst) in enumerate(((hid_in, hid), (slope_in, dgelu), (rowst_in, rowst)))
        ]
        for copy in loads[k]:
            copy.start()

    many = unit_p.shape[0]
    many_q, emb = q_all.shape
    own = P_OWN
    each = many // own
    n = unit_q.shape[0]
    half = many_q // NC
    base = ((y * NZ + z) * NC + c) * (own * NX) + x * own
    emb_p[...] = unit_p[...].astype(BF16)
    den[...] = jnp.ones(den.shape, F32)

    def score(j, carry):
        at_q = pl.ds(pl.multiple_of(j * CHUNK, CHUNK), CHUNK)
        row = lax.broadcasted_iota(jnp.int32, (each, CHUNK), 0)
        for k in range(own):
            rows_k = slice(k * each, (k + 1) * each)
            similar = nt(emb_p[rows_k, :], q_all[at_q, :])
            value = jnp.where(row < lens[base + k], jnp.exp(similar * (1.0 / TAU)), 0.0)
            terms[rows_k, at_q] = value
            den[k : k + 1, at_q] = jnp.sum(value, axis=0, keepdims=True)
        return carry

    lax.fori_loop(0, many_q // CHUNK, score, 0)
    scores = TAU * spread_sum(jnp.log(den[...]), Q_LEN)
    student = side[0] * jnp.exp(scores)
    scale[...] = student
    first = jnp.sum(student, axis=0, keepdims=True)
    second = jnp.sum(side[1] * scores, axis=0, keepdims=True)
    lane = lax.broadcasted_iota(jnp.int32, (1, 128), 1) % Q_LEN
    for r, line in enumerate((first, second)):
        for u in range(held.shape[1] // 128):
            packed = jnp.zeros((1, 128), F32)
            for j in range(min(Q_LEN, many_q // 128 - u * Q_LEN)):
                v = u * Q_LEN + j
                packed = jnp.where(lane == j, line[:, v * 128 : (v + 1) * 128], packed)
            held[r : r + 1, u * 128 : (u + 1) * 128] = packed
    held[2:8, :] = jnp.zeros((6, held.shape[1]), F32)
    pl.semaphore_wait(barrier, NY * NX + NZ * NC - 2)
    sum_sems = [sem.pop(0) for _ in range(4)]
    copies = circle_sum(groups[0], held, near_sums, summed, sum_sems[0], sum_sems[1])
    copies += circle_sum(groups[1], summed, far_sums, totals, sum_sems[2], sum_sems[3])
    lane = lax.broadcasted_iota(jnp.int32, (8, 128), 1) % Q_LEN
    got = totals[...]
    lane_1 = lax.broadcasted_iota(jnp.int32, (1, 128), 1)
    first_token = ((c * NY + y) * NZ + z) * n
    picks = [jnp.zeros((1, 128), F32)] * (n // Q_LEN)
    for v in range(many_q // 128):
        u, j = v // Q_LEN, v % Q_LEN
        at_v = slice(v * 128, (v + 1) * 128)
        here = jnp.where(lane == j, got[:, u * 128 : (u + 1) * 128], 0.0)
        here = spread_sum(here, Q_LEN)
        student_sum, cross = here[0:1, :], here[1:2, :]
        teacher_sum, teacher_dot = side[2, 0:1, at_v], side[2, 1:2, at_v]
        loss = (teacher_dot - cross) / teacher_sum - jnp.log(teacher_sum) + jnp.log(student_sum)
        picks = [
            jnp.where(lane_1 == first_token + (a * Q_LEN - v * 128), loss, pick)
            for a, pick in enumerate(picks)
        ]
        cotangent = scale[:, at_v] / student_sum - side[1, :, at_v] / teacher_sum
        scale[:, at_v] = cotangent / den[:, at_v]
    line = jnp.zeros((1, 128), F32)
    for a, pick in enumerate(picks):
        line = jnp.where(lane_1 == a, jnp.sum(pick, axis=1, keepdims=True), line)
    out_loss[...] = line
    cot_p[...] = jnp.zeros(cot_p.shape, F32)

    def spread(side_of):
        def body(j, carry):
            inside = pl.ds(pl.multiple_of(j * CHUNK, CHUNK), CHUNK)
            at_q = pl.ds(pl.multiple_of(side_of * half + j * CHUNK, CHUNK), CHUNK)
            weights = jnp.concatenate(
                [
                    (terms[k * each : (k + 1) * each, at_q] * scale[k : k + 1, at_q]).astype(BF16)
                    for k in range(own)
                ],
                axis=0,
            )
            cot[side_of, inside, :] = dot(weights, emb_p[...], ((0,), (0,))).astype(BF16)
            cot_p[...] += jnp.dot(weights, q_all[at_q, :], preferred_element_type=F32)
            return carry

        lax.fori_loop(0, half // CHUNK, body, 0)

    sc, su, sy, sz, sx = (stage(a) for a in "cxyzx")
    spread(1 - c)
    sc.start(lambda to: cot.at[to], lambda k: cbuf)
    spread(c)
    g = cot_p[...]
    along = jnp.sum(g * unit_p[...], axis=-1, keepdims=True)
    uc[...] = (inv_p[...] * (g - unit_p[...] * along)).astype(BF16)
    su.start(lambda to: uc, lambda k: uc_all.at[x])
    uc_all[x] = uc[...]

    def prepare(u, m, mt):
        def body(j, carry):
            m[:, cut(j)] = nt(u[...], proj[cut(j), :]).astype(BF16)
            mt[cut(j), :] = nt(projp[cut(j), :], u[...]).astype(BF16)
            return carry

        lax.fori_loop(0, tiles, body, 0)

    unit_matrix = lax.broadcasted_iota(jnp.int32, (emb, emb), 0)
    unit_matrix = unit_matrix == lax.broadcasted_iota(jnp.int32, (emb, emb), 1)
    unit_matrix = jnp.where(unit_matrix, 1.0, 0.0).astype(BF16)

    def passages(k, first):
        g = lax.rem(x + k, NX)
        prepare(uc_all.at[g], mc, mct)
        for copy in loads[k]:
            copy.wait()
        uct = nt(unit_matrix, uc_all[g]).astype(BF16)
        cot_hid = jnp.dot(uct, hid[g], preferred_element_type=F32)
        if first:
            turned[...] = cot_hid
        else:
            turned[...] += cot_hid

        def body(j, carry):
            term = jnp.dot(mct[...], hid[g, :, cut(j)], preferred_element_type=F32)
            back = nt(mc[...], down[cut(j), :])
            pre = (back * dgelu[g, :, cut(j)]).astype(BF16)
            up = jnp.dot(rowst[g], pre, preferred_element_type=F32)
            if first:
                acc_down[:, cut(j)] = term
                acc_up[:, cut(j)] = up
            else:
                acc_down[:, cut(j)] += term
                acc_up[:, cut(j)] += up
            return carry

        lax.fori_loop(0, tiles, body, 0)

    passages(0, True)
    acc_proj[...] = jnp.dot(rowst[x], uc[...], preferred_element_type=F32)

    sc.arrive(lambda k, frm: cbuf)
    for i in range(NY):
        def block(ref, j):
            return ref[pl.ds(pl.multiple_of((i * NZ + j) * n, 16), n), :]

        def near(j, carry):
            value = block(cot.at[c], j).astype(F32) + block(cbuf, j).astype(F32)
            abuf[i, j] = value.astype(BF16)
            return carry

        lax.fori_loop(0, NZ, near, 0)
    sy.start(lambda to: abuf.at[to], lambda k: ybuf.at[k - 1])
    su.arrive(lambda k, frm: uc_all.at[frm])
    passages(3, False)
    sy.arrive(lambda k, frm: ybuf.at[k - 1])
    add_into(bbuf, NZ, lambda j: abuf[y, j], [ybuf.at[i] for i in range(NY - 1)])
    sz.start(lambda to: bbuf.at[to], lambda k: zbuf.at[k - 1])
    passages(1, False)
    sz.arrive(lambda k, frm: zbuf.at[k - 1])
    value = bbuf[z].astype(F32)
    for i in range(NZ - 1):
        value = value + zbuf[i].astype(F32)
    xbuf[x] = value.astype(BF16)
    sx.start(lambda to: xbuf.at[x], lambda k: xbuf.at[x])
    passages(2, False)
    sx.arrive(lambda k, frm: xbuf.at[frm])
    g = xbuf[0].astype(F32)
    for i in range(1, NX):
        g = g + xbuf[i].astype(F32)
    along = jnp.sum(g * unit_q[...], axis=-1, keepdims=True)
    ucq[...] = jnp.zeros(ucq.shape, BF16)
    ucq[0:n, :] = (inv_q[...] * (g - unit_q[...] * along)).astype(BF16)
    prepare(ucq, mcq, mctq)
    blocks = gp.shape[:3]
    chunks = []

    def onward(chunk):
        grads, near, total_a, far, _, _, _, s1, s2, _ = chunk
        s1.arrive(lambda k, frm: near)
        add_into(total_a, NY, lambda j: grads[c, j], [near])
        s2.start(lambda to: total_a.at[to], lambda k: far.at[k - 1])

    def leave(refs):
        chunk = tuple(refs) + tuple(stage(a) for a in "cyz")
        chunk[7].start(lambda to: chunk[0].at[to], lambda k: chunk[1])
        if chunks:
            onward(chunks[-1])
        chunks.append(chunk)

    def columns(i):
        return tuple(buf[i] for buf in bufs)

    for j in range(tiles):
        at_j = slice(j * TILE, (j + 1) * TILE)
        term = acc_down[:, at_j] + jnp.dot(
            mctq[...], hid_q[:, at_j], preferred_element_type=F32
        )
        bufs[0][j][...] = term.astype(BF16).reshape(blocks + (TILE,))
        leave(columns(j))

    part = n // NX
    at_row = lax.broadcasted_iota(jnp.int32, ucq.shape, 0)
    mine = jnp.logical_and(at_row >= x * part, at_row < (x + 1) * part)
    own = jnp.where(mine, ucq[...].astype(F32), 0.0).astype(BF16)
    term = acc_proj[...] + jnp.dot(rowstq[...], own, preferred_element_type=F32)
    cot_hid = turned[...] + jnp.dot(
        nt(unit_matrix, ucq[...]).astype(BF16), hid_q[...], preferred_element_type=F32
    )
    high = cot_hid.astype(BF16)
    low = (cot_hid - high.astype(F32)).astype(BF16)
    term = term + nt(downt[...], high) + nt(downt[...], low)
    gp[...] = term.astype(BF16).reshape(gp.shape)
    leave((gp, cp, ap, yp, fp, bp, zp))
    for j in range(tiles):
        at_j = slice(j * TILE, (j + 1) * TILE)
        back = nt(mcq[...], down[at_j, :])
        pre = (back * dgelu_q[:, at_j]).astype(BF16)
        up = acc_up[:, at_j] + jnp.dot(rowstq[...], pre, preferred_element_type=F32)
        bufs[0][tiles + j][...] = up.astype(BF16).reshape(blocks + (TILE,))
        leave(columns(tiles + j))

    onward(chunks[-1])
    per = width // (NY * NZ * NC)
    for grads, near, total_a, far, f32_sum, padded, last, s1, s2, s3 in chunks:
        s2.arrive(lambda k, frm: far.at[k - 1])
        value = total_a[y].astype(F32)
        for i in range(NY - 1):
            value = value + far[i].astype(F32)
        tall = value.shape[0]
        f32_sum[0:tall, :] = value
        f32_sum[tall : tall + 8, :] = jnp.zeros((8, value.shape[1]), F32)
        for i in range(NZ):
            padded[i] = f32_sum[i * per : i * per + 16, :].astype(BF16)
        s3.start(lambda to: padded.at[to], lambda k: last.at[k - 1])
    s4 = stage("x")
    for at_chunk in [tiles] + [i for i in range(len(chunks)) if i != tiles]:
        grads, near, total_a, far, f32_sum, padded, last, s1, s2, s3 = chunks[at_chunk]
        s3.arrive(lambda k, frm: last.at[k - 1])
        value = padded[z].astype(F32)
        for i in range(NZ - 1):
            value = value + last[i].astype(F32)
        if at_chunk == tiles:
            xp[x] = value
            s4.start(lambda to: xp.at[x], lambda k: xp.at[x])
        elif at_chunk < tiles:
            out_down[:, at_chunk * TILE : (at_chunk + 1) * TILE] = value
        else:
            at_j = at_chunk - tiles - 1
            out_up[:, at_j * TILE : (at_j + 1) * TILE] = value
    s4.arrive(lambda k, frm: xp.at[frm])
    value = xp[0]
    for i in range(1, NX):
        value = value + xp[i]
    out_proj[...] = value
    for copy in copies:
        copy.wait_send()
    for s in [sc, su, sy, sz, sx, s4] + [s for chunk in chunks for s in chunk[7:]]:
        s.finish()


def backward(own, q_len, *args):
    q_all, rowst, hid, rowstq, unit_q = args[0], args[5], args[6], args[9], args[12]
    n, emb = unit_q.shape
    many_q = q_all.shape[0]
    width, many = rowst.shape[1:]
    hidden = hid.shape[2]
    few = rowstq.shape[1]
    tall = width // (NC * NY)
    V = pltpu.VMEM
    outs = [jax.ShapeDtypeStruct((16, w), F32) for w in (hidden, hidden, emb)]
    outs.append(jax.ShapeDtypeStruct((1, 128), F32))
    packed = (8, -(-many_q // (128 * q_len)) * 128)
    scratch = [
        V((many, many_q), F32),
        V((many, emb), BF16),
        V((8, many_q), F32),
        V((8, many_q), F32),
        V((many, emb), F32),
        V(packed, F32),
        V(packed, F32),
        V(packed, F32),
        V((NY * NX,) + packed, F32),
        V((NZ * NC,) + packed, F32),
        V((NC, many_q // NC, emb), BF16),
        V((many, emb), BF16),
        V((NX, many, emb), BF16),
        V((many_q // NC, emb), BF16),
        V((NY, NZ, n, emb), BF16),
        V((NY - 1, NZ, n, emb), BF16),
        V((NZ, n, emb), BF16),
        V((NZ - 1, n, emb), BF16),
        V((NX, n, emb), BF16),
        V((many, width), BF16),
        V((width, many), BF16),
        V((few, width), BF16),
        V((width, few), BF16),
        V((few, emb), BF16),
        V((NX, width, many), BF16),
        V((NX, many, hidden), BF16),
        V((NX, many, hidden), F32),
        V((emb, hidden), F32),
        V((width, hidden), F32),
        V((width, hidden), F32),
        V((width, emb), F32),
    ]
    parts = 2 * (hidden // TILE)

    def chunk_buffers(w):
        return [
            V((NC, NY, tall, w), BF16),
            V((NY, tall, w), BF16),
            V((NY, tall, w), BF16),
            V((NY - 1, tall, w), BF16),
            V((tall + 8, w), F32),
            V((NZ, 16, w), BF16),
            V((NZ - 1, 16, w), BF16),
        ]

    scratch += chunk_buffers(emb)
    scratch += [V((NX, 16, emb), F32), pltpu.SemaphoreType.DMA((3 * NX,))]
    for buffer in chunk_buffers(TILE):
        scratch += [buffer] * parts
    scratch += sems(NY * NX - 1) + sems(NZ * NC - 1)
    for a in "cxyzx" + "cyz" * (parts + 1) + "x":
        scratch += sems({"x": NX, "y": NY, "z": NZ, "c": NC}[a] - 1)
    kernel = functools.partial(back_kernel, own, q_len)
    return call(kernel, outs, scratch, 3, *args, outer=([5, 6, 7], ()), scalars=[4])


def trim_kernel(n, *refs):
    half = len(refs) // 2
    for src, dst in zip(refs[:half], refs[half:]):
        dst[...] = src[0:n, :]


def trim(n, *arrays):
    return pl.pallas_call(
        functools.partial(trim_kernel, n),
        out_shape=[jax.ShapeDtypeStruct((n, a.shape[1]), a.dtype) for a in arrays],
        in_specs=[VMEM] * len(arrays),
        out_specs=[VMEM] * len(arrays),
    )(*arrays)


def local(
    passage_states,
    query_states,
    lengths,
    owner_map,
    candidates,
    teacher_scores,
    up_weight,
    down_weight,
    proj_weight,
):
    p_dev, pass_len, width = passage_states.shape
    q_dev, q_len, _ = query_states.shape
    emb = proj_weight.shape[1]
    n_dp = NY * NZ * NC
    p_own = p_dev // NX
    q_rows = q_dev * q_len
    rows = width // n_dp

    order = np.arange(width).reshape(NY, NZ, NC, rows).transpose(2, 0, 1, 3).reshape(-1)
    perm = jnp.asarray(np.eye(width)[order], BF16)
    (
        rowst, hid_p, slope_p, downt, unit_p, inv_p, q_all, side,
        rowstq, hid_q, slope_q, unit_q, inv_q, projp,
    ) = encode(
        passage_states, query_states.reshape(q_rows, width), up_weight, down_weight,
        proj_weight, perm, owner_map, candidates, teacher_scores,
    )
    q_all = q_all.reshape(n_dp * q_rows, emb)
    up, down, grad_proj, loss = backward(
        p_own, q_len, q_all, unit_p, inv_p, side, lengths,
        rowst, hid_p, slope_p, downt, rowstq, hid_q, slope_q, unit_q, inv_q,
        down_weight, proj_weight, projp,
    )
    up, down, grad_proj = trim(rows, up, down, grad_proj)
    return loss[0, :q_dev], up, down.T, grad_proj


def solution(mesh):
    return jax.shard_map(
        local,
        mesh=mesh,
        in_specs=(
            P("dp", None, None),
            P("dp", None, None),
            P(),
            P(),
            P("dp", "mp"),
            P("dp", "mp"),
            P(None, "mp"),
            P("mp", None),
            P(),
        ),
        out_specs=(P("dp"), P("dp", "mp"), P("mp", "dp"), P("dp", None)),
        check_vma=False,
    )
```

```python
import functools

import jax
import numpy as np
import jax.numpy as jnp
from jax import lax
from jax.experimental import pallas as pl
from jax.experimental.pallas import tpu as pltpu
from jax.sharding import PartitionSpec as P

TAU = 0.05
EPS = 1e-06
F32 = jnp.float32
BF16 = jnp.bfloat16
NY, NZ, NC, NX = 4, 8, 2, 4
MESH = pl.DeviceIdType.MESH
VMEM = pl.BlockSpec(memory_space=pltpu.VMEM)


def dot(a, b, dims):
    return lax.dot_general(a, b, (dims, ((), ())), preferred_element_type=F32)


def place():
    dp, x = lax.axis_index("dp"), lax.axis_index("mp")
    return dp // (NZ * NC), (dp // NC) % NZ, dp % NC, x


def at(y, z, c, x):
    return ((y * NZ + z) * NC + c, x)


def peers(axis):
    y, z, c, x = place()
    out = []
    size = {"x": NX, "y": NY, "z": NZ, "c": NC}[axis]
    mine = {"x": x, "y": y, "z": z, "c": c}[axis]
    for k in range(1, size):
        to = (mine + k) % size
        frm = (mine + size - k) % size
        who = {"x": (y, z, c, to), "y": (to, z, c, x), "z": (y, to, c, x), "c": (y, z, to, x)}[axis]
        out.append((k, at(*who), to, frm))
    return out


def greet(axes):
    barrier = pltpu.get_barrier_semaphore()
    total = 0
    for axis in axes:
        for _, who, _, _ in peers(axis):
            pl.semaphore_signal(barrier, inc=1, device_id=who, device_id_type=MESH)
            total += 1
    pl.semaphore_wait(barrier, total)


class Stage:
    def __init__(self, axis, send_sem, recv_sem):
        self.axis, self.send_sem, self.recv_sem = axis, send_sem, recv_sem
        self.sent = []

    def start(self, src, dst):
        for k, who, to, _ in peers(self.axis):
            copy = pltpu.make_async_remote_copy(
                src_ref=src(to),
                dst_ref=dst(k),
                send_sem=self.send_sem.at[k - 1],
                recv_sem=self.recv_sem.at[k - 1],
                device_id=who,
                device_id_type=MESH,
            )
            copy.start()
            self.sent.append(copy)

    def arrive(self, dst):
        for k, who, _, frm in peers(self.axis):
            ref = dst(k, frm)
            pltpu.make_async_remote_copy(
                src_ref=ref,
                dst_ref=ref,
                send_sem=self.send_sem.at[k - 1],
                recv_sem=self.recv_sem.at[k - 1],
                device_id=who,
                device_id_type=MESH,
            ).wait_recv()

    def finish(self):
        for copy in self.sent:
            copy.wait_send()


def sems(n):
    return [pltpu.SemaphoreType.DMA((max(n, 1),)), pltpu.SemaphoreType.DMA((max(n, 1),))]


def call(kernel, outs, scratch, number, *args, outer=((), ()), scalars=()):
    def spec(i, which, small=()):
        if i in small:
            return pl.BlockSpec(memory_space=pltpu.SMEM)
        return pl.BlockSpec(memory_space=pl.ANY) if i in which else VMEM

    return pl.pallas_call(
        kernel,
        out_shape=outs,
        in_specs=[spec(i, outer[0], scalars) for i in range(len(args))],
        out_specs=[spec(i, outer[1]) for i in range(len(outs))],
        scratch_shapes=scratch,
        compiler_params=pltpu.CompilerParams(
            collective_id=number, has_side_effects=True, vmem_limit_bytes=58 * 2**20
        ),
        cost_estimate=pl.CostEstimate(flops=10**9, bytes_accessed=60 * 10**6, transcendentals=0),
    )(*args)


TILE = 256
ROOT = (2.0 / np.pi) ** 0.5


def cut(j):
    return pl.ds(pl.multiple_of(j * TILE, TILE), TILE)


def nt(a, b):
    return dot(a, b, ((1,), (1,)))


def tiled(tiles, body):
    def step(j, carry):
        body(j)
        return carry

    lax.fori_loop(0, tiles, step, 0)


def encode_kernel(
    q_len, states, rows_q, up, down, proj, perm, owner_map, candidates, teacher,
    rows_out, hid_out, slope_out, unit, inverse, q_all, side,
    rowstq, hid_q, slope_q, unit_q, inv_q, projp,
    rows, hid, slope, part, sent, arrived, padq, partq, sent_q, pbuf, tbuf, table, t_all,
    ring_send, ring_recv, save, *sem
):
    y, z, c, x = place()
    greet("xzyc")
    sx, tx = Stage("x", sem[0], sem[1]), Stage("x", sem[2], sem[3])
    sz, tz = Stage("z", sem[4], sem[5]), Stage("z", sem[6], sem[7])
    sy, ty = Stage("y", sem[8], sem[9]), Stage("y", sem[10], sem[11])
    sc, tc = Stage("c", sem[12], sem[13]), Stage("c", sem[14], sem[15])
    width = up.shape[0]
    tiles = width // TILE
    nq = rows_q.shape[0]
    own, length = states.shape[0] // NX, states.shape[1]
    many = rows.shape[1]
    each = many // own
    ring, saves = [], []

    def ring_copy(i, src, dst, who):
        return pltpu.make_async_remote_copy(
            src_ref=src, dst_ref=dst, send_sem=ring_send.at[i], recv_sem=ring_recv.at[i],
            device_id=who, device_id_type=MESH,
        )

    def send(i, src, dst, who):
        copy = ring_copy(i, src, dst, who)
        copy.start()
        ring.append(copy)

    def keep(src, dst):
        copy = pltpu.make_async_copy(src, dst, save.at[len(saves)])
        copy.start()
        saves.append(copy)

    def feed(r, h, d, out):
        def first(j):
            v = jnp.dot(r[...], up[:, cut(j)], preferred_element_type=F32)
            v2 = v * v
            t = jnp.tanh(ROOT * v * (1.0 + 0.044715 * v2))
            h[:, cut(j)] = (0.5 * v * (1.0 + t)).astype(BF16)
            d[:, cut(j)] = 0.5 * (1.0 + t) + (0.5 * ROOT) * v * (1.0 - t * t) * (
                1.0 + (3 * 0.044715) * v2
            )

        tiled(tiles, first)

        def second(j):
            out[:, cut(j)] = jnp.dot(
                h[...], down[:, cut(j)], preferred_element_type=F32
            ).astype(BF16)

        tiled(tiles, second)

    def group(k):
        g = lax.rem(x + k, NX)
        for i in range(own):
            rows[g, each * (i + 1) - 16 : each * (i + 1), :] = jnp.zeros((16, width), BF16)
            rows[g, each * i : each * i + length, :] = states[g * own + i]
        keep(rows.at[g], rows_out.at[g])
        feed(rows.at[g], hid.at[g], slope.at[g], part)
        sent[k] = jnp.dot(part[...], proj[...], preferred_element_type=F32)
        if k:
            send(k - 1, sent.at[k], arrived.at[k - 1], at(y, z, c, g))
        keep(hid.at[g], hid_out.at[g])
        keep(slope.at[g], slope_out.at[g])

    row = lax.broadcasted_iota(jnp.int32, table.shape, 0)
    lane = lax.broadcasted_iota(jnp.int32, table.shape, 1)
    value = jnp.zeros(table.shape, F32)
    few_c = candidates.shape[1]
    for b in range(few_c):
        at_b = jnp.logical_and(lane % (few_c * NX) == x * few_c + b, row < candidates.shape[0])
        for a in range(candidates.shape[0]):
            here = jnp.logical_and(at_b, row == a)
            position = owner_map[candidates[a, b]].astype(F32)
            value = jnp.where(here, jnp.where(lane < few_c * NX, position, teacher[a, b]), value)
    table[...] = value
    tx.start(lambda to: table, lambda k: tbuf.at[x])
    tbuf[x] = table[...]
    padq[...] = jnp.zeros(padq.shape, BF16)
    padq[0:nq, :] = rows_q[...]
    feed(padq, hid_q, slope_q, partq)
    sent_q[...] = jnp.dot(partq[0:nq, :], proj[...], preferred_element_type=F32)
    sx.start(lambda to: sent_q, lambda k: pbuf.at[x])
    pbuf[x] = sent_q[...]
    group(2)
    tx.arrive(lambda k, frm: tbuf.at[frm])
    merged = tbuf[0]
    for i in range(1, NX):
        merged = merged + tbuf[i]
    t_all[c, y, z] = merged
    tz.start(lambda to: t_all.at[c, y, z], lambda k: t_all.at[c, y, z])
    sx.arrive(lambda k, frm: pbuf.at[frm])
    projected = jnp.dot(rows_q[...], proj[...], preferred_element_type=F32)
    for i in range(NX):
        projected = projected + pbuf[i]
    inv = lax.rsqrt(jnp.sum(projected * projected, axis=-1, keepdims=True) + EPS)
    inv_q[...] = inv
    unit_q[...] = projected * inv
    q_all[c, y, z] = (projected * inv).astype(BF16)
    sz.start(lambda to: q_all.at[c, y, z], lambda k: q_all.at[c, y, z])
    group(1)
    tz.arrive(lambda k, frm: t_all.at[c, y, frm])
    ty.start(lambda to: t_all.at[c, y], lambda k: t_all.at[c, y])
    group(3)
    sz.arrive(lambda k, frm: q_all.at[c, y, frm])
    sy.start(lambda to: q_all.at[c, y], lambda k: q_all.at[c, y])
    ty.arrive(lambda k, frm: t_all.at[c, frm])
    tc.start(lambda to: t_all.at[c], lambda k: t_all.at[c])
    group(0)

    def turn_q(j):
        rowstq[cut(j), :] = nt(perm[cut(j), :], padq[...]).astype(BF16)
        projp[cut(j), :] = jnp.dot(
            perm[cut(j), :], proj[...], preferred_element_type=F32
        ).astype(BF16)

    tiled(tiles, turn_q)

    sy.arrive(lambda k, frm: q_all.at[c, frm])
    sc.start(lambda to: q_all.at[c], lambda k: q_all.at[c])
    tc.arrive(lambda k, frm: t_all.at[frm])

    side[...] = jnp.zeros(side.shape, F32)
    base = ((y * NZ + z) * NC + c) * (own * NX) + x * own
    rows4, span = 4 * t_all.shape[3], 4 * nq
    all_c = few_c * NX
    r = lax.broadcasted_iota(jnp.int32, (rows4, span), 0)
    start = (r // 8) * nq + (r % 8) * q_len
    token = lax.broadcasted_iota(jnp.int32, (rows4, span), 1)
    spread = jnp.logical_and(token >= start, token < start + q_len)
    spread = jnp.logical_and(spread, r % 8 < candidates.shape[0]).astype(F32)
    left_half = lax.broadcasted_iota(jnp.int32, (rows4, 2 * all_c), 1) < all_c

    def tally(b):
        per_y = NZ // 4
        got = t_all[b // (NY * per_y), (b // per_y) % NY, pl.ds((b % per_y) * 4, 4)]
        got = got.reshape(rows4, 2 * all_c)
        scores = jnp.where(left_half, pltpu.roll(got, all_c, 1), 0.0)
        mass = jnp.where(left_half, jnp.exp(scores), 0.0)
        tokens = pl.ds(pl.multiple_of(b * span, 128), span)

        def put(i, k, column):
            line = jnp.sum(jnp.sum(column, axis=1, keepdims=True) * spread, axis=0, keepdims=True)
            side[i, k : k + 1, tokens] = line

        for k in range(own):
            hit = jnp.logical_and(left_half, got == (base + k).astype(F32))
            put(0, k, jnp.where(hit, 1.0, 0.0))
            put(1, k, jnp.where(hit, mass, 0.0))
        put(2, 0, mass)
        put(2, 1, mass * scores)

    tiled(NC * NY * NZ // 4, tally)
    for i in range(NX - 1):
        ring_copy(i, arrived.at[i], arrived.at[i], at(y, z, c, x)).wait_recv()

    def finish_rows(i):
        at_rows = pl.ds(pl.multiple_of(i * each, 16), each)
        projected = jnp.dot(rows[x, at_rows, :], proj[...], preferred_element_type=F32)
        projected = projected + sent[0, at_rows, :]
        for k in range(NX - 1):
            projected = projected + arrived[k, at_rows, :]
        inv = lax.rsqrt(jnp.sum(projected * projected, axis=-1, keepdims=True) + EPS)
        inverse[at_rows, :] = inv
        unit[at_rows, :] = projected * inv

    tiled(own, finish_rows)
    sc.arrive(lambda k, frm: q_all.at[frm])
    for stage in (sx, tx, sz, tz, sy, ty, sc, tc):
        stage.finish()
    for copy in ring:
        copy.wait_send()
    for copy in saves:
        copy.wait()


def encode(states, rows_q, up, down, proj, perm, owner_map, candidates, teacher):
    nq, width = rows_q.shape
    hidden, emb = up.shape[1], proj.shape[1]
    own = states.shape[0] // NX
    many = own * ((states.shape[1] + 15) // 16 * 16)
    few = (nq + 127) // 128 * 128
    shape, V = jax.ShapeDtypeStruct, pltpu.VMEM
    table = (8, 2 * NX * candidates.shape[1])
    outs = [
        shape((NX, many, width), BF16),
        shape((NX, many, hidden), BF16),
        shape((NX, many, hidden), F32),
        shape((many, emb), F32),
        shape((many, 1), F32),
        shape((NC, NY, NZ, nq, emb), BF16),
        shape((3, 8, NC * NY * NZ * nq), F32),
        shape((width, few), BF16),
        shape((few, hidden), BF16),
        shape((few, hidden), F32),
        shape((nq, emb), F32),
        shape((nq, 1), F32),
        shape((width, emb), BF16),
    ]
    scratch = [
        V((NX, many, width), BF16),
        V((NX, many, hidden), BF16),
        V((NX, many, hidden), F32),
        V((many, width), BF16),
        V((NX, many, emb), F32),
        V((NX - 1, many, emb), F32),
        V((few, width), BF16),
        V((few, width), BF16),
        V((nq, emb), F32),
        V((NX, nq, emb), F32),
        V((NX,) + table, F32),
        V(table, F32),
        V((NC, NY, NZ) + table, F32),
    ] + sems(NX - 1) + [pltpu.SemaphoreType.DMA((3 * NX,))]
    for size in (NX, NX, NZ, NZ, NY, NY, NC, NC):
        scratch += sems(size - 1)
    args = (states, rows_q, up, down, proj, perm, owner_map, candidates, teacher)
    kernel = functools.partial(encode_kernel, nq // candidates.shape[0])
    return call(kernel, outs, scratch, 1, *args, outer=([], [0, 1, 2]), scalars=[6, 7, 8])


def circles(y, z, c, x):
    return (
        (NY * NX, y * NX + x, lambda i: at(i // NX, z, c, i % NX)),
        (NZ * NC, z * NC + c, lambda i: at(y, i // NC, i % NC, x)),
    )


def circle_sum(group, held, buf, out, send, recv, meanwhile):
    size, mine, who = group
    copies = []
    buf[mine] = held[...]
    for k in range(1, size):
        copy = pltpu.make_async_remote_copy(
            src_ref=held, dst_ref=buf.at[mine], send_sem=send.at[k - 1], recv_sem=recv.at[k - 1],
            device_id=who((mine + k) % size), device_id_type=MESH,
        )
        copy.start()
        copies.append(copy)
    meanwhile()
    for k in range(1, size):
        ref = buf.at[(mine + size - k) % size]
        pltpu.make_async_remote_copy(
            src_ref=ref, dst_ref=ref, send_sem=send.at[k - 1], recv_sem=recv.at[k - 1],
            device_id=who((mine + k) % size), device_id_type=MESH,
        ).wait_recv()
    total = buf[0]
    for i in range(1, size):
        total = total + buf[i]
    out[...] = total
    return copies


def spread_sum(v, span):
    lane = lax.broadcasted_iota(jnp.int32, v.shape, 1)
    width = v.shape[1]
    k = 1
    while k < span:
        other = jnp.where((lane & k) != 0, pltpu.roll(v, k, 1), pltpu.roll(v, width - k, 1))
        v = v + other
        k *= 2
    return v


def add_into(dst, index, first, others):
    def body(i, carry):
        value = first(i).astype(F32)
        for other in others:
            value = value + other[i].astype(F32)
        dst[i] = value.astype(dst.dtype)
        return carry

    lax.fori_loop(0, index, body, 0)


CHUNK = 512


def back_kernel(
    P_OWN, Q_LEN,
    q_all, unit_p, inv_p, side, lens, rows_in, hid_in, slope_in, perm, rowstq, hid_q, dgelu_q,
    unit_q, inv_q, down, proj, projp,
    out_up, out_down, out_proj, out_loss,
    terms, emb_p, den, scale, cot_p, held, summed, totals, near_sums, far_sums, cot, uc,
    uc_all, cbuf, abuf, ybuf, bbuf, zbuf, xbuf, mc, mct, mcq, mctq, ucq, rowst, hid, dgelu, turned, downt,
    acc_up, acc_down, acc_proj,
    gp, cp, yp, fp, bp, zp, xp, load, *rest
):
    y, z, c, x = place()
    tiles = down.shape[1] // TILE
    parts = 2 * tiles
    bufs = [rest[i * parts : (i + 1) * parts] for i in range(6)]
    sem = list(rest[6 * parts :])

    def stage(axis):
        send, recv = sem.pop(0), sem.pop(0)
        return Stage(axis, send, recv)

    barrier = pltpu.get_barrier_semaphore()
    groups = circles(y, z, c, x)
    for size, mine, who in groups:
        for k in range(1, size):
            pl.semaphore_signal(
                barrier, inc=1, device_id=who((mine + k) % size), device_id_type=MESH
            )
    width = down.shape[1]

    loads, row_loads = {}, []
    for i, k in enumerate((0, 3, 1, 2)):
        g = lax.rem(x + k, NX)
        loads[k] = [
            pltpu.make_async_copy(src.at[g], dst.at[g], load.at[2 * i + n])
            for n, (src, dst) in enumerate(((hid_in, hid), (slope_in, dgelu)))
        ]
        row_loads.append(
            pltpu.make_async_copy(rows_in.at[g], mc, load.at[2 * NX + i])
        )
    row_loads[0].start()
    for k in (0, 3, 1, 2):
        for copy in loads[k]:
            copy.start()

    def turn(i, k):
        row_loads[i].wait()

        def body(j):
            rowst[lax.rem(x + k, NX), cut(j), :] = nt(perm[cut(j), :], mc[...]).astype(BF16)

        tiled(tiles, body)
        if i + 1 < NX:
            row_loads[i + 1].start()

    def turn_first():
        for i, k in ((0, 0), (1, 3)):
            turn(i, k)

    def turn_rest():
        def body(j):
            downt[cut(j), :] = nt(perm[cut(j), :], down[...]).astype(BF16)

        tiled(tiles, body)
        for i, k in ((2, 1), (3, 2)):
            turn(i, k)

    many = unit_p.shape[0]
    many_q, emb = q_all.shape
    own = P_OWN
    each = many // own
    n = unit_q.shape[0]
    half = many_q // NC
    base = ((y * NZ + z) * NC + c) * (own * NX) + x * own
    emb_p[...] = unit_p[...].astype(BF16)
    den[...] = jnp.ones(den.shape, F32)

    def score(j, carry):
        at_q = pl.ds(pl.multiple_of(j * CHUNK, CHUNK), CHUNK)
        row = lax.broadcasted_iota(jnp.int32, (each, CHUNK), 0)
        for k in range(own):
            rows_k = slice(k * each, (k + 1) * each)
            similar = nt(emb_p[rows_k, :], q_all[at_q, :])
            value = jnp.where(row < lens[base + k], jnp.exp(similar * (1.0 / TAU)), 0.0)
            terms[rows_k, at_q] = value
            den[k : k + 1, at_q] = jnp.sum(value, axis=0, keepdims=True)
        return carry

    lax.fori_loop(0, many_q // CHUNK, score, 0)
    scores = TAU * spread_sum(jnp.log(den[...]), Q_LEN)
    student = side[0] * jnp.exp(scores)
    scale[...] = student
    first = jnp.sum(student, axis=0, keepdims=True)
    second = jnp.sum(side[1] * scores, axis=0, keepdims=True)
    lane = lax.broadcasted_iota(jnp.int32, (1, 128), 1) % Q_LEN
    for r, line in enumerate((first, second)):
        for u in range(held.shape[1] // 128):
            packed = jnp.zeros((1, 128), F32)
            for j in range(min(Q_LEN, many_q // 128 - u * Q_LEN)):
                v = u * Q_LEN + j
                packed = jnp.where(lane == j, line[:, v * 128 : (v + 1) * 128], packed)
            held[r : r + 1, u * 128 : (u + 1) * 128] = packed
    held[2:8, :] = jnp.zeros((6, held.shape[1]), F32)
    pl.semaphore_wait(barrier, NY * NX + NZ * NC - 2)
    sum_sems = [sem.pop(0) for _ in range(4)]
    copies = circle_sum(groups[0], held, near_sums, summed, sum_sems[0], sum_sems[1], turn_first)
    copies += circle_sum(groups[1], summed, far_sums, totals, sum_sems[2], sum_sems[3], turn_rest)
    lane = lax.broadcasted_iota(jnp.int32, (8, 128), 1) % Q_LEN
    got = totals[...]
    lane_1 = lax.broadcasted_iota(jnp.int32, (1, 128), 1)
    first_token = ((c * NY + y) * NZ + z) * n
    picks = [jnp.zeros((1, 128), F32)] * (n // Q_LEN)
    for v in range(many_q // 128):
        u, j = v // Q_LEN, v % Q_LEN
        at_v = slice(v * 128, (v + 1) * 128)
        here = jnp.where(lane == j, got[:, u * 128 : (u + 1) * 128], 0.0)
        here = spread_sum(here, Q_LEN)
        student_sum, cross = here[0:1, :], here[1:2, :]
        teacher_sum, teacher_dot = side[2, 0:1, at_v], side[2, 1:2, at_v]
        loss = (teacher_dot - cross) / teacher_sum - jnp.log(teacher_sum) + jnp.log(student_sum)
        picks = [
            jnp.where(lane_1 == first_token + (a * Q_LEN - v * 128), loss, pick)
            for a, pick in enumerate(picks)
        ]
        cotangent = scale[:, at_v] / student_sum - side[1, :, at_v] / teacher_sum
        scale[:, at_v] = cotangent / den[:, at_v]
    line = jnp.zeros((1, 128), F32)
    for a, pick in enumerate(picks):
        line = jnp.where(lane_1 == a, jnp.sum(pick, axis=1, keepdims=True), line)
    out_loss[...] = line
    cot_p[...] = jnp.zeros(cot_p.shape, F32)

    def spread(side_of):
        def body(j, carry):
            inside = pl.ds(pl.multiple_of(j * CHUNK, CHUNK), CHUNK)
            at_q = pl.ds(pl.multiple_of(side_of * half + j * CHUNK, CHUNK), CHUNK)
            weights = jnp.concatenate(
                [
                    (terms[k * each : (k + 1) * each, at_q] * scale[k : k + 1, at_q]).astype(BF16)
                    for k in range(own)
                ],
                axis=0,
            )
            cot[side_of, inside, :] = dot(weights, emb_p[...], ((0,), (0,))).astype(BF16)
            cot_p[...] += jnp.dot(weights, q_all[at_q, :], preferred_element_type=F32)
            return carry

        lax.fori_loop(0, half // CHUNK, body, 0)

    sc, su, sy, sz, sx = (stage(a) for a in "cxyzx")
    spread(1 - c)
    sc.start(lambda to: cot.at[to], lambda k: cbuf)
    spread(c)
    g = cot_p[...]
    along = jnp.sum(g * unit_p[...], axis=-1, keepdims=True)
    uc[...] = (inv_p[...] * (g - unit_p[...] * along)).astype(BF16)
    su.start(lambda to: uc, lambda k: uc_all.at[x])
    uc_all[x] = uc[...]

    def prepare(u, m, mt):
        def body(j, carry):
            m[:, cut(j)] = nt(u[...], proj[cut(j), :]).astype(BF16)
            mt[cut(j), :] = nt(projp[cut(j), :], u[...]).astype(BF16)
            return carry

        lax.fori_loop(0, tiles, body, 0)

    unit_matrix = lax.broadcasted_iota(jnp.int32, (emb, emb), 0)
    unit_matrix = unit_matrix == lax.broadcasted_iota(jnp.int32, (emb, emb), 1)
    unit_matrix = jnp.where(unit_matrix, 1.0, 0.0).astype(BF16)

    def passages(k, first):
        g = lax.rem(x + k, NX)
        prepare(uc_all.at[g], mc, mct)
        for copy in loads[k]:
            copy.wait()
        uct = nt(unit_matrix, uc_all[g]).astype(BF16)
        cot_hid = jnp.dot(uct, hid[g], preferred_element_type=F32)
        if first:
            turned[...] = cot_hid
        else:
            turned[...] += cot_hid

        def body(j, carry):
            term = jnp.dot(mct[...], hid[g, :, cut(j)], preferred_element_type=F32)
            back = nt(mc[...], down[cut(j), :])
            pre = (back * dgelu[g, :, cut(j)]).astype(BF16)
            up = jnp.dot(rowst[g], pre, preferred_element_type=F32)
            if first:
                acc_down[:, cut(j)] = term
                acc_up[:, cut(j)] = up
            else:
                acc_down[:, cut(j)] += term
                acc_up[:, cut(j)] += up
            return carry

        lax.fori_loop(0, tiles, body, 0)

    passages(0, True)
    acc_proj[...] = jnp.dot(rowst[x], uc[...], preferred_element_type=F32)

    sc.arrive(lambda k, frm: cbuf)
    for i in range(NY):
        def block(ref, j):
            return ref[pl.ds(pl.multiple_of((i * NZ + j) * n, 16), n), :]

        def near(j, carry):
            value = block(cot.at[c], j).astype(F32) + block(cbuf, j).astype(F32)
            abuf[i, j] = value.astype(BF16)
            return carry

        lax.fori_loop(0, NZ, near, 0)
    sy.start(lambda to: abuf.at[to], lambda k: ybuf.at[k - 1])
    su.arrive(lambda k, frm: uc_all.at[frm])
    passages(3, False)
    sy.arrive(lambda k, frm: ybuf.at[k - 1])
    add_into(bbuf, NZ, lambda j: abuf[y, j], [ybuf.at[i] for i in range(NY - 1)])
    sz.start(lambda to: bbuf.at[to], lambda k: zbuf.at[k - 1])
    passages(1, False)
    sz.arrive(lambda k, frm: zbuf.at[k - 1])
    value = bbuf[z].astype(F32)
    for i in range(NZ - 1):
        value = value + zbuf[i].astype(F32)
    xbuf[x] = value.astype(BF16)
    sx.start(lambda to: xbuf.at[x], lambda k: xbuf.at[x])
    passages(2, False)
    sx.arrive(lambda k, frm: xbuf.at[frm])
    g = xbuf[0].astype(F32)
    for i in range(1, NX):
        g = g + xbuf[i].astype(F32)
    along = jnp.sum(g * unit_q[...], axis=-1, keepdims=True)
    ucq[...] = jnp.zeros(ucq.shape, BF16)
    ucq[0:n, :] = (inv_q[...] * (g - unit_q[...] * along)).astype(BF16)
    prepare(ucq, mcq, mctq)
    blocks = gp.shape[:3]
    chunks = []

    def onward(chunk):
        grads, near, far, _, _, _, s1, s2, _ = chunk
        s1.arrive(lambda k, frm: near)
        add_into(grads.at[c], NY, lambda j: grads[c, j], [near])
        s2.start(lambda to: grads.at[c, to], lambda k: far.at[k - 1])

    def leave(refs):
        chunk = tuple(refs) + tuple(stage(a) for a in "cyz")
        chunk[6].start(lambda to: chunk[0].at[to], lambda k: chunk[1])
        if chunks:
            onward(chunks[-1])
        chunks.append(chunk)

    def columns(i):
        return tuple(buf[i] for buf in bufs)

    for j in range(tiles):
        at_j = slice(j * TILE, (j + 1) * TILE)
        term = acc_down[:, at_j] + jnp.dot(
            mctq[...], hid_q[:, at_j], preferred_element_type=F32
        )
        bufs[0][j][...] = term.astype(BF16).reshape(blocks + (TILE,))
        leave(columns(j))

    part = n // NX
    at_row = lax.broadcasted_iota(jnp.int32, ucq.shape, 0)
    mine = jnp.logical_and(at_row >= x * part, at_row < (x + 1) * part)
    own = jnp.where(mine, ucq[...].astype(F32), 0.0).astype(BF16)
    term = acc_proj[...] + jnp.dot(rowstq[...], own, preferred_element_type=F32)
    cot_hid = turned[...] + jnp.dot(
        nt(unit_matrix, ucq[...]).astype(BF16), hid_q[...], preferred_element_type=F32
    )
    high = cot_hid.astype(BF16)
    low = (cot_hid - high.astype(F32)).astype(BF16)
    term = term + nt(downt[...], high) + nt(downt[...], low)
    gp[...] = term.astype(BF16).reshape(gp.shape)
    leave((gp, cp, yp, fp, bp, zp))
    for j in range(tiles):
        at_j = slice(j * TILE, (j + 1) * TILE)
        back = nt(mcq[...], down[at_j, :])
        pre = (back * dgelu_q[:, at_j]).astype(BF16)
        up = acc_up[:, at_j] + jnp.dot(rowstq[...], pre, preferred_element_type=F32)
        bufs[0][tiles + j][...] = up.astype(BF16).reshape(blocks + (TILE,))
        leave(columns(tiles + j))

    onward(chunks[-1])
    per = width // (NY * NZ * NC)
    for grads, near, far, f32_sum, padded, last, s1, s2, s3 in chunks:
        s2.arrive(lambda k, frm: far.at[k - 1])
        value = grads[c, y].astype(F32)
        for i in range(NY - 1):
            value = value + far[i].astype(F32)
        tall = value.shape[0]
        f32_sum[0:tall, :] = value
        f32_sum[tall : tall + 8, :] = jnp.zeros((8, value.shape[1]), F32)
        for i in range(NZ):
            padded[i] = f32_sum[i * per : i * per + 16, :].astype(BF16)
        s3.start(lambda to: padded.at[to], lambda k: last.at[k - 1])
    s4 = stage("x")
    for at_chunk in [tiles] + [i for i in range(len(chunks)) if i != tiles]:
        grads, near, far, f32_sum, padded, last, s1, s2, s3 = chunks[at_chunk]
        s3.arrive(lambda k, frm: last.at[k - 1])
        value = padded[z].astype(F32)
        for i in range(NZ - 1):
            value = value + last[i].astype(F32)
        if at_chunk == tiles:
            xp[x] = value
            s4.start(lambda to: xp.at[x], lambda k: xp.at[x])
        elif at_chunk < tiles:
            out_down[:, at_chunk * TILE : (at_chunk + 1) * TILE] = value
        else:
            at_j = at_chunk - tiles - 1
            out_up[:, at_j * TILE : (at_j + 1) * TILE] = value
    s4.arrive(lambda k, frm: xp.at[frm])
    value = xp[0]
    for i in range(1, NX):
        value = value + xp[i]
    out_proj[...] = value
    for copy in copies:
        copy.wait_send()
    for s in [sc, su, sy, sz, sx, s4] + [s for chunk in chunks for s in chunk[6:]]:
        s.finish()


def backward(own, q_len, *args):
    q_all, rows, hid, rowstq, unit_q = args[0], args[5], args[6], args[9], args[12]
    n, emb = unit_q.shape
    many_q = q_all.shape[0]
    many, width = rows.shape[1:]
    hidden = hid.shape[2]
    few = rowstq.shape[1]
    tall = width // (NC * NY)
    V = pltpu.VMEM
    outs = [jax.ShapeDtypeStruct((16, w), F32) for w in (hidden, hidden, emb)]
    outs.append(jax.ShapeDtypeStruct((1, 128), F32))
    packed = (8, -(-many_q // (128 * q_len)) * 128)
    scratch = [
        V((many, many_q), F32),
        V((many, emb), BF16),
        V((8, many_q), F32),
        V((8, many_q), F32),
        V((many, emb), F32),
        V(packed, F32),
        V(packed, F32),
        V(packed, F32),
        V((NY * NX,) + packed, F32),
        V((NZ * NC,) + packed, F32),
        V((NC, many_q // NC, emb), BF16),
        V((many, emb), BF16),
        V((NX, many, emb), BF16),
        V((many_q // NC, emb), BF16),
        V((NY, NZ, n, emb), BF16),
        V((NY - 1, NZ, n, emb), BF16),
        V((NZ, n, emb), BF16),
        V((NZ - 1, n, emb), BF16),
        V((NX, n, emb), BF16),
        V((many, width), BF16),
        V((width, many), BF16),
        V((few, width), BF16),
        V((width, few), BF16),
        V((few, emb), BF16),
        V((NX, width, many), BF16),
        V((NX, many, hidden), BF16),
        V((NX, many, hidden), F32),
        V((emb, hidden), F32),
        V((width, hidden), BF16),
        V((width, hidden), F32),
        V((width, hidden), F32),
        V((width, emb), F32),
    ]
    parts = 2 * (hidden // TILE)

    def chunk_buffers(w):
        return [
            V((NC, NY, tall, w), BF16),
            V((NY, tall, w), BF16),
            V((NY - 1, tall, w), BF16),
            V((tall + 8, w), F32),
            V((NZ, 16, w), BF16),
            V((NZ - 1, 16, w), BF16),
        ]

    scratch += chunk_buffers(emb)
    scratch += [V((NX, 16, emb), F32), pltpu.SemaphoreType.DMA((3 * NX,))]
    for buffer in chunk_buffers(TILE):
        scratch += [buffer] * parts
    scratch += sems(NY * NX - 1) + sems(NZ * NC - 1)
    for a in "cxyzx" + "cyz" * (parts + 1) + "x":
        scratch += sems({"x": NX, "y": NY, "z": NZ, "c": NC}[a] - 1)
    kernel = functools.partial(back_kernel, own, q_len)
    return call(kernel, outs, scratch, 3, *args, outer=([5, 6, 7], ()), scalars=[4])


def trim_kernel(n, *refs):
    half = len(refs) // 2
    for src, dst in zip(refs[:half], refs[half:]):
        dst[...] = src[0:n, :]


def trim(n, *arrays):
    return pl.pallas_call(
        functools.partial(trim_kernel, n),
        out_shape=[jax.ShapeDtypeStruct((n, a.shape[1]), a.dtype) for a in arrays],
        in_specs=[VMEM] * len(arrays),
        out_specs=[VMEM] * len(arrays),
    )(*arrays)


def local(
    passage_states,
    query_states,
    lengths,
    owner_map,
    candidates,
    teacher_scores,
    up_weight,
    down_weight,
    proj_weight,
):
    p_dev, pass_len, width = passage_states.shape
    q_dev, q_len, _ = query_states.shape
    emb = proj_weight.shape[1]
    n_dp = NY * NZ * NC
    p_own = p_dev // NX
    q_rows = q_dev * q_len
    rows = width // n_dp

    order = np.arange(width).reshape(NY, NZ, NC, rows).transpose(2, 0, 1, 3).reshape(-1)
    perm = jnp.asarray(np.eye(width)[order], BF16)
    (
        rows_p, hid_p, slope_p, unit_p, inv_p, q_all, side,
        rowstq, hid_q, slope_q, unit_q, inv_q, projp,
    ) = encode(
        passage_states, query_states.reshape(q_rows, width), up_weight, down_weight,
        proj_weight, perm, owner_map, candidates, teacher_scores,
    )
    q_all = q_all.reshape(n_dp * q_rows, emb)
    up, down, grad_proj, loss = backward(
        p_own, q_len, q_all, unit_p, inv_p, side, lengths,
        rows_p, hid_p, slope_p, perm, rowstq, hid_q, slope_q, unit_q, inv_q,
        down_weight, proj_weight, projp,
    )
    up, down, grad_proj = trim(rows, up, down, grad_proj)
    return loss[0, :q_dev], up, down.T, grad_proj


def solution(mesh):
    return jax.shard_map(
        local,
        mesh=mesh,
        in_specs=(
            P("dp", None, None),
            P("dp", None, None),
            P(),
            P(),
            P("dp", "mp"),
            P("dp", "mp"),
            P(None, "mp"),
            P("mp", None),
            P(),
        ),
        out_specs=(P("dp"), P("dp", "mp"), P("mp", "dp"), P("dp", None)),
        check_vma=False,
    )
```
